32 devices in a mesh: expert: 4 (over y, x), rows: 8 (over z, core).
Axes of the slice: x: 2, y: 2, z: 4, core: 2. Of those that a mesh axis runs over, the one named last changes fastest.
Arguments:
- expert_inputs: bfloat16 [65536, 768], P(('expert', 'rows')), may hold values from -54 to 54
- row_expert: int32 [65536, 1], P(('expert', 'rows')), may hold values from 0 to 7; in each aligned block of 2048 rows (0 to 2047, 2048 to 4095, ...) at most 256 rows name the same one
- down_weight: bfloat16 [8, 2048, 768], P('expert', 'rows'), may hold values from -6 to 6
- keep_mask: bfloat16 [8, 2048, 768], P('expert', 'rows'), may hold values from 0 to 1, as said below
Outputs:
- pruned: float32 [8, 2048, 768], P('expert', 'rows')
The draws below stay inside these ranges and needn't reach their ends.
Inputs may be any that keep to these rules, and one draw needn't show every extreme that they name: `row_expert`: at most 256 of the 2048 rows of one device name the same expert, and in every draw some device names some expert exactly 256 times; every expert is named by some row. `keep_mask`: every entry is 0 or 1.
All inputs are finite; a program needn't handle non-finite values.
Results may differ from the reference program's by a relative error of at most 0.0003.
Values may be sent and summed in bfloat16 or wider, within the bound.
No kernel may reach another device: no remote copies, remote signals or barrier semaphores. Data moves between devices by JAX's collectives and lax.ppermute only.
A program may use at most 64 MiB of HBM per device.

```python
import math
import jax
import jax.numpy as jnp
import numpy as np
from jax import lax

H = 768
DOUT = 2048
TOK = 2048
STEPS = 4
EXPERTS = 8
CAP = 256
ROWS = 65536
N_EXPERT = 4
N_ROWS = 8


def draw_expert_inputs(key, part):
    base = jax.random.fold_in(key, 101)
    key_noise, key_row, key_col = jax.random.split(base, 3)
    noise = jnp.clip(jax.random.normal(key_noise, (ROWS, H), jnp.float32), -6.0, 6.0)
    row_scale = jnp.exp(jax.random.uniform(key_row, (ROWS, 1), jnp.float32, math.log(0.3), math.log(3.0)))
    col_scale = jnp.exp(jax.random.uniform(key_col, (1, H), jnp.float32, math.log(0.3), math.log(3.0)))
    return (noise * row_scale * col_scale).astype(jnp.bfloat16)


def draw_keep_mask(key, part):
    bits = jax.random.randint(jax.random.fold_in(key, 202), (EXPERTS, DOUT, H), 0, 2)
    return bits.astype(jnp.float32).astype(jnp.bfloat16)


def steps_of(key, shape, cuts, low, top_value):
    level = 1.0
    for dim, shards_of in cuts:
        draws = jax.random.uniform(jax.random.fold_in(jax.random.fold_in(key, 6), dim), (shards_of,), jnp.float32, low / len(cuts), top_value / len(cuts))
        level = level * jnp.repeat(jnp.exp(draws), shape[dim] // shards_of).reshape((-1,) + (1,) * (len(shape) - 1 - dim))
    return level


def shared_out(rng, own, number, rows, count, top, limit, slope):
    sequence = jax.random.permutation(rng, count)
    crowded, common = shares(count, rows * top, limit, slope, True), shares(count, rows * top, limit, slope, False)
    places = jnp.arange(count)

    def named(tallies, rotation):
        used = int((tallies > 0).sum())
        fixed = max(1, used // 4)
        moved = fixed + (places - fixed + rotation * (used - fixed)) % max(1, count - fixed)
        return jnp.zeros((count,), jnp.int32).at[sequence[jnp.where(places < fixed, places, moved)]].set(jnp.asarray(tallies, jnp.int32))

    tallies = jnp.where(number % 4 == 0, named(crowded, number // 4), named(common, number - number // 4 - 1))
    mixed = jax.random.permutation(jax.random.fold_in(own, 3), count)
    source_of, sink = mixed[0:count // 2 * 2:2], mixed[1:count // 2 * 2:2]
    room = jnp.minimum(tallies[source_of] - 1, limit - tallies[sink]) // 2
    room = jnp.where((source_of == sequence[0]) | (sink == sequence[0]) | (tallies[sink] == 0), 0, jnp.maximum(room, 0))
    moved = jax.random.randint(jax.random.fold_in(own, 4), (count // 2,), 0, 1 << 20) % (room + 1)
    tallies = tallies.at[source_of].add(-moved).at[sink].add(moved)
    items = jnp.searchsorted(jnp.cumsum(tallies), jnp.arange(rows * top), side="right").astype(jnp.int32)
    table = items.reshape(top, rows).T
    table = table[jax.random.permutation(jax.random.fold_in(own, 1), rows)]
    rotation = jax.random.randint(jax.random.fold_in(own, 2), (rows, 1), 0, top)
    return jnp.take_along_axis(table, (jnp.arange(top)[None, :] + rotation) % top, axis=1)


def shares(amount, total, most, skew, full):
    loads = [(1 << 20) // math.isqrt(rank ** skew) + 1 for rank in range(1, amount + 1)]
    largest = most if full else min(most, max(-(-total // amount), total * loads[0] // sum(loads)))
    least = 1 if total - largest >= amount - 1 else 0
    given, rest = [largest] + [least] * (amount - 1), total - largest - least * (amount - 1)
    while rest > 0:
        movable = [i for i in range(1, amount) if given[i] < largest] or [i for i in range(1, amount) if given[i] < most]
        pool, left = sum([loads[i] for i in movable]), rest
        for i in movable:
            extra = min(most - given[i], max(1, left * loads[i] // pool), rest)
            given[i] = given[i] + extra
            rest = rest - extra
    return np.array(given)


def gaussian(rng, shape, spread, reach, cuts=(), held_as=jnp.bfloat16):
    factor_of = steps_of(rng, shape, cuts, -0.22, 0.18) if cuts else 1.0
    array = jax.random.normal(rng, shape, jnp.float32) * spread * factor_of
    return jnp.minimum(jnp.maximum(array, -reach), reach).astype(held_as)


def setup_inputs(seed: int = 0) -> dict:
    streams_of = jax.random.split(jax.random.key(seed), 5)
    expert_inputs = draw_expert_inputs(jax.random.fold_in(streams_of[4], 71), 0)
    row_expert_keys = jax.random.split(jax.random.fold_in(streams_of[1], 1), ROWS // TOK)
    row_expert_turns = jax.random.permutation(jax.random.fold_in(streams_of[1], 3), ROWS // TOK)
    row_expert = jax.vmap(lambda own, number: shared_out(jax.random.fold_in(streams_of[1], 2), own, number, TOK, EXPERTS, 1, CAP, 2))(row_expert_keys, row_expert_turns).reshape((ROWS, 1))
    down_weight = gaussian(streams_of[2], (EXPERTS, DOUT, H), 1.0, 6.0, ((0, 4), (1, 8)))
    keep_mask = draw_keep_mask(jax.random.fold_in(streams_of[4], 71), 0)
    return dict(expert_inputs=expert_inputs, row_expert=row_expert, down_weight=down_weight, keep_mask=keep_mask)


def reference(expert_inputs, row_expert, down_weight, keep_mask):
    owners = row_expert[:, 0].astype(jnp.int32)
    labels = jnp.arange(EXPERTS, dtype=jnp.int32)
    counts = jnp.sum((owners[:, None] == labels[None, :]).astype(jnp.int32), axis=0)
    starts = (jnp.cumsum(counts) - counts).astype(jnp.int32)
    ordering = jnp.argsort(owners, stable=True).astype(jnp.int32)
    largest = CAP * N_EXPERT * N_ROWS
    offsets = jnp.arange(largest, dtype=jnp.int32)

    def one_expert(packed):
        expert_id, weight_tile, keep_tile = packed
        chosen = jnp.clip(starts[expert_id] + offsets, 0, ROWS - 1).astype(jnp.int32)
        usable = (offsets < counts[expert_id]).astype(jnp.float32)
        gathered = expert_inputs[ordering[chosen]].astype(jnp.float32) * usable[:, None]
        gram_matrix = jnp.dot(gathered.T, gathered, precision=lax.Precision.HIGHEST, preferred_element_type=jnp.float32)
        inverse = 1.0 / (jnp.diagonal(gram_matrix) + 1e-6)
        target_weight = weight_tile.astype(jnp.float32)
        keep_float = keep_tile.astype(jnp.float32)
        pruned = keep_float * target_weight
        for sweep in range(STEPS):
            gradient = jnp.dot(pruned - target_weight, gram_matrix, precision=lax.Precision.HIGHEST, preferred_element_type=jnp.float32)
            pruned = keep_float * (pruned - 0.5 * gradient * inverse[None, :])
        return pruned

    return lax.map(one_expert, (labels, down_weight, keep_mask))
```

```python
import functools

import jax
import jax.numpy as jnp
from jax import lax
from jax.experimental import pallas as pl
from jax.experimental.pallas import tpu as pltpu
from jax.sharding import PartitionSpec as P

STEPS = 4
BLOCK = 128
relax_factor = 0.5
diagonal_eps = 1e-06
VMEM_LIMIT = 50 * 2**20

VMEM = pl.BlockSpec(memory_space=pltpu.VMEM)
SMEM = pl.BlockSpec(memory_space=pltpu.SMEM)
F32, BF16, I32 = jnp.float32, jnp.bfloat16, jnp.int32


def call(kernel, out_shape, in_specs, scratch=(), flops=0, moved=0, out_specs=None, aliases=None, name=None):
    many = isinstance(out_shape, (list, tuple))
    return pl.pallas_call(
        kernel,
        out_shape=out_shape,
        in_specs=in_specs,
        out_specs=out_specs if out_specs is not None else ([VMEM] * len(out_shape) if many else VMEM),
        scratch_shapes=list(scratch),
        input_output_aliases=aliases or {},
        cost_estimate=pl.CostEstimate(flops=flops, bytes_accessed=moved, transcendentals=0),
        compiler_params=pltpu.CompilerParams(vmem_limit_bytes=VMEM_LIMIT),
        name=name,
    )


def slots_of(owners, experts, capacity):
    tokens = owners.shape[1]
    lanes = 128
    blocks = tokens // lanes
    named = owners == lax.broadcasted_iota(I32, (experts, tokens), 0)
    ones = named.astype(F32)
    stacked = jnp.concatenate([ones[:, b * lanes:(b + 1) * lanes] for b in range(blocks)], axis=0)
    upto = lax.broadcasted_iota(I32, (lanes, lanes), 0) <= lax.broadcasted_iota(I32, (lanes, lanes), 1)
    within = jnp.dot(stacked.astype(BF16), upto.astype(F32).astype(BF16), preferred_element_type=F32)
    carry = jnp.zeros((experts, 1), F32)
    parts = []
    for b in range(blocks):
        part = within[b * experts:(b + 1) * experts]
        parts.append(part + carry)
        carry = carry + part[:, lanes - 1:lanes]
    counted = jnp.concatenate(parts, axis=1)
    rank = jnp.sum(jnp.where(named, counted - 1.0, 0.0), axis=0, keepdims=True)
    return owners * capacity + rank.astype(I32)


def place(key, rows_ref, experts, capacity, out_refs):
    tokens, hidden = rows_ref.shape
    places = lax.broadcasted_iota(I32, (capacity, tokens), 0)
    chosen = jnp.concatenate(
        [(places == key - e * capacity).astype(F32).astype(BF16) for e in experts], axis=0
    )
    width = 256
    for c in range(0, hidden, width):
        got = jnp.dot(chosen, rows_ref[:, c:c + width], preferred_element_type=F32).astype(BF16)
        for k, out_ref in enumerate(out_refs):
            out_ref[:, c:c + width] = got[k * capacity:(k + 1) * capacity]


def first_kernel(peers, slots, all_experts, capacity, me_ref, owner_ref, rows_ref, key_ref, *out_refs):
    me = me_ref[0]
    key = slots_of(owner_ref[...], all_experts, capacity)
    key_ref[...] = key
    place(key, rows_ref, [lax.bitwise_xor(me, k) * slots for k in range(1, peers)], capacity, out_refs)


def second_kernel(peers, slots, capacity, me_ref, key_ref, rows_ref, *out_refs):
    me = me_ref[0]
    experts = [me * slots + a for a in range(slots)]
    for a in range(1, slots):
        experts += [lax.bitwise_xor(me, k) * slots + a for k in range(1, peers)]
    place(key_ref[...], rows_ref, experts, capacity, out_refs)


def upper(blocks):
    return [(i, j) for i in range(blocks) for j in range(i, blocks)]


def gram_kernel(pieces, bit, where_ref, *refs):
    chunk_refs, (keep_ref, send_ref, packed) = refs[:pieces], refs[pieces:]
    hidden = chunk_refs[0].shape[1]
    blocks = hidden // BLOCK
    at = {pair: n for n, pair in enumerate(upper(blocks))}
    x = jnp.concatenate([r[...] for r in chunk_refs], axis=0)
    strip = 2 * BLOCK if blocks % 2 == 0 else BLOCK
    for s in range(0, hidden, strip):
        product = lax.dot_general(
            x[:, s:s + strip], x[:, s:], (((0,), (0,)), ((), ())), preferred_element_type=F32
        )
        for i in range(strip // BLOCK):
            for j in range((hidden - s) // BLOCK):
                pair = (s // BLOCK + i, s // BLOCK + j)
                if pair in at:
                    n = at[pair]
                    packed[n * BLOCK:(n + 1) * BLOCK] = product[i * BLOCK:(i + 1) * BLOCK, j * BLOCK:(j + 1) * BLOCK]
    half = keep_ref.shape[0]
    mine = lax.bitwise_and(lax.shift_right_logical(where_ref[0], bit), 1)
    keep_ref[...] = packed[pl.ds(pl.multiple_of(mine * half, 8), half)]
    send_ref[...] = packed[pl.ds(pl.multiple_of((1 - mine) * half, 8), half)]


def halve_kernel(bit, where_ref, keep_ref, got_ref, keep_out, send_out):
    half = keep_out.shape[0]
    mine = lax.bitwise_and(lax.shift_right_logical(where_ref[0], bit), 1)
    ours = pl.ds(pl.multiple_of(mine * half, 8), half)
    theirs = pl.ds(pl.multiple_of((1 - mine) * half, 8), half)
    keep_out[...] = keep_ref[ours] + got_ref[ours]
    send_out[...] = keep_ref[theirs] + got_ref[theirs]


def add_kernel(a_ref, b_ref, out_ref):
    out_ref[...] = a_ref[...] + b_ref[...]


def steps_kernel(bits, flips, where_ref, weight_ref, mask_ref, *refs):
    pieces = len(flips)
    piece_refs = refs[:pieces]
    out_ref, packed, high, low, scale = refs[-5:]
    hidden = weight_ref.shape[-1]
    blocks = hidden // BLOCK
    size = piece_refs[0].shape[0]
    where = where_ref[0]
    for flip, piece_ref in zip(flips, piece_refs):
        owner = lax.bitwise_xor(where, flip)
        start = 0
        length = size * pieces
        for b in range(bits):
            length = length // 2
            start = start + lax.bitwise_and(lax.shift_right_logical(owner, b), 1) * length
        packed[pl.ds(pl.multiple_of(start, 8), size)] = piece_ref[...]
    eye = lax.broadcasted_iota(I32, (BLOCK, BLOCK), 0) == lax.broadcasted_iota(I32, (BLOCK, BLOCK), 1)
    for n, (i, j) in enumerate(upper(blocks)):
        block = packed[n * BLOCK:(n + 1) * BLOCK]
        rows, cols = slice(i * BLOCK, (i + 1) * BLOCK), slice(j * BLOCK, (j + 1) * BLOCK)
        hi = block.astype(BF16)
        high[rows, cols] = hi
        low[rows, cols] = (block - hi.astype(F32)).astype(BF16)
        if i == j:
            diagonal = jnp.sum(jnp.where(eye, block, 0.0), axis=0, keepdims=True)
            scale[:, cols] = relax_factor * (1.0 / (diagonal + diagonal_eps))
        else:
            block = block.T
            hi = block.astype(BF16)
            high[cols, rows] = hi
            low[cols, rows] = (block - hi.astype(F32)).astype(BF16)
    weight = weight_ref[0].astype(F32)
    keep = mask_ref[0].astype(F32)
    factor = scale[...]
    pruned = keep * weight
    for sweep in range(STEPS):
        change = pruned - weight
        top = change.astype(BF16)
        if sweep == 0:
            gradient = jnp.dot(top, high[...], preferred_element_type=F32)
        else:
            rest = (change - top.astype(F32)).astype(BF16)
            both = jnp.dot(jnp.concatenate([top, rest], axis=0), high[...], preferred_element_type=F32)
            gradient = both[:top.shape[0]] + both[top.shape[0]:]
        gradient = gradient + jnp.dot(top, low[...], preferred_element_type=F32)
        pruned = keep * (pruned - gradient * factor)
    out_ref[0] = pruned


def on_device(expert_inputs, row_expert, down_weight, keep_mask):
    tokens, hidden = expert_inputs.shape
    slots, features, _ = down_weight.shape
    peers = lax.axis_size("expert")
    copies = lax.axis_size("rows")
    all_experts = slots * peers
    capacity = tokens // 8
    bits = copies.bit_length() - 1
    me = jnp.reshape(lax.axis_index("expert").astype(I32), (1,))
    where = jnp.reshape(lax.axis_index("rows").astype(I32), (1,))
    owners = row_expert.reshape(1, tokens)

    def over(axis, size, array, flip):
        return lax.ppermute(array, axis, [(i, i ^ flip) for i in range(size)])

    chunk = jax.ShapeDtypeStruct((capacity, hidden), BF16)
    place_flops = 2 * capacity * tokens * hidden
    sent_first = peers - 1
    key, *outgoing = call(
        functools.partial(first_kernel, peers, slots, all_experts, capacity),
        [jax.ShapeDtypeStruct((1, tokens), I32)] + [chunk] * sent_first,
        [SMEM, VMEM, VMEM], flops=place_flops * sent_first, moved=expert_inputs.size * 4, name="place_first",
    )(me, owners, expert_inputs)
    arrived = [[over("expert", peers, outgoing[k - 1], k) for k in range(1, peers)]]
    count = slots + (slots - 1) * (peers - 1)
    rest = call(
        functools.partial(second_kernel, peers, slots, capacity),
        [chunk] * count,
        [SMEM, VMEM, VMEM], flops=place_flops * count, moved=expert_inputs.size * 4, name="place_rest",
    )(me, key, expert_inputs)
    own = rest[:slots]
    for a in range(1, slots):
        outgoing = rest[slots + (a - 1) * (peers - 1):slots + a * (peers - 1)]
        arrived.append([over("expert", peers, outgoing[k - 1], k) for k in range(1, peers)])

    blocks = hidden // BLOCK
    packed_rows = len(upper(blocks)) * BLOCK
    result = None
    for a in range(slots):
        size = packed_rows // 2
        keep, send = call(
            functools.partial(gram_kernel, peers, 0),
            [jax.ShapeDtypeStruct((size, BLOCK), F32)] * 2,
            [SMEM] + [VMEM] * peers,
            scratch=[pltpu.VMEM((packed_rows, BLOCK), F32)],
            flops=2 * capacity * peers * hidden * hidden, moved=packed_rows * BLOCK * 4, name=f"gram_{a}",
        )(where, own[a], *arrived[a])
        for bit in range(1, bits - 1):
            got = over("rows", copies, send, 1 << (bit - 1))
            size = size // 2
            keep, send = call(
                functools.partial(halve_kernel, bit),
                [jax.ShapeDtypeStruct((size, BLOCK), F32)] * 2,
                [SMEM, VMEM, VMEM], moved=size * BLOCK * 4 * 6, name=f"halve_{a}_{bit}",
            )(where, keep, got)
        got = over("rows", copies, send, 1 << (bits - 2))
        whole = call(
            add_kernel, jax.ShapeDtypeStruct((size, BLOCK), F32), [VMEM, VMEM], moved=size * BLOCK * 12,
            name=f"sum_{a}",
        )(keep, got)
        last = over("rows", copies, whole, 1 << (bits - 1))
        whole = call(
            add_kernel, jax.ShapeDtypeStruct((size, BLOCK), F32), [VMEM, VMEM], moved=size * BLOCK * 12,
            name=f"total_{a}",
        )(whole, last)
        held = [(0, whole)]
        for bit in range(bits - 2, -1, -1):
            held += [(flip ^ (1 << bit), over("rows", copies, piece, 1 << bit)) for flip, piece in held]
        pieces = [piece for _, piece in held]
        flips = [flip for flip, _ in held]
        out_spec = pl.BlockSpec((1, features, hidden), functools.partial(lambda a, i: (a, 0, 0), a))
        in_specs = [SMEM, out_spec, out_spec] + [pl.BlockSpec(p.shape, lambda i: (0, 0)) for p in pieces]
        args = [where, down_weight, keep_mask] + pieces
        aliases = {}
        if result is not None:
            in_specs.append(pl.BlockSpec(memory_space=pl.ANY))
            aliases = {len(args): 0}
            args.append(result)
        result = pl.pallas_call(
            functools.partial(steps_kernel, bits - 1, flips),
            out_shape=jax.ShapeDtypeStruct((slots, features, hidden), F32),
            grid=(1,),
            in_specs=in_specs,
            out_specs=out_spec,
            scratch_shapes=[
                pltpu.VMEM((packed_rows, BLOCK), F32),
                pltpu.VMEM((hidden, hidden), BF16),
                pltpu.VMEM((hidden, hidden), BF16),
                pltpu.VMEM((1, hidden), F32),
            ],
            input_output_aliases=aliases,
            cost_estimate=pl.CostEstimate(
                flops=2 * 11 * features * hidden * hidden, bytes_accessed=packed_rows * BLOCK * 4, transcendentals=0
            ),
            compiler_params=pltpu.CompilerParams(vmem_limit_bytes=VMEM_LIMIT),
            name=f"steps_{a}",
        )(*args)
    return result


def solution(mesh):
    return jax.shard_map(
        on_device,
        mesh=mesh,
        in_specs=(
            P(("expert", "rows"), None),
            P(("expert", "rows"), None),
            P("expert", "rows", None),
            P("expert", "rows", None),
        ),
        out_specs=P("expert", "rows", None),
        check_vma=False,
    )
```

```python
import functools

import jax
import jax.numpy as jnp
from jax import lax
from jax.experimental import pallas as pl
from jax.experimental.pallas import tpu as pltpu
from jax.sharding import PartitionSpec as P

STEPS = 4
BLOCK = 128
CHUNKS = 2
relax_factor = 0.5
diagonal_eps = 1e-06
VMEM_LIMIT = 50 * 2**20

VMEM = pl.BlockSpec(memory_space=pltpu.VMEM)
ANY = pl.BlockSpec(memory_space=pl.ANY)
SMEM = pl.BlockSpec(memory_space=pltpu.SMEM)
F32, BF16, I32 = jnp.float32, jnp.bfloat16, jnp.int32


def call(kernel, out_shape, in_specs, scratch=(), flops=0, moved=0, out_specs=None, aliases=None, name=None, after=()):
    many = isinstance(out_shape, (list, tuple))
    used, idle = len(in_specs), len(after)

    def body(*refs):
        kernel(*refs[:used], *refs[used + idle:])

    inner = pl.pallas_call(
        body,
        out_shape=out_shape,
        in_specs=list(in_specs) + [ANY] * idle,
        out_specs=out_specs if out_specs is not None else ([VMEM] * len(out_shape) if many else VMEM),
        scratch_shapes=list(scratch),
        input_output_aliases=aliases or {},
        cost_estimate=pl.CostEstimate(flops=flops, bytes_accessed=moved, transcendentals=0),
        compiler_params=pltpu.CompilerParams(vmem_limit_bytes=VMEM_LIMIT),
        name=name,
    )
    return lambda *args: inner(*args, *after)


def cuts(size, chunks):
    ends = [size * (c + 1) // (8 * chunks) * 8 for c in range(chunks)]
    return [end - start for start, end in zip([0] + ends, ends)]


def slots_of(owners, experts, capacity):
    tokens = owners.shape[1]
    lanes = 128
    blocks = tokens // lanes
    named = owners == lax.broadcasted_iota(I32, (experts, tokens), 0)
    ones = named.astype(F32)
    stacked = jnp.concatenate([ones[:, b * lanes:(b + 1) * lanes] for b in range(blocks)], axis=0)
    upto = lax.broadcasted_iota(I32, (lanes, lanes), 0) <= lax.broadcasted_iota(I32, (lanes, lanes), 1)
    within = jnp.dot(stacked.astype(BF16), upto.astype(F32).astype(BF16), preferred_element_type=F32)
    carry = jnp.zeros((experts, 1), F32)
    parts = []
    for b in range(blocks):
        part = within[b * experts:(b + 1) * experts]
        parts.append(part + carry)
        carry = carry + part[:, lanes - 1:lanes]
    counted = jnp.concatenate(parts, axis=1)
    rank = jnp.sum(jnp.where(named, counted - 1.0, 0.0), axis=0, keepdims=True)
    return owners * capacity + rank.astype(I32)


def place(key, rows_ref, experts, capacity, out_refs):
    tokens, hidden = rows_ref.shape
    places = lax.broadcasted_iota(I32, (capacity, tokens), 0)
    chosen = jnp.concatenate(
        [(places == key - e * capacity).astype(F32).astype(BF16) for e in experts], axis=0
    )
    width = 256
    for c in range(0, hidden, width):
        got = jnp.dot(chosen, rows_ref[:, c:c + width], preferred_element_type=F32).astype(BF16)
        for k, out_ref in enumerate(out_refs):
            out_ref[:, c:c + width] = got[k * capacity:(k + 1) * capacity]


def first_kernel(peers, slots, all_experts, capacity, me_ref, owner_ref, rows_ref, key_ref, *out_refs):
    me = me_ref[0]
    key = slots_of(owner_ref[...], all_experts, capacity)
    key_ref[...] = key
    place(key, rows_ref, [lax.bitwise_xor(me, k) * slots for k in range(1, peers)], capacity, out_refs)


def second_kernel(peers, slots, capacity, me_ref, key_ref, rows_ref, *out_refs):
    me = me_ref[0]
    experts = [me * slots + a for a in range(slots)]
    for a in range(1, slots):
        experts += [lax.bitwise_xor(me, k) * slots + a for k in range(1, peers)]
    place(key_ref[...], rows_ref, experts, capacity, out_refs)


def layout(hidden, halvings):
    blocks = hidden // BLOCK
    off = [(i, j) for i in range(blocks) for j in range(i + 1, blocks)]
    pairs = [(i, i + 1 if i + 1 < blocks else None) for i in range(0, blocks, 2)]
    tail = (len(off) + len(pairs)) * BLOCK
    unit = 8 << halvings
    return off, pairs, tail, -(-(tail + len(pairs)) // unit) * unit


def eye_of(compare):
    return compare(lax.broadcasted_iota(I32, (BLOCK, BLOCK), 0), lax.broadcasted_iota(I32, (BLOCK, BLOCK), 1))


def bit_of(where, bit):
    return lax.bitwise_and(lax.shift_right_logical(where, bit), 1)


def gram_kernel(halvings, pieces, where_ref, *refs):
    chunk_refs, (keep_ref, send_ref, packed) = refs[:pieces], refs[pieces:]
    hidden = chunk_refs[0].shape[1]
    off, pairs, tail, length = layout(hidden, halvings)
    at = {pair: n for n, pair in enumerate(off)}
    x = jnp.concatenate([r[...] for r in chunk_refs], axis=0)
    strip = 2 * BLOCK
    packed[tail:length] = jnp.zeros((length - tail, BLOCK), F32)
    for n, (first, second) in enumerate(pairs):
        low, high = first * BLOCK, min(first * BLOCK + strip, hidden)
        product = lax.dot_general(
            x[:, low:high], x[:, low:], (((0,), (0,)), ((), ())), preferred_element_type=F32
        )
        for i in range((high - low) // BLOCK):
            for j in range((hidden - low) // BLOCK):
                pair = (first + i, first + j)
                if pair in at:
                    row = at[pair] * BLOCK
                    packed[row:row + BLOCK] = product[i * BLOCK:(i + 1) * BLOCK, j * BLOCK:(j + 1) * BLOCK]
        mixed = product[:BLOCK, :BLOCK]
        if second is not None:
            other = product[BLOCK:, BLOCK:2 * BLOCK]
            mixed = jnp.where(eye_of(lax.le), mixed, other)
            packed[tail + n:tail + n + 1] = jnp.sum(jnp.where(eye_of(lax.eq), other, 0.0), axis=0, keepdims=True)
        row = (len(off) + n) * BLOCK
        packed[row:row + BLOCK] = mixed
    half = keep_ref.shape[0]
    mine = bit_of(where_ref[0], 0)
    keep_ref[...] = packed[pl.ds(pl.multiple_of(mine * half, 8), half)]
    send_ref[...] = packed[pl.ds(pl.multiple_of((1 - mine) * half, 8), half)]


def halve_kernel(bit, where_ref, keep_ref, got_ref, *out_refs):
    chunks = len(out_refs) // 2
    half = keep_ref.shape[0] // 2
    mine = bit_of(where_ref[0], bit)
    for side, refs in ((mine, out_refs[:chunks]), (1 - mine, out_refs[chunks:])):
        start = 0
        for ref in refs:
            size = ref.shape[0]
            part = pl.ds(pl.multiple_of(side * half + start, 8), size)
            ref[...] = keep_ref[part] + got_ref[part]
            start += size


def add_kernel(a_ref, b_ref, out_ref):
    out_ref[...] = a_ref[...] + b_ref[...]


def steps_kernel(slot, halvings, places, where_ref, weight_ref, mask_ref, *refs):
    piece_refs = refs[:len(places)]
    out_ref, token_ref, packed, high, low, scale, result, done = refs[-8:]
    hidden = weight_ref.shape[-1]
    off, pairs, tail, length = layout(hidden, halvings)
    where = where_ref[0]
    for (flip, offset), piece_ref in zip(places, piece_refs):
        owner = lax.bitwise_xor(where, flip)
        start = offset
        for b in range(halvings):
            start = start + bit_of(owner, b) * (length >> (b + 1))
        packed[pl.ds(pl.multiple_of(start, 8), piece_ref.shape[0])] = piece_ref[...]

    def put(i, j, block):
        rows, cols = slice(i * BLOCK, (i + 1) * BLOCK), slice(j * BLOCK, (j + 1) * BLOCK)
        hi = block.astype(BF16)
        high[rows, cols] = hi
        low[rows, cols] = (block - hi.astype(F32)).astype(BF16)

    for n, (i, j) in enumerate(off):
        block = packed[n * BLOCK:(n + 1) * BLOCK]
        put(i, j, block)
        put(j, i, block.T)
    eye = eye_of(lax.eq)
    for n, (first, second) in enumerate(pairs):
        row = (len(off) + n) * BLOCK
        block = packed[row:row + BLOCK]
        turned = block.T
        put(first, first, jnp.where(eye_of(lax.le), block, turned))
        diagonals = [(first, jnp.sum(jnp.where(eye, block, 0.0), axis=0, keepdims=True))]
        if second is not None:
            diagonal = packed[tail + n:tail + n + 1]
            put(second, second, jnp.where(eye, diagonal, jnp.where(eye_of(lax.gt), block, turned)))
            diagonals.append((second, diagonal))
        for i, diagonal in diagonals:
            scale[:, i * BLOCK:(i + 1) * BLOCK] = relax_factor * (1.0 / (diagonal + diagonal_eps))
    weight = weight_ref[slot].astype(F32)
    keep = mask_ref[slot].astype(F32)
    factor = scale[...]
    pruned = keep * weight
    for sweep in range(STEPS):
        change = pruned - weight
        top = change.astype(BF16)
        if sweep == 0:
            gradient = jnp.dot(top, high[...], preferred_element_type=F32)
        else:
            rest = (change - top.astype(F32)).astype(BF16)
            both = jnp.dot(jnp.concatenate([top, rest], axis=0), high[...], preferred_element_type=F32)
            gradient = both[:top.shape[0]] + both[top.shape[0]:]
        gradient = gradient + jnp.dot(top, low[...], preferred_element_type=F32)
        pruned = keep * (pruned - gradient * factor)
    result[...] = pruned
    token_ref[...] = pruned[:8, :BLOCK]
    copy = pltpu.make_async_copy(result, out_ref.at[slot], done)
    copy.start()
    copy.wait()


def on_device(expert_inputs, row_expert, down_weight, keep_mask):
    tokens, hidden = expert_inputs.shape
    slots, features, _ = down_weight.shape
    peers = lax.axis_size("expert")
    copies = lax.axis_size("rows")
    all_experts = slots * peers
    capacity = tokens // 8
    bits = copies.bit_length() - 1
    me = jnp.reshape(lax.axis_index("expert").astype(I32), (1,))
    where = jnp.reshape(lax.axis_index("rows").astype(I32), (1,))
    owners = row_expert.reshape(1, tokens)

    def over(axis, size, array, flip):
        return lax.ppermute(array, axis, [(i, i ^ flip) for i in range(size)])

    chunk = jax.ShapeDtypeStruct((capacity, hidden), BF16)
    place_flops = 2 * capacity * tokens * hidden
    sent_first = peers - 1
    key, *outgoing = call(
        functools.partial(first_kernel, peers, slots, all_experts, capacity),
        [jax.ShapeDtypeStruct((1, tokens), I32)] + [chunk] * sent_first,
        [SMEM, VMEM, VMEM], flops=place_flops * sent_first, moved=expert_inputs.size * 4, name="place_first",
    )(me, owners, expert_inputs)
    arrived = [[over("expert", peers, outgoing[k - 1], k) for k in range(1, peers)]]
    count = slots + (slots - 1) * (peers - 1)
    rest = call(
        functools.partial(second_kernel, peers, slots, capacity),
        [chunk] * count,
        [SMEM, VMEM, VMEM], flops=place_flops * count, moved=expert_inputs.size * 4, name="place_rest",
    )(me, key, expert_inputs)
    own = rest[:slots]
    for a in range(1, slots):
        outgoing = rest[slots + (a - 1) * (peers - 1):slots + a * (peers - 1)]
        arrived.append([over("expert", peers, outgoing[k - 1], k) for k in range(1, peers)])

    halvings = bits - 1
    length = layout(hidden, halvings)[3]

    def rows_of(size):
        return jax.ShapeDtypeStruct((size, BLOCK), F32)

    def over_rows(array, bit):
        return over("rows", copies, array, 1 << bit)

    def add(a, b, name, after=()):
        return call(
            add_kernel, rows_of(a.shape[0]), [VMEM, VMEM], moved=a.size * 12, name=name, after=after,
        )(a, b)

    def steps(slot, pieces, places, result, after=()):
        in_specs = [SMEM] + [VMEM] * (2 + len(pieces))
        args = [where, down_weight, keep_mask] + pieces
        aliases = {}
        if result is not None:
            aliases = {len(args): 0}
            in_specs.append(ANY)
            args.append(result)
        return call(
            functools.partial(steps_kernel, slot, halvings, places),
            [jax.ShapeDtypeStruct((slots, features, hidden), F32), rows_of(8)],
            in_specs,
            out_specs=[ANY, VMEM],
            scratch=[
                pltpu.VMEM((length, BLOCK), F32),
                pltpu.VMEM((hidden, hidden), BF16),
                pltpu.VMEM((hidden, hidden), BF16),
                pltpu.VMEM((1, hidden), F32),
                pltpu.VMEM((features, hidden), F32),
                pltpu.SemaphoreType.DMA,
            ],
            aliases=aliases,
            flops=2 * 11 * features * hidden * hidden, moved=length * BLOCK * 4, name=f"steps_{slot}", after=after,
        )(*args)

    result, waiting, summed, token = None, None, (), ()
    for a in range(slots):
        size = length // 2
        keep, send = call(
            functools.partial(gram_kernel, halvings, peers),
            [rows_of(size)] * 2,
            [SMEM] + [VMEM] * peers,
            scratch=[pltpu.VMEM((length, BLOCK), F32)],
            flops=2 * capacity * peers * hidden * hidden, moved=length * BLOCK * 4, name=f"gram_{a}",
            after=summed,
        )(where, own[a], *arrived[a])
        keep, send = [keep], [send]
        for bit in range(1, halvings):
            got = over_rows(send[0], bit - 1)
            size = size // 2
            chunks = CHUNKS if bit == halvings - 1 and a == slots - 1 else 1
            shapes = [rows_of(n) for n in cuts(size, chunks)]
            halves = call(
                functools.partial(halve_kernel, bit), shapes * 2,
                [SMEM, VMEM, VMEM], moved=size * BLOCK * 4 * 6, name=f"halve_{a}_{bit}",
            )(where, keep[0], got)
            keep, send = halves[:chunks], halves[chunks:]
        summed = [
            add(mine, over_rows(theirs, halvings - 1), f"sum_{a}_{c}") for c, (mine, theirs) in enumerate(zip(keep, send))
        ]
        if waiting is not None:
            result, *token = steps(*waiting, result, after=summed)
        pieces, places, offset = [], [], 0
        for c, mine in enumerate(summed):
            total = add(mine, over_rows(mine, halvings), f"total_{a}_{c}", after=token)
            held = [(0, total)]
            for bit in range(halvings - 1, -1, -1):
                held += [(flip ^ (1 << bit), over_rows(piece, bit)) for flip, piece in held]
            places += [(flip, offset) for flip, _ in held]
            pieces += [piece for _, piece in held]
            offset += mine.shape[0]
        waiting = (a, pieces, places)
    return steps(*waiting, result)[0]


def solution(mesh):
    return jax.shard_map(
        on_device,
        mesh=mesh,
        in_specs=(
            P(("expert", "rows"), None),
            P(("expert", "rows"), None),
            P("expert", "rows", None),
            P("expert", "rows", None),
        ),
        out_specs=P("expert", "rows", None),
        check_vma=False,
    )
```

```python
import functools

import jax
import jax.numpy as jnp
from jax import lax
from jax.experimental import pallas as pl
from jax.experimental.pallas import tpu as pltpu
from jax.sharding import PartitionSpec as P

STEPS = 4
BLOCK = 128
TILE = 16
CHUNKS = 1
LEVELS = 32760.0
OCTAVE = 8.0
relax_factor = 0.5
diagonal_eps = 1e-06
tiny = 1e-30
VMEM_LIMIT = 50 * 2**20

VMEM = pl.BlockSpec(memory_space=pltpu.VMEM)
ANY = pl.BlockSpec(memory_space=pl.ANY)
SMEM = pl.BlockSpec(memory_space=pltpu.SMEM)
F32, BF16, I32, I16 = jnp.float32, jnp.bfloat16, jnp.int32, jnp.int16


def call(kernel, out_shape, in_specs, scratch=(), flops=0, moved=0, out_specs=None, aliases=None, name=None, after=()):
    many = isinstance(out_shape, (list, tuple))
    used, idle = len(in_specs), len(after)

    def body(*refs):
        kernel(*refs[:used], *refs[used + idle:])

    inner = pl.pallas_call(
        body,
        out_shape=out_shape,
        in_specs=list(in_specs) + [ANY] * idle,
        out_specs=out_specs if out_specs is not None else ([VMEM] * len(out_shape) if many else VMEM),
        scratch_shapes=list(scratch),
        input_output_aliases=aliases or {},
        cost_estimate=pl.CostEstimate(flops=flops, bytes_accessed=moved, transcendentals=0),
        compiler_params=pltpu.CompilerParams(vmem_limit_bytes=VMEM_LIMIT),
        name=name,
    )
    return lambda *args: inner(*args, *after)


def cuts(size, chunks):
    ends = [size * (c + 1) // (TILE * chunks) * TILE for c in range(chunks)]
    return [end - start for start, end in zip([0] + ends, ends)]


def slots_of(owners, experts, capacity):
    tokens = owners.shape[1]
    lanes = 128
    blocks = tokens // lanes
    named = owners == lax.broadcasted_iota(I32, (experts, tokens), 0)
    ones = named.astype(F32)
    stacked = jnp.concatenate([ones[:, b * lanes:(b + 1) * lanes] for b in range(blocks)], axis=0)
    upto = lax.broadcasted_iota(I32, (lanes, lanes), 0) <= lax.broadcasted_iota(I32, (lanes, lanes), 1)
    within = jnp.dot(stacked.astype(BF16), upto.astype(F32).astype(BF16), preferred_element_type=F32)
    carry = jnp.zeros((experts, 1), F32)
    parts = []
    for b in range(blocks):
        part = within[b * experts:(b + 1) * experts]
        parts.append(part + carry)
        carry = carry + part[:, lanes - 1:lanes]
    counted = jnp.concatenate(parts, axis=1)
    rank = jnp.sum(jnp.where(named, counted - 1.0, 0.0), axis=0, keepdims=True)
    return owners * capacity + rank.astype(I32)


def place(key, rows_ref, experts, capacity, out_refs, squares):
    tokens, hidden = rows_ref.shape
    places = lax.broadcasted_iota(I32, (capacity, tokens), 0)
    chosen = jnp.concatenate(
        [(places == key - e * capacity).astype(F32).astype(BF16) for e in experts], axis=0
    )
    width = 2 * BLOCK
    for c in range(0, hidden, width):
        got = jnp.dot(chosen, rows_ref[:, c:c + width], preferred_element_type=F32)
        for k, (out_ref, (sum_ref, row)) in enumerate(zip(out_refs, squares)):
            part = got[k * capacity:(k + 1) * capacity]
            out_ref[:, c:c + width] = part.astype(BF16)
            sum_ref[row:row + 1, c:c + width] = jnp.sum(part * part, axis=0, keepdims=True)


def first_kernel(peers, slots, all_experts, capacity, me_ref, owner_ref, rows_ref, key_ref, square_ref, *out_refs):
    me = me_ref[0]
    key = slots_of(owner_ref[...], all_experts, capacity)
    key_ref[...] = key
    square_ref[...] = jnp.zeros_like(square_ref)
    others = range(1, peers)
    place(
        key, rows_ref, [lax.bitwise_xor(me, k) * slots for k in others], capacity, out_refs,
        [(square_ref, k * slots) for k in others],
    )


def second_kernel(peers, slots, capacity, me_ref, key_ref, rows_ref, square_ref, near_ref, far_ref, *refs):
    out_refs, total = refs[:-1], refs[-1]
    me = me_ref[0]
    total[...] = square_ref[...]
    where = [(0, a) for a in range(slots)] + [(k, a) for a in range(1, slots) for k in range(1, peers)]
    place(
        key_ref[...], rows_ref, [lax.bitwise_xor(me, k) * slots + a for k, a in where], capacity, out_refs,
        [(total, k * slots + a) for k, a in where],
    )
    half = near_ref.shape[0]
    near_ref[...] = total[:half]
    far_ref[...] = total[half:]


def layout(hidden, halvings):
    blocks = hidden // BLOCK
    off = [(i, j) for i in range(blocks) for j in range(i + 1, blocks)]
    pairs = [(i, i + 1 if i + 1 < blocks else None) for i in range(0, blocks, 2)]
    tail = (len(off) + len(pairs)) * BLOCK
    unit = TILE << halvings
    return off, pairs, tail, -(-tail // unit) * unit


def eye_of(compare):
    return compare(lax.broadcasted_iota(I32, (BLOCK, BLOCK), 0), lax.broadcasted_iota(I32, (BLOCK, BLOCK), 1))


def bit_of(where, bit):
    return lax.bitwise_and(lax.shift_right_logical(where, bit), 1)


def root_of(diagonal):
    return lax.rsqrt(jnp.maximum(diagonal, tiny))


def scale_kernel(slot, halvings, diagonal_ref, out_ref):
    hidden = diagonal_ref.shape[1]
    off, pairs, tail, length = layout(hidden, halvings)
    if length > tail:
        out_ref[tail:length] = jnp.zeros((length - tail, BLOCK), F32)
    root = root_of(diagonal_ref[slot:slot + 1])
    across = [jnp.broadcast_to(root[:, b * BLOCK:(b + 1) * BLOCK], (BLOCK, BLOCK)) for b in range(hidden // BLOCK)]
    down = [a.T for a in across]
    for n, (i, j) in enumerate(off):
        out_ref[n * BLOCK:(n + 1) * BLOCK] = down[i] * across[j]
    for n, (first, second) in enumerate(pairs):
        block = down[first] * across[first]
        if second is not None:
            block = jnp.where(eye_of(lax.lt), block, down[second] * across[second])
        row = (len(off) + n) * BLOCK
        out_ref[row:row + BLOCK] = block


def add_gram(halvings, chunk_refs, before, packed):
    hidden = chunk_refs[0].shape[1]
    off, pairs, tail, length = layout(hidden, halvings)
    at = {pair: n for n, pair in enumerate(off)}
    x = jnp.concatenate([r[...] for r in chunk_refs], axis=0) if len(chunk_refs) > 1 else chunk_refs[0][...]
    strip = 2 * BLOCK

    def put(n, value):
        rows = slice(n * BLOCK, (n + 1) * BLOCK)
        packed[rows] = value if before is None else before[rows] + value

    if length > tail:
        packed[tail:length] = jnp.zeros((length - tail, BLOCK), F32)
    for n, (first, second) in enumerate(pairs):
        low, high = first * BLOCK, min(first * BLOCK + strip, hidden)
        product = lax.dot_general(
            x[:, low:high], x[:, low:], (((0,), (0,)), ((), ())), preferred_element_type=F32
        )
        for i in range((high - low) // BLOCK):
            for j in range((hidden - low) // BLOCK):
                pair = (first + i, first + j)
                if pair in at:
                    put(at[pair], product[i * BLOCK:(i + 1) * BLOCK, j * BLOCK:(j + 1) * BLOCK])
        mixed = product[:BLOCK, :BLOCK]
        if second is not None:
            mixed = jnp.where(eye_of(lax.lt), mixed, product[BLOCK:, BLOCK:2 * BLOCK])
        put(len(off) + n, jnp.where(eye_of(lax.eq), 0.0, mixed))


def early_gram_kernel(halvings, *refs):
    add_gram(halvings, refs[:-1], None, refs[-1])


def late_gram_kernel(halvings, pieces, where_ref, before_ref, *refs):
    chunk_refs, (keep_ref, send_ref, packed) = refs[:pieces], refs[pieces:]
    add_gram(halvings, chunk_refs, before_ref, packed)
    half = keep_ref.shape[0]
    mine = bit_of(where_ref[0], 0)
    keep_ref[...] = packed[pl.ds(pl.multiple_of(mine * half, TILE), half)]
    send_ref[...] = packed[pl.ds(pl.multiple_of((1 - mine) * half, TILE), half)]


def encode(values, ref):
    rows = values.shape[0]
    largest = jnp.max(jnp.abs(values), axis=0, keepdims=True)
    exponent = jnp.ceil(OCTAVE * jnp.log2(jnp.maximum(largest, tiny)))
    factor = jnp.exp2(exponent * (-1.0 / OCTAVE)) * LEVELS
    ref[:rows] = jnp.floor(values * factor + 0.5).astype(I32).astype(I16)
    ref[rows:rows + TILE] = jnp.broadcast_to(exponent, (TILE, BLOCK)).astype(I32).astype(I16)


def decode(coded):
    rows = coded.shape[0] - TILE
    exponent = coded[rows:].astype(I32).astype(F32)[:1]
    return coded[:rows].astype(I32).astype(F32) * (jnp.exp2(exponent * (1.0 / OCTAVE)) * (1.0 / LEVELS))


def scaled_halve_kernel(bit, where_ref, keep_ref, got_ref, scale_ref, *out_refs):
    chunks = len(out_refs) // 2
    half = keep_ref.shape[0] // 2
    where = where_ref[0]
    outer = bit_of(where, 0) * keep_ref.shape[0]
    mine = bit_of(where, bit)
    for side, refs, coded in ((1 - mine, out_refs[chunks:], True), (mine, out_refs[:chunks], False)):
        start = 0
        for ref in refs:
            size = ref.shape[0] - TILE if coded else ref.shape[0]
            part = pl.ds(pl.multiple_of(side * half + start, TILE), size)
            factor = scale_ref[pl.ds(pl.multiple_of(outer + side * half + start, TILE), size)]
            value = (keep_ref[part] + got_ref[part]) * factor
            if coded:
                encode(value, ref)
            else:
                ref[...] = value
            start += size


def halve_kernel(bit, where_ref, keep_ref, got_ref, *refs):
    out_refs, total = refs[:-1], refs[-1]
    chunks = len(out_refs) // 2
    total[...] = keep_ref[...] + decode(got_ref[...])
    half = keep_ref.shape[0] // 2
    mine = bit_of(where_ref[0], bit)
    for side, refs, coded in ((1 - mine, out_refs[chunks:], True), (mine, out_refs[:chunks], False)):
        start = 0
        for ref in refs:
            size = ref.shape[0] - TILE if coded else ref.shape[0]
            value = total[pl.ds(pl.multiple_of(side * half + start, TILE), size)]
            if coded:
                encode(value, ref)
            else:
                ref[...] = value
            start += size


def sum_kernel(keep_ref, got_ref, coded_ref, value_ref):
    value = keep_ref[...] + decode(got_ref[...])
    encode(value, coded_ref)
    value_ref[...] = value


def total_kernel(keep_ref, got_ref, coded_ref):
    encode(keep_ref[...] + decode(got_ref[...]), coded_ref)


def unpack_kernel(slot, halvings, places, where_ref, diagonal_ref, *refs):
    piece_refs, (high_ref, low_ref, packed) = refs[:len(places)], refs[len(places):]
    hidden = diagonal_ref.shape[1]
    off, pairs, tail, length = layout(hidden, halvings)
    where = where_ref[0]
    for (flip, offset), piece_ref in zip(places, piece_refs):
        owner = lax.bitwise_xor(where, flip)
        start = offset
        for b in range(halvings):
            start = start + bit_of(owner, b) * (length >> (b + 1))
        value = decode(piece_ref[...])
        packed[pl.ds(pl.multiple_of(start, TILE), value.shape[0])] = value

    def put(i, j, block):
        rows, cols = slice(i * BLOCK, (i + 1) * BLOCK), slice(j * BLOCK, (j + 1) * BLOCK)
        hi = block.astype(BF16)
        high_ref[rows, cols] = hi
        low_ref[rows, cols] = (block - hi.astype(F32)).astype(BF16)

    for n, (i, j) in enumerate(off):
        block = packed[n * BLOCK:(n + 1) * BLOCK]
        put(i, j, block)
        put(j, i, block.T)
    diagonal = diagonal_ref[slot:slot + 1]
    root = root_of(diagonal)
    ones = diagonal * root * root
    for n, (first, second) in enumerate(pairs):
        row = (len(off) + n) * BLOCK
        block = packed[row:row + BLOCK]
        turned = block.T
        for i, above in ((first, lax.lt), (second, lax.gt)):
            if i is not None:
                whole = jnp.where(eye_of(above), block, turned)
                put(i, i, jnp.where(eye_of(lax.eq), ones[:, i * BLOCK:(i + 1) * BLOCK], whole))


def sweeps_kernel(slot, diagonal_ref, weight_ref, mask_ref, high_ref, low_ref, *refs):
    out_ref, token_ref, result, done = refs[-4:]
    diagonal = diagonal_ref[slot:slot + 1]
    back = 1.0 / root_of(diagonal)
    factor = relax_factor * (1.0 / (diagonal + diagonal_eps)) * back
    weight = weight_ref[slot].astype(F32)
    keep = mask_ref[slot].astype(F32)
    pruned = keep * weight
    for sweep in range(STEPS):
        change = (pruned - weight) * back
        top = change.astype(BF16)
        rest = (change - top.astype(F32)).astype(BF16)
        both = jnp.dot(jnp.concatenate([top, rest], axis=0), high_ref[...], preferred_element_type=F32)
        gradient = both[:top.shape[0]] + both[top.shape[0]:]
        gradient = gradient + jnp.dot(top, low_ref[...], preferred_element_type=F32)
        pruned = keep * (pruned - gradient * factor)
    result[...] = pruned
    token_ref[...] = pruned[:8, :BLOCK]
    copy = pltpu.make_async_copy(result, out_ref.at[slot], done)
    copy.start()
    copy.wait()


def on_device(expert_inputs, row_expert, down_weight, keep_mask):
    tokens, hidden = expert_inputs.shape
    slots, features, _ = down_weight.shape
    peers = lax.axis_size("expert")
    copies = lax.axis_size("rows")
    all_experts = slots * peers
    capacity = tokens // 8
    halvings = copies.bit_length() - 2
    length = layout(hidden, halvings)[3]
    me = jnp.reshape(lax.axis_index("expert").astype(I32), (1,))
    where = jnp.reshape(lax.axis_index("rows").astype(I32), (1,))
    owners = row_expert.reshape(1, tokens)

    def shape(rows, columns=BLOCK, dtype=F32):
        return jax.ShapeDtypeStruct((rows, columns), dtype)

    def over_experts(array, flip):
        return lax.ppermute(array, "expert", [(i, i ^ flip) for i in range(peers)])

    def over_rows(array, bit):
        return lax.ppermute(array, "rows", [(i, i ^ (1 << bit)) for i in range(copies)])

    chunk = shape(capacity, hidden, BF16)
    place_flops = 2 * capacity * tokens * hidden
    key, squares, *outgoing = call(
        functools.partial(first_kernel, peers, slots, all_experts, capacity),
        [shape(1, tokens, I32), shape(all_experts, hidden)] + [chunk] * (peers - 1),
        [SMEM, VMEM, VMEM], flops=place_flops * (peers - 1), moved=expert_inputs.size * 4, name="place_first",
    )(me, owners, expert_inputs)
    arrived = [[over_experts(outgoing[k - 1], k) for k in range(1, peers)]]
    count = slots + (slots - 1) * (peers - 1)
    near, far, *rest = call(
        functools.partial(second_kernel, peers, slots, capacity),
        [shape(all_experts // 2, hidden)] * 2 + [chunk] * count,
        [SMEM, VMEM, VMEM, VMEM], scratch=[pltpu.VMEM((all_experts, hidden), F32)],
        flops=place_flops * count, moved=expert_inputs.size * 4, name="place_rest",
    )(me, key, expert_inputs, squares)
    own = rest[:slots]
    for a in range(1, slots):
        outgoing = rest[slots + (a - 1) * (peers - 1):slots + a * (peers - 1)]
        arrived.append([over_experts(outgoing[k - 1], k) for k in range(1, peers)])

    flip = peers // 2
    diagonal = near + over_experts(far, flip)
    while flip > 1:
        flip = flip // 2
        half = flip * slots
        diagonal = diagonal[:half] + over_experts(diagonal[half:], flip)
    for bit in range(halvings + 1):
        diagonal = diagonal + over_rows(diagonal, bit)

    def begin(a, after):
        chunks = [own[a]] + arrived[a][:-1]
        return call(
            functools.partial(early_gram_kernel, halvings), shape(length), [VMEM] * len(chunks),
            flops=2 * capacity * len(chunks) * hidden * hidden, moved=length * BLOCK * 4, name=f"begin_{a}", after=after,
        )(*chunks)

    def reduce(a, before, after):
        scale = call(
            functools.partial(scale_kernel, a, halvings), shape(length), [VMEM], moved=length * BLOCK * 4, name=f"scale_{a}",
        )(diagonal)
        size = length // 2
        keep, send = call(
            functools.partial(late_gram_kernel, halvings, 1), [shape(size)] * 2, [SMEM] + [VMEM] * 2,
            scratch=[pltpu.VMEM((length, BLOCK), F32)],
            flops=2 * capacity * hidden * hidden, moved=length * BLOCK * 4, name=f"gram_{a}", after=[*after, scale],
        )(where, before, arrived[a][-1])
        keep, send = [keep], [send]
        for bit in range(1, halvings):
            got = over_rows(send[0], bit - 1)
            size = size // 2
            sizes = cuts(size, CHUNKS if bit == halvings - 1 else 1)
            first = bit == 1
            parts = call(
                functools.partial(scaled_halve_kernel if first else halve_kernel, bit),
                [shape(n) for n in sizes] + [shape(n + TILE, dtype=I16) for n in sizes],
                [SMEM] + [VMEM] * (3 if first else 2),
                scratch=() if first else [pltpu.VMEM((2 * size, BLOCK), F32)],
                moved=size * BLOCK * 4 * 6, name=f"halve_{a}_{bit}",
            )(where, keep[0], got, *([scale] if first else []))
            keep, send = parts[:len(sizes)], parts[len(sizes):]
        sums = []
        for c, (mine, theirs) in enumerate(zip(keep, send)):
            rows = mine.shape[0]
            sums.append(call(
                sum_kernel, [shape(rows + TILE, dtype=I16), shape(rows)], [VMEM, VMEM], moved=rows * BLOCK * 12,
                name=f"sum_{a}_{c}",
            )(mine, over_rows(theirs, halvings - 1)))
        return sums

    def totals(a, sums, after):
        totals = []
        for c, (coded, value) in enumerate(sums):
            rows = value.shape[0]
            totals.append(call(
                total_kernel, shape(rows + TILE, dtype=I16), [VMEM, VMEM], moved=rows * BLOCK * 12,
                name=f"total_{a}_{c}", after=after,
            )(value, over_rows(coded, halvings)))
        return totals

    def gather(a, totals):
        pieces, places, offset = [], [], 0
        for total in totals:
            held = [(0, total)]
            for bit in range(halvings - 1, -1, -1):
                held += [(flip ^ (1 << bit), over_rows(piece, bit)) for flip, piece in held]
            places += [(flip, offset) for flip, _ in held]
            pieces += [piece for _, piece in held]
            offset += total.shape[0] - TILE
        return call(
            functools.partial(unpack_kernel, a, halvings, places),
            [shape(hidden, hidden, BF16)] * 2, [SMEM] + [VMEM] * (1 + len(pieces)),
            scratch=[pltpu.VMEM((length, BLOCK), F32)], moved=length * BLOCK * 4, name=f"unpack_{a}",
        )(where, diagonal, *pieces)

    def sweeps(a, high, low, result, after):
        args = [diagonal, down_weight, keep_mask, high, low] + ([] if result is None else [result])
        return call(
            functools.partial(sweeps_kernel, a),
            [jax.ShapeDtypeStruct((slots, features, hidden), F32), shape(8)],
            [VMEM] * 5 + [ANY] * (len(args) - 5),
            out_specs=[ANY, VMEM],
            scratch=[pltpu.VMEM((features, hidden), F32), pltpu.SemaphoreType.DMA],
            aliases={} if result is None else {5: 0},
            flops=2 * 3 * STEPS * features * hidden * hidden, moved=hidden * hidden * 4, name=f"sweeps_{a}", after=after,
        )(*args)

    result, whole, total, sums = None, None, (), ()
    for a in range(slots):
        before = begin(a, [s[0] for s in sums])
        sums = reduce(a, before, total)
        token = ()
        if a > 0:
            result, *token = sweeps(a - 1, *whole, result, (sums[-1][0],))
        total = totals(a, sums, token)
        whole = gather(a, total)
    return sweeps(slots - 1, *whole, result, ())[0]


def solution(mesh):
    return jax.shard_map(
        on_device,
        mesh=mesh,
        in_specs=(
            P(("expert", "rows"), None),
            P(("expert", "rows"), None),
            P("expert", "rows", None),
            P("expert", "rows", None),
        ),
        out_specs=P("expert", "rows", None),
        check_vma=False,
    )
```

```python
import functools

import jax
import jax.numpy as jnp
from jax import lax
from jax.experimental import pallas as pl
from jax.experimental.pallas import tpu as pltpu
from jax.sharding import PartitionSpec as P

STEPS = 4
BLOCK = 128
TILE = 16
PARTS = 2
LEVELS = 32760.0
OCTAVE = 8.0
relax_factor = 0.5
diagonal_eps = 1e-06
tiny = 1e-30
VMEM_LIMIT = 50 * 2**20

VMEM = pl.BlockSpec(memory_space=pltpu.VMEM)
ANY = pl.BlockSpec(memory_space=pl.ANY)
SMEM = pl.BlockSpec(memory_space=pltpu.SMEM)
F32, BF16, I32, I16 = jnp.float32, jnp.bfloat16, jnp.int32, jnp.int16


def call(kernel, out_shape, in_specs, scratch=(), flops=0, moved=0, out_specs=None, aliases=None, name=None, after=()):
    many = isinstance(out_shape, (list, tuple))
    used, idle = len(in_specs), len(after)

    def body(*refs):
        kernel(*refs[:used], *refs[used + idle:])

    inner = pl.pallas_call(
        body,
        out_shape=out_shape,
        in_specs=list(in_specs) + [ANY] * idle,
        out_specs=out_specs if out_specs is not None else ([VMEM] * len(out_shape) if many else VMEM),
        scratch_shapes=list(scratch),
        input_output_aliases=aliases or {},
        cost_estimate=pl.CostEstimate(flops=flops, bytes_accessed=moved, transcendentals=0),
        compiler_params=pltpu.CompilerParams(vmem_limit_bytes=VMEM_LIMIT),
        name=name,
    )
    return lambda *args: inner(*args, *after)


def cuts(size, chunks):
    ends = [size * (c + 1) // (TILE * chunks) * TILE for c in range(chunks)]
    return [end - start for start, end in zip([0] + ends, ends)]


def slots_of(owners, experts, capacity):
    tokens = owners.shape[1]
    lanes = 128
    blocks = tokens // lanes
    named = owners == lax.broadcasted_iota(I32, (experts, tokens), 0)
    ones = named.astype(F32)
    stacked = jnp.concatenate([ones[:, b * lanes:(b + 1) * lanes] for b in range(blocks)], axis=0)
    upto = lax.broadcasted_iota(I32, (lanes, lanes), 0) <= lax.broadcasted_iota(I32, (lanes, lanes), 1)
    within = jnp.dot(stacked.astype(BF16), upto.astype(F32).astype(BF16), preferred_element_type=F32)
    carry = jnp.zeros((experts, 1), F32)
    parts = []
    for b in range(blocks):
        part = within[b * experts:(b + 1) * experts]
        parts.append(part + carry)
        carry = carry + part[:, lanes - 1:lanes]
    counted = jnp.concatenate(parts, axis=1)
    rank = jnp.sum(jnp.where(named, counted - 1.0, 0.0), axis=0, keepdims=True)
    return owners * capacity + rank.astype(I32)


def place(key, rows_ref, experts, capacity, out_refs):
    tokens, hidden = rows_ref.shape
    places = lax.broadcasted_iota(I32, (capacity, tokens), 0)
    chosen = jnp.concatenate(
        [(places == key - e * capacity).astype(F32).astype(BF16) for e in experts], axis=0
    )
    width = 2 * BLOCK
    for c in range(0, hidden, width):
        got = jnp.dot(chosen, rows_ref[:, c:c + width], preferred_element_type=F32).astype(BF16)
        for k, out_ref in enumerate(out_refs):
            out_ref[:, c:c + width] = got[k * capacity:(k + 1) * capacity]


def first_kernel(peers, slots, all_experts, capacity, me_ref, owner_ref, rows_ref, key_ref, *out_refs):
    me = me_ref[0]
    key = slots_of(owner_ref[...], all_experts, capacity)
    key_ref[...] = key
    place(key, rows_ref, [lax.bitwise_xor(me, k) * slots for k in range(1, peers)], capacity, out_refs)


def second_kernel(peers, slots, capacity, me_ref, key_ref, rows_ref, *out_refs):
    me = me_ref[0]
    where = [(0, a) for a in range(slots)] + [(k, a) for a in range(1, slots) for k in range(1, peers)]
    place(key_ref[...], rows_ref, [lax.bitwise_xor(me, k) * slots + a for k, a in where], capacity, out_refs)


def layout(hidden, halvings):
    blocks = hidden // BLOCK
    off = [(i, j) for i in range(blocks) for j in range(i + 1, blocks)]
    pairs = [(i, i + 1 if i + 1 < blocks else None) for i in range(0, blocks, 2)]
    tail = (len(off) + len(pairs)) * BLOCK
    unit = TILE << halvings
    return off, pairs, tail, -(-tail // unit) * unit


def eye_of(compare):
    return compare(lax.broadcasted_iota(I32, (BLOCK, BLOCK), 0), lax.broadcasted_iota(I32, (BLOCK, BLOCK), 1))


def bit_of(where, bit):
    return lax.bitwise_and(lax.shift_right_logical(where, bit), 1)


def diagonal_rows(hidden):
    return -(-(hidden // BLOCK) // 8) * 8


def exponent_of(diagonal):
    return jnp.ceil(0.5 * jnp.log2(jnp.maximum(diagonal, tiny)))


def spread(hidden, halvings, factor, out_ref):
    off, pairs, tail, length = layout(hidden, halvings)
    if length > tail:
        out_ref[tail:length] = jnp.zeros((length - tail, BLOCK), F32)
    across = [jnp.broadcast_to(factor[b:b + 1], (BLOCK, BLOCK)) for b in range(hidden // BLOCK)]
    down = [a.T for a in across]
    for n, (i, j) in enumerate(off):
        out_ref[n * BLOCK:(n + 1) * BLOCK] = down[i] * across[j]
    for n, (first, second) in enumerate(pairs):
        block = down[first] * across[first]
        if second is not None:
            block = jnp.where(eye_of(lax.lt), block, down[second] * across[second])
        row = (len(off) + n) * BLOCK
        out_ref[row:row + BLOCK] = block


def add_gram(halvings, chunk_refs, before, packed):
    hidden = chunk_refs[0].shape[1]
    off, pairs, tail, length = layout(hidden, halvings)
    at = {pair: n for n, pair in enumerate(off)}
    x = jnp.concatenate([r[...] for r in chunk_refs], axis=0) if len(chunk_refs) > 1 else chunk_refs[0][...]
    strip = 2 * BLOCK

    def put(n, value):
        rows = slice(n * BLOCK, (n + 1) * BLOCK)
        packed[rows] = value if before is None else before[rows] + value

    def put_diagonal(i, block):
        value = jnp.sum(jnp.where(eye_of(lax.eq), block, 0.0), axis=0, keepdims=True)
        row = slice(length + i, length + i + 1)
        packed[row] = value if before is None else before[row] + value

    packed[tail:] = jnp.zeros((packed.shape[0] - tail, BLOCK), F32)
    for n, (first, second) in enumerate(pairs):
        low, high = first * BLOCK, min(first * BLOCK + strip, hidden)
        product = lax.dot_general(
            x[:, low:high], x[:, low:], (((0,), (0,)), ((), ())), preferred_element_type=F32
        )
        for i in range((high - low) // BLOCK):
            for j in range((hidden - low) // BLOCK):
                pair = (first + i, first + j)
                if pair in at:
                    put(at[pair], product[i * BLOCK:(i + 1) * BLOCK, j * BLOCK:(j + 1) * BLOCK])
        mixed = product[:BLOCK, :BLOCK]
        put_diagonal(first, mixed)
        if second is not None:
            other = product[BLOCK:, BLOCK:2 * BLOCK]
            put_diagonal(second, other)
            mixed = jnp.where(eye_of(lax.lt), mixed, other)
        put(len(off) + n, jnp.where(eye_of(lax.eq), 0.0, mixed))


def early_gram_kernel(halvings, *refs):
    add_gram(halvings, refs[:-1], None, refs[-1])


def late_gram_kernel(halvings, pieces, where_ref, before_ref, *refs):
    chunk_refs, (keep_ref, diagonal_ref, *send_refs, packed) = refs[:pieces], refs[pieces:]
    add_gram(halvings, chunk_refs, before_ref, packed)
    half, rows = keep_ref.shape[0], diagonal_ref.shape[0]
    mine = bit_of(where_ref[0], 0)
    keep_ref[...] = packed[pl.ds(pl.multiple_of(mine * half, TILE), half)]
    diagonal = packed[2 * half:]
    diagonal_ref[...] = diagonal
    start = 0
    for n, send_ref in enumerate(send_refs):
        size = send_ref.shape[0] - (rows if n == 0 else 0)
        send_ref[:size] = packed[pl.ds(pl.multiple_of((1 - mine) * half + start, TILE), size)]
        if n == 0:
            send_ref[size:] = diagonal
        start += size


def encode(values, ref, exponent=None, digits=()):
    rows = values.shape[0]
    largest = jnp.max(jnp.abs(values), axis=0, keepdims=True)
    steps = jnp.ceil(OCTAVE * jnp.log2(jnp.maximum(largest, tiny)))
    factor = jnp.exp2(steps * (-1.0 / OCTAVE)) * LEVELS
    ref[:rows] = jnp.floor(values * factor + 0.5).astype(I32).astype(I16)
    notes = [jnp.broadcast_to(steps, (8, BLOCK))]
    if exponent is None:
        notes += notes
    else:
        notes += [exponent, *digits]
    notes = jnp.concatenate(notes, axis=0)
    if notes.shape[0] < ref.shape[0] - rows:
        notes = jnp.concatenate([notes, jnp.zeros((ref.shape[0] - rows - notes.shape[0], BLOCK), F32)], axis=0)
    ref[rows:] = notes.astype(I32).astype(I16)


def decode(ref, rows):
    notes = ref[rows:].astype(I32).astype(F32)
    return ref[:rows].astype(I32).astype(F32) * (jnp.exp2(notes[:1] * (1.0 / OCTAVE)) * (1.0 / LEVELS)), notes[8:]


def digits_of(diagonal, exponent):
    value = diagonal * jnp.exp2(-2.0 * exponent) * LEVELS
    first = jnp.floor(value + 0.5)
    return first, jnp.floor((value - first) * LEVELS + 0.5)


def from_digits(first, second, exponent):
    return (first + second * (1.0 / LEVELS)) * (1.0 / LEVELS) * jnp.exp2(2.0 * exponent)


def stage_kernel(hidden, halvings, bit, first, cut, parts, where_ref, keep_ref, diagonal_ref, *refs):
    got_refs, refs = refs[:parts], refs[parts:]
    sent_ref, diagonal_out, *kept, factors, total = refs
    rows, many = keep_ref.shape[0], diagonal_ref.shape[0]
    length = layout(hidden, halvings)[3]
    where = where_ref[0]
    place = sum(bit_of(where, b) * (length >> (b + 1)) for b in range(bit))
    here = pl.ds(pl.multiple_of(place, TILE), rows)
    diagonal = diagonal_ref[...]
    if first:
        start = 0
        for n, ref in enumerate(got_refs):
            size = ref.shape[0] - (many if n == 0 else 0)
            total[start:start + size] = keep_ref[start:start + size] + ref[:size]
            if n == 0:
                diagonal = diagonal + ref[size:]
            start += size
    else:
        value, notes = decode(got_refs[0], rows)
        theirs = notes[:many]
        spread(hidden, halvings, jnp.exp2(theirs), factors)
        total[...] = keep_ref[...] + value * factors[here]
        exponent = exponent_of(diagonal)
        ours = from_digits(*digits_of(diagonal, exponent), exponent)
        diagonal = ours + from_digits(notes[many:2 * many], notes[2 * many:3 * many], theirs)
    diagonal_out[...] = diagonal
    exponent = exponent_of(diagonal)
    spread(hidden, halvings, jnp.exp2(-exponent), factors)
    if cut:
        half = rows // 2
        mine = bit_of(where, bit)
        kept[0][...] = total[pl.ds(pl.multiple_of(mine * half, TILE), half)]
        away = (1 - mine) * half
        value = total[pl.ds(pl.multiple_of(away, TILE), half)] * factors[pl.ds(pl.multiple_of(place + away, TILE), half)]
        encode(value, sent_ref, exponent, digits_of(diagonal, exponent))
    elif kept:
        kept[0][...] = total[...]
        encode(total[...] * factors[here], sent_ref, exponent, digits_of(diagonal, exponent))
    else:
        encode(total[...] * factors[here], sent_ref)


def unpack_kernel(hidden, halvings, flips, where_ref, diagonal_ref, *refs):
    piece_refs, (high_ref, low_ref, packed) = refs[:len(flips)], refs[len(flips):]
    off, pairs, tail, length = layout(hidden, halvings)
    where = where_ref[0]
    rows = length >> halvings
    for flip, piece_ref in zip(flips, piece_refs):
        owner = lax.bitwise_xor(where, flip)
        start = sum(bit_of(owner, b) * (length >> (b + 1)) for b in range(halvings))
        packed[pl.ds(pl.multiple_of(start, TILE), rows)] = decode(piece_ref, rows)[0]

    def put(i, j, block):
        rows, cols = slice(i * BLOCK, (i + 1) * BLOCK), slice(j * BLOCK, (j + 1) * BLOCK)
        hi = block.astype(BF16)
        high_ref[rows, cols] = hi
        low_ref[rows, cols] = (block - hi.astype(F32)).astype(BF16)

    for n, (i, j) in enumerate(off):
        block = packed[n * BLOCK:(n + 1) * BLOCK]
        put(i, j, block)
        put(j, i, block.T)
    diagonal = diagonal_ref[...]
    ones = diagonal * jnp.exp2(-2.0 * exponent_of(diagonal))
    for n, (first, second) in enumerate(pairs):
        row = (len(off) + n) * BLOCK
        block = packed[row:row + BLOCK]
        turned = block.T
        for i, above in ((first, lax.lt), (second, lax.gt)):
            if i is not None:
                whole = jnp.where(eye_of(above), block, turned)
                put(i, i, jnp.where(eye_of(lax.eq), ones[i:i + 1], whole))


def sweeps_kernel(slot, diagonal_ref, weight_ref, mask_ref, high_ref, low_ref, *refs):
    out_ref, token_ref, result, done = refs[-4:]
    diagonal = jnp.concatenate([diagonal_ref[b:b + 1] for b in range(weight_ref.shape[-1] // BLOCK)], axis=1)
    back = jnp.exp2(exponent_of(diagonal))
    factor = relax_factor * (1.0 / (diagonal + diagonal_eps)) * back
    weight = weight_ref[slot].astype(F32)
    keep = mask_ref[slot].astype(F32)
    pruned = keep * weight
    for sweep in range(STEPS):
        change = (pruned - weight) * back
        top = change.astype(BF16)
        if sweep == 0:
            gradient = jnp.dot(top, high_ref[...], preferred_element_type=F32)
        else:
            rest = (change - top.astype(F32)).astype(BF16)
            both = jnp.dot(jnp.concatenate([top, rest], axis=0), high_ref[...], preferred_element_type=F32)
            gradient = both[:top.shape[0]] + both[top.shape[0]:]
        gradient = gradient + jnp.dot(top, low_ref[...], preferred_element_type=F32)
        pruned = keep * (pruned - gradient * factor)
    result[...] = pruned
    token_ref[...] = pruned[:8, :BLOCK]
    copy = pltpu.make_async_copy(result, out_ref.at[slot], done)
    copy.start()
    copy.wait()


def on_device(expert_inputs, row_expert, down_weight, keep_mask):
    tokens, hidden = expert_inputs.shape
    slots, features, _ = down_weight.shape
    peers = lax.axis_size("expert")
    copies = lax.axis_size("rows")
    all_experts = slots * peers
    capacity = tokens // 8
    halvings = copies.bit_length() - 2
    length = layout(hidden, halvings)[3]
    me = jnp.reshape(lax.axis_index("expert").astype(I32), (1,))
    where = jnp.reshape(lax.axis_index("rows").astype(I32), (1,))
    owners = row_expert.reshape(1, tokens)

    def shape(rows, columns=BLOCK, dtype=F32):
        return jax.ShapeDtypeStruct((rows, columns), dtype)

    def over_experts(array, flip):
        return lax.ppermute(array, "expert", [(i, i ^ flip) for i in range(peers)])

    def over_rows(array, bit):
        return lax.ppermute(array, "rows", [(i, i ^ (1 << bit)) for i in range(copies)])

    chunk = shape(capacity, hidden, BF16)
    place_flops = 2 * capacity * tokens * hidden
    key, *outgoing = call(
        functools.partial(first_kernel, peers, slots, all_experts, capacity),
        [shape(1, tokens, I32)] + [chunk] * (peers - 1), [SMEM, VMEM, VMEM],
        flops=place_flops * (peers - 1), moved=expert_inputs.size * 4, name="place_first",
    )(me, owners, expert_inputs)
    arrived = [[over_experts(outgoing[k - 1], k) for k in range(1, peers)]]
    count = slots + (slots - 1) * (peers - 1)
    rest = call(
        functools.partial(second_kernel, peers, slots, capacity), [chunk] * count, [SMEM, VMEM, VMEM],
        flops=place_flops * count, moved=expert_inputs.size * 4, name="place_rest",
    )(me, key, expert_inputs)
    own = rest[:slots]
    for a in range(1, slots):
        outgoing = rest[slots + (a - 1) * (peers - 1):slots + a * (peers - 1)]
        arrived.append([over_experts(outgoing[k - 1], k) for k in range(1, peers)])

    many = diagonal_rows(hidden)
    notes = -(-(8 + 3 * many) // TILE) * TILE

    def begin(a, after):
        chunks = [own[a]] + arrived[a][:-1]
        return call(
            functools.partial(early_gram_kernel, halvings), shape(length + many), [VMEM] * len(chunks),
            flops=2 * capacity * len(chunks) * hidden * hidden, moved=length * BLOCK * 4, name=f"begin_{a}", after=after,
        )(*chunks)

    def stage(name, bit, keep, diagonal, got, cut, kept, after=()):
        rows = keep.shape[0]
        left = rows // 2 if cut else rows
        return call(
            functools.partial(stage_kernel, hidden, halvings, bit, got[0].dtype == F32, cut, len(got)),
            [shape(left + (notes if kept else TILE), dtype=I16), shape(many)] + ([shape(left)] if kept else []),
            [SMEM] + [VMEM] * (2 + len(got)),
            scratch=[pltpu.VMEM((length, BLOCK), F32), pltpu.VMEM((rows, BLOCK), F32)],
            moved=rows * BLOCK * 12, name=name, after=after,
        )(where, keep, diagonal, *got)

    def reduce(a, before, after):
        size = length // 2
        sizes = cuts(size, PARTS)
        keep, diagonal, *sent = call(
            functools.partial(late_gram_kernel, halvings, 1),
            [shape(size), shape(many)] + [shape(n + (many if i == 0 else 0)) for i, n in enumerate(sizes)],
            [SMEM] + [VMEM] * 2, scratch=[pltpu.VMEM((length + many, BLOCK), F32)],
            flops=2 * capacity * hidden * hidden, moved=length * BLOCK * 4, name=f"gram_{a}", after=after,
        )(where, before, arrived[a][-1])
        for bit in range(1, halvings + 1):
            cut = bit < halvings
            got = [over_rows(part, bit - 1) for part in sent]
            coded, diagonal, keep = stage(f"stage_{a}_{bit}", bit, keep, diagonal, got, cut, True)
            sent = [coded]
            if bit == 1:
                halved = coded
        return halved, (coded, diagonal, keep)

    def end(a, sums, after):
        coded, diagonal, keep = sums
        return stage(f"total_{a}", halvings, keep, diagonal, [over_rows(coded, halvings)], False, False, after)

    def gather(a, total, after):
        coded, diagonal = total
        held = [(0, coded)]
        for bit in range(halvings - 1, -1, -1):
            held += [(flip ^ (1 << bit), over_rows(piece, bit)) for flip, piece in held]
        high, low = call(
            functools.partial(unpack_kernel, hidden, halvings, [flip for flip, _ in held]),
            [shape(hidden, hidden, BF16)] * 2, [SMEM] + [VMEM] * (1 + len(held)),
            scratch=[pltpu.VMEM((length, BLOCK), F32)], moved=length * BLOCK * 4, name=f"unpack_{a}", after=after,
        )(where, diagonal, *[piece for _, piece in held])
        return diagonal, high, low

    def sweeps(a, diagonal, high, low, result):
        args = [diagonal, down_weight, keep_mask, high, low] + ([] if result is None else [result])
        return call(
            functools.partial(sweeps_kernel, a),
            [jax.ShapeDtypeStruct((slots, features, hidden), F32), shape(8)],
            [VMEM] * 5 + [ANY] * (len(args) - 5),
            out_specs=[ANY, VMEM],
            scratch=[pltpu.VMEM((features, hidden), F32), pltpu.SemaphoreType.DMA],
            aliases={} if result is None else {5: 0},
            flops=2 * 3 * STEPS * features * hidden * hidden, moved=hidden * hidden * 4, name=f"sweeps_{a}",
        )(*args)

    result, total, halved = None, (), ()
    for a in range(slots):
        before = begin(a, halved)
        halved, sums = reduce(a, before, total[:1])
        halved, token = [halved], ()
        if a > 0:
            result, *token = sweeps(a - 1, *gather(a - 1, total, [sums[0]]), result)
        total = end(a, sums, token)
    return sweeps(slots - 1, *gather(slots - 1, total, ()), result)[0]


def solution(mesh):
    return jax.shard_map(
        on_device,
        mesh=mesh,
        in_specs=(
            P(("expert", "rows"), None),
            P(("expert", "rows"), None),
            P("expert", "rows", None),
            P("expert", "rows", None),
        ),
        out_specs=P("expert", "rows", None),
        check_vma=False,
    )
```

```python
import functools

import jax
import jax.numpy as jnp
from jax import lax
from jax.experimental import pallas as pl
from jax.experimental.pallas import tpu as pltpu
from jax.sharding import PartitionSpec as P

STEPS = 4
BLOCK = 128
TILE = 16
PARTS = 2
LEVELS = 32760.0
OCTAVE = 8.0
relax_factor = 0.5
diagonal_eps = 1e-06
tiny = 1e-30
VMEM_LIMIT = 50 * 2**20

VMEM = pl.BlockSpec(memory_space=pltpu.VMEM)
ANY = pl.BlockSpec(memory_space=pl.ANY)
SMEM = pl.BlockSpec(memory_space=pltpu.SMEM)
F32, BF16, I32, I16 = jnp.float32, jnp.bfloat16, jnp.int32, jnp.int16


def call(kernel, out_shape, in_specs, scratch=(), flops=0, moved=0, out_specs=None, aliases=None, name=None, after=()):
    many = isinstance(out_shape, (list, tuple))
    used, idle = len(in_specs), len(after)

    def body(*refs):
        kernel(*refs[:used], *refs[used + idle:])

    inner = pl.pallas_call(
        body,
        out_shape=out_shape,
        in_specs=list(in_specs) + [ANY] * idle,
        out_specs=out_specs if out_specs is not None else ([VMEM] * len(out_shape) if many else VMEM),
        scratch_shapes=list(scratch),
        input_output_aliases=aliases or {},
        cost_estimate=pl.CostEstimate(flops=flops, bytes_accessed=moved, transcendentals=0),
        compiler_params=pltpu.CompilerParams(vmem_limit_bytes=VMEM_LIMIT),
        name=name,
    )
    return lambda *args: inner(*args, *after)


def cuts(size, chunks):
    ends = [size * (c + 1) // (TILE * chunks) * TILE for c in range(chunks)]
    return [end - start for start, end in zip([0] + ends, ends)]


def slots_of(owners, experts, capacity):
    tokens = owners.shape[1]
    lanes = 128
    blocks = tokens // lanes
    named = owners == lax.broadcasted_iota(I32, (experts, tokens), 0)
    ones = named.astype(F32)
    stacked = jnp.concatenate([ones[:, b * lanes:(b + 1) * lanes] for b in range(blocks)], axis=0)
    upto = lax.broadcasted_iota(I32, (lanes, lanes), 0) <= lax.broadcasted_iota(I32, (lanes, lanes), 1)
    within = jnp.dot(stacked.astype(BF16), upto.astype(F32).astype(BF16), preferred_element_type=F32)
    carry = jnp.zeros((experts, 1), F32)
    parts = []
    for b in range(blocks):
        part = within[b * experts:(b + 1) * experts]
        parts.append(part + carry)
        carry = carry + part[:, lanes - 1:lanes]
    counted = jnp.concatenate(parts, axis=1)
    rank = jnp.sum(jnp.where(named, counted - 1.0, 0.0), axis=0, keepdims=True)
    return owners * capacity + rank.astype(I32)


def place(key, rows_ref, experts, capacity, out_refs):
    tokens, hidden = rows_ref.shape
    places = lax.broadcasted_iota(I32, (capacity, tokens), 0)
    chosen = jnp.concatenate(
        [(places == key - e * capacity).astype(F32).astype(BF16) for e in experts], axis=0
    )
    width = 2 * BLOCK
    for c in range(0, hidden, width):
        got = jnp.dot(chosen, rows_ref[:, c:c + width], preferred_element_type=F32).astype(BF16)
        for k, out_ref in enumerate(out_refs):
            out_ref[:, c:c + width] = got[k * capacity:(k + 1) * capacity]


def first_kernel(peers, slots, all_experts, capacity, me_ref, owner_ref, rows_ref, key_ref, *out_refs):
    me = me_ref[0]
    key = slots_of(owner_ref[...], all_experts, capacity)
    key_ref[...] = key
    place(key, rows_ref, [lax.bitwise_xor(me, k) * slots for k in range(1, peers)], capacity, out_refs)


def second_kernel(peers, slots, capacity, me_ref, key_ref, rows_ref, *out_refs):
    me = me_ref[0]
    where = [(0, a) for a in range(slots)] + [(k, a) for a in range(1, slots) for k in range(1, peers)]
    place(key_ref[...], rows_ref, [lax.bitwise_xor(me, k) * slots + a for k, a in where], capacity, out_refs)


def layout(hidden, halvings):
    blocks = hidden // BLOCK
    off = [(i, j) for i in range(blocks) for j in range(i + 1, blocks)]
    pairs = [(i, i + 1 if i + 1 < blocks else None) for i in range(0, blocks, 2)]
    tail = (len(off) + len(pairs)) * BLOCK
    unit = TILE << halvings
    return off, pairs, tail, -(-tail // unit) * unit


def eye_of(compare):
    return compare(lax.broadcasted_iota(I32, (BLOCK, BLOCK), 0), lax.broadcasted_iota(I32, (BLOCK, BLOCK), 1))


def bit_of(where, bit):
    return lax.bitwise_and(lax.shift_right_logical(where, bit), 1)


def diagonal_rows(hidden):
    return -(-(hidden // BLOCK) // 8) * 8


def exponent_of(diagonal):
    return jnp.ceil(0.5 * jnp.log2(jnp.maximum(diagonal, tiny)))


def spread(hidden, halvings, factor, out_ref):
    off, pairs, tail, length = layout(hidden, halvings)
    if length > tail:
        out_ref[tail:length] = jnp.zeros((length - tail, BLOCK), F32)
    across = [jnp.broadcast_to(factor[b:b + 1], (BLOCK, BLOCK)) for b in range(hidden // BLOCK)]
    down = [a.T for a in across]
    for n, (i, j) in enumerate(off):
        out_ref[n * BLOCK:(n + 1) * BLOCK] = down[i] * across[j]
    for n, (first, second) in enumerate(pairs):
        block = down[first] * across[first]
        if second is not None:
            block = jnp.where(eye_of(lax.lt), block, down[second] * across[second])
        row = (len(off) + n) * BLOCK
        out_ref[row:row + BLOCK] = block


def add_gram(halvings, chunk_refs, before, packed):
    hidden = chunk_refs[0].shape[1]
    off, pairs, tail, length = layout(hidden, halvings)
    at = {pair: n for n, pair in enumerate(off)}
    x = jnp.concatenate([r[...] for r in chunk_refs], axis=0) if len(chunk_refs) > 1 else chunk_refs[0][...]
    strip = 2 * BLOCK

    def put(n, value):
        rows = slice(n * BLOCK, (n + 1) * BLOCK)
        packed[rows] = value if before is None else before[rows] + value

    def put_diagonal(i, block):
        value = jnp.sum(jnp.where(eye_of(lax.eq), block, 0.0), axis=0, keepdims=True)
        row = slice(length + i, length + i + 1)
        packed[row] = value if before is None else before[row] + value

    packed[tail:] = jnp.zeros((packed.shape[0] - tail, BLOCK), F32)
    for n, (first, second) in enumerate(pairs):
        low, high = first * BLOCK, min(first * BLOCK + strip, hidden)
        product = lax.dot_general(
            x[:, low:high], x[:, low:], (((0,), (0,)), ((), ())), preferred_element_type=F32
        )
        for i in range((high - low) // BLOCK):
            for j in range((hidden - low) // BLOCK):
                pair = (first + i, first + j)
                if pair in at:
                    put(at[pair], product[i * BLOCK:(i + 1) * BLOCK, j * BLOCK:(j + 1) * BLOCK])
        mixed = product[:BLOCK, :BLOCK]
        put_diagonal(first, mixed)
        if second is not None:
            other = product[BLOCK:, BLOCK:2 * BLOCK]
            put_diagonal(second, other)
            mixed = jnp.where(eye_of(lax.lt), mixed, other)
        put(len(off) + n, jnp.where(eye_of(lax.eq), 0.0, mixed))


def early_gram_kernel(halvings, *refs):
    add_gram(halvings, refs[:-1], None, refs[-1])


def late_gram_kernel(halvings, pieces, where_ref, before_ref, *refs):
    chunk_refs, (keep_ref, diagonal_ref, *send_refs, packed) = refs[:pieces], refs[pieces:]
    add_gram(halvings, chunk_refs, before_ref, packed)
    half, rows = keep_ref.shape[0], diagonal_ref.shape[0]
    mine = bit_of(where_ref[0], 0)
    keep_ref[...] = packed[pl.ds(pl.multiple_of(mine * half, TILE), half)]
    diagonal = packed[2 * half:]
    diagonal_ref[...] = diagonal
    start = 0
    for n, send_ref in enumerate(send_refs):
        size = send_ref.shape[0] - (rows if n == 0 else 0)
        send_ref[:size] = packed[pl.ds(pl.multiple_of((1 - mine) * half + start, TILE), size)]
        if n == 0:
            send_ref[size:] = diagonal
        start += size


def encode(values, ref, exponent=None, digits=()):
    rows = values.shape[0]
    largest = jnp.max(jnp.abs(values), axis=0, keepdims=True)
    steps = jnp.ceil(OCTAVE * jnp.log2(jnp.maximum(largest, tiny)))
    factor = jnp.exp2(steps * (-1.0 / OCTAVE)) * LEVELS
    ref[:rows] = jnp.floor(values * factor + 0.5).astype(I32).astype(I16)
    notes = [jnp.broadcast_to(steps, (8, BLOCK))]
    if exponent is None:
        notes += notes
    else:
        notes += [exponent, *digits]
    notes = jnp.concatenate(notes, axis=0)
    if notes.shape[0] < ref.shape[0] - rows:
        notes = jnp.concatenate([notes, jnp.zeros((ref.shape[0] - rows - notes.shape[0], BLOCK), F32)], axis=0)
    ref[rows:] = notes.astype(I32).astype(I16)


def decode(ref, rows):
    notes = ref[rows:].astype(I32).astype(F32)
    return ref[:rows].astype(I32).astype(F32) * (jnp.exp2(notes[:1] * (1.0 / OCTAVE)) * (1.0 / LEVELS)), notes[8:]


def digits_of(diagonal, exponent):
    value = diagonal * jnp.exp2(-2.0 * exponent) * LEVELS
    first = jnp.floor(value + 0.5)
    return first, jnp.floor((value - first) * LEVELS + 0.5)


def from_digits(first, second, exponent):
    return (first + second * (1.0 / LEVELS)) * (1.0 / LEVELS) * jnp.exp2(2.0 * exponent)


def stage_kernel(hidden, halvings, bit, first, cut, parts, where_ref, keep_ref, diagonal_ref, *refs):
    got_refs, refs = refs[:parts], refs[parts:]
    sent_ref, diagonal_out, *kept, factors, total = refs
    rows, many = keep_ref.shape[0], diagonal_ref.shape[0]
    length = layout(hidden, halvings)[3]
    where = where_ref[0]
    place = sum(bit_of(where, b) * (length >> (b + 1)) for b in range(bit))
    here = pl.ds(pl.multiple_of(place, TILE), rows)
    diagonal = diagonal_ref[...]
    if first:
        start = 0
        for n, ref in enumerate(got_refs):
            size = ref.shape[0] - (many if n == 0 else 0)
            total[start:start + size] = keep_ref[start:start + size] + ref[:size]
            if n == 0:
                diagonal = diagonal + ref[size:]
            start += size
    else:
        value, notes = decode(got_refs[0], rows)
        theirs = notes[:many]
        spread(hidden, halvings, jnp.exp2(theirs), factors)
        total[...] = keep_ref[...] + value * factors[here]
        exponent = exponent_of(diagonal)
        ours = from_digits(*digits_of(diagonal, exponent), exponent)
        diagonal = ours + from_digits(notes[many:2 * many], notes[2 * many:3 * many], theirs)
    diagonal_out[...] = diagonal
    exponent = exponent_of(diagonal)
    spread(hidden, halvings, jnp.exp2(-exponent), factors)
    if cut:
        half = rows // 2
        mine = bit_of(where, bit)
        kept[0][...] = total[pl.ds(pl.multiple_of(mine * half, TILE), half)]
        away = (1 - mine) * half
        value = total[pl.ds(pl.multiple_of(away, TILE), half)] * factors[pl.ds(pl.multiple_of(place + away, TILE), half)]
        encode(value, sent_ref, exponent, digits_of(diagonal, exponent))
    elif kept:
        kept[0][...] = total[...]
        encode(total[...] * factors[here], sent_ref, exponent, digits_of(diagonal, exponent))
    else:
        encode(total[...] * factors[here], sent_ref)


def unpack_kernel(hidden, halvings, flips, where_ref, diagonal_ref, *refs):
    piece_refs, (high_ref, low_ref, packed) = refs[:len(flips)], refs[len(flips):]
    off, pairs, tail, length = layout(hidden, halvings)
    where = where_ref[0]
    rows = length >> halvings
    for flip, piece_ref in zip(flips, piece_refs):
        owner = lax.bitwise_xor(where, flip)
        start = sum(bit_of(owner, b) * (length >> (b + 1)) for b in range(halvings))
        packed[pl.ds(pl.multiple_of(start, TILE), rows)] = decode(piece_ref, rows)[0]

    def put(i, j, block):
        rows, cols = slice(i * BLOCK, (i + 1) * BLOCK), slice(j * BLOCK, (j + 1) * BLOCK)
        hi = block.astype(BF16)
        high_ref[rows, cols] = hi
        low_ref[rows, cols] = (block - hi.astype(F32)).astype(BF16)

    for n, (i, j) in enumerate(off):
        block = packed[n * BLOCK:(n + 1) * BLOCK]
        put(i, j, block)
        put(j, i, block.T)
    diagonal = diagonal_ref[...]
    ones = diagonal * jnp.exp2(-2.0 * exponent_of(diagonal))
    for n, (first, second) in enumerate(pairs):
        row = (len(off) + n) * BLOCK
        block = packed[row:row + BLOCK]
        turned = block.T
        for i, above in ((first, lax.lt), (second, lax.gt)):
            if i is not None:
                whole = jnp.where(eye_of(above), block, turned)
                put(i, i, jnp.where(eye_of(lax.eq), ones[i:i + 1], whole))


def sweeps_kernel(slot, diagonal_ref, weight_ref, mask_ref, high_ref, low_ref, *refs):
    out_ref, token_ref, result, done = refs[-4:]
    diagonal = jnp.concatenate([diagonal_ref[b:b + 1] for b in range(weight_ref.shape[-1] // BLOCK)], axis=1)
    back = jnp.exp2(exponent_of(diagonal))
    factor = relax_factor * (1.0 / (diagonal + diagonal_eps)) * back
    weight = weight_ref[slot].astype(F32)
    keep = mask_ref[slot].astype(F32)
    pruned = keep * weight
    for sweep in range(STEPS):
        change = (pruned - weight) * back
        top = change.astype(BF16)
        if sweep == 0:
            gradient = jnp.dot(top, high_ref[...], preferred_element_type=F32)
        else:
            rest = (change - top.astype(F32)).astype(BF16)
            both = jnp.dot(jnp.concatenate([top, rest], axis=0), high_ref[...], preferred_element_type=F32)
            gradient = both[:top.shape[0]] + both[top.shape[0]:]
        gradient = gradient + jnp.dot(top, low_ref[...], preferred_element_type=F32)
        pruned = keep * (pruned - gradient * factor)
    result[...] = pruned
    token_ref[...] = pruned[:8, :BLOCK]
    copy = pltpu.make_async_copy(result, out_ref.at[slot], done)
    copy.start()
    copy.wait()


def on_device(expert_inputs, row_expert, down_weight, keep_mask):
    tokens, hidden = expert_inputs.shape
    slots, features, _ = down_weight.shape
    peers = lax.axis_size("expert")
    copies = lax.axis_size("rows")
    all_experts = slots * peers
    capacity = tokens // 8
    halvings = copies.bit_length() - 2
    length = layout(hidden, halvings)[3]
    me = jnp.reshape(lax.axis_index("expert").astype(I32), (1,))
    where = jnp.reshape(lax.axis_index("rows").astype(I32), (1,))
    owners = row_expert.reshape(1, tokens)

    def shape(rows, columns=BLOCK, dtype=F32):
        return jax.ShapeDtypeStruct((rows, columns), dtype)

    def over_experts(array, flip):
        return lax.ppermute(array, "expert", [(i, i ^ flip) for i in range(peers)])

    def over_rows(array, bit):
        return lax.ppermute(array, "rows", [(i, i ^ (1 << bit)) for i in range(copies)])

    chunk = shape(capacity, hidden, BF16)
    place_flops = 2 * capacity * tokens * hidden
    key, *outgoing = call(
        functools.partial(first_kernel, peers, slots, all_experts, capacity),
        [shape(1, tokens, I32)] + [chunk] * (peers - 1), [SMEM, VMEM, VMEM],
        flops=place_flops * (peers - 1), moved=expert_inputs.size * 4, name="place_first",
    )(me, owners, expert_inputs)
    arrived = [[over_experts(outgoing[k - 1], k) for k in range(1, peers)]]
    count = slots + (slots - 1) * (peers - 1)
    rest = call(
        functools.partial(second_kernel, peers, slots, capacity), [chunk] * count, [SMEM, VMEM, VMEM],
        flops=place_flops * count, moved=expert_inputs.size * 4, name="place_rest",
    )(me, key, expert_inputs)
    own = rest[:slots]
    for a in range(1, slots):
        outgoing = rest[slots + (a - 1) * (peers - 1):slots + a * (peers - 1)]
        arrived.append([over_experts(outgoing[k - 1], k) for k in range(1, peers)])

    many = diagonal_rows(hidden)
    notes = -(-(8 + 3 * many) // TILE) * TILE

    def begin(a, after):
        chunks = [own[a]] + arrived[a][:-1]
        return call(
            functools.partial(early_gram_kernel, halvings), shape(length + many), [VMEM] * len(chunks),
            name=f"begin_{a}", after=after,
        )(*chunks)

    def stage(name, bit, keep, diagonal, got, cut, kept, after=()):
        rows = keep.shape[0]
        left = rows // 2 if cut else rows
        return call(
            functools.partial(stage_kernel, hidden, halvings, bit, got[0].dtype == F32, cut, len(got)),
            [shape(left + (notes if kept else TILE), dtype=I16), shape(many)] + ([shape(left)] if kept else []),
            [SMEM] + [VMEM] * (2 + len(got)),
            scratch=[pltpu.VMEM((length, BLOCK), F32), pltpu.VMEM((rows, BLOCK), F32)],
            moved=rows * BLOCK * 12, name=name, after=after,
        )(where, keep, diagonal, *got)

    def reduce(a, before, after, behind):
        size = length // 2
        sizes = cuts(size, PARTS)
        keep, diagonal, *sent = call(
            functools.partial(late_gram_kernel, halvings, 1),
            [shape(size), shape(many)] + [shape(n + (many if i == 0 else 0)) for i, n in enumerate(sizes)],
            [SMEM] + [VMEM] * 2, scratch=[pltpu.VMEM((length + many, BLOCK), F32)],
            name=f"gram_{a}", after=after,
        )(where, before, arrived[a][-1])
        for bit in range(1, halvings + 1):
            cut = bit < halvings
            got = [over_rows(part, bit - 1) for part in sent]
            coded, diagonal, keep = stage(f"stage_{a}_{bit}", bit, keep, diagonal, got, cut, True, behind if bit == 1 else ())
            sent = [coded]
        return coded, diagonal, keep

    def end(a, sums, after):
        coded, diagonal, keep = sums
        return stage(f"total_{a}", halvings, keep, diagonal, [over_rows(coded, halvings)], False, False, after)

    def gather(a, total, after):
        coded, diagonal = total
        held = [(0, coded)]
        for bit in range(halvings - 1, -1, -1):
            held += [(flip ^ (1 << bit), over_rows(piece, bit)) for flip, piece in held]
        high, low = call(
            functools.partial(unpack_kernel, hidden, halvings, [flip for flip, _ in held]),
            [shape(hidden, hidden, BF16)] * 2, [SMEM] + [VMEM] * (1 + len(held)),
            scratch=[pltpu.VMEM((length, BLOCK), F32)], moved=length * BLOCK * 4, name=f"unpack_{a}", after=after,
        )(where, diagonal, *[piece for _, piece in held])
        return diagonal, high, low

    def sweeps(a, diagonal, high, low, result):
        args = [diagonal, down_weight, keep_mask, high, low] + ([] if result is None else [result])
        return call(
            functools.partial(sweeps_kernel, a),
            [jax.ShapeDtypeStruct((slots, features, hidden), F32), shape(8)],
            [VMEM] * 5 + [ANY] * (len(args) - 5),
            out_specs=[ANY, VMEM],
            scratch=[pltpu.VMEM((features, hidden), F32), pltpu.SemaphoreType.DMA],
            aliases={} if result is None else {5: 0},
            flops=2 * 3 * STEPS * features * hidden * hidden, moved=hidden * hidden * 4, name=f"sweeps_{a}",
        )(*args)

    result, total, started = None, (), [begin(a, ()) for a in range(slots)]
    for a in range(slots):
        sums = reduce(a, started[a], total[:1], started[a + 1:a + 2])
        token = ()
        if a > 0:
            result, *token = sweeps(a - 1, *gather(a - 1, total, [sums[0]]), result)
        total = end(a, sums, token)
    return sweeps(slots - 1, *gather(slots - 1, total, ()), result)[0]


def solution(mesh):
    return jax.shard_map(
        on_device,
        mesh=mesh,
        in_specs=(
            P(("expert", "rows"), None),
            P(("expert", "rows"), None),
            P("expert", "rows", None),
            P("expert", "rows", None),
        ),
        out_specs=P("expert", "rows", None),
        check_vma=False,
    )
```

```python
import functools

import jax
import jax.numpy as jnp
from jax import lax
from jax.experimental import pallas as pl
from jax.experimental.pallas import tpu as pltpu
from jax.sharding import PartitionSpec as P

STEPS = 4
BLOCK = 128
TILE = 16
PARTS = 4
WIDTH = 2 * BLOCK
LEVELS = 32760.0
OCTAVE = 8.0
relax_factor = 0.5
diagonal_eps = 1e-06
tiny = 1e-30
VMEM_LIMIT = 50 * 2**20

VMEM = pl.BlockSpec(memory_space=pltpu.VMEM)
ANY = pl.BlockSpec(memory_space=pl.ANY)
SMEM = pl.BlockSpec(memory_space=pltpu.SMEM)
F32, BF16, I32, I16 = jnp.float32, jnp.bfloat16, jnp.int32, jnp.int16


def call(kernel, out_shape, in_specs, scratch=(), flops=0, moved=0, out_specs=None, aliases=None, name=None, after=()):
    many = isinstance(out_shape, (list, tuple))
    used, idle = len(in_specs), len(after)

    def body(*refs):
        kernel(*refs[:used], *refs[used + idle:])

    inner = pl.pallas_call(
        body,
        out_shape=out_shape,
        in_specs=list(in_specs) + [ANY] * idle,
        out_specs=out_specs if out_specs is not None else ([VMEM] * len(out_shape) if many else VMEM),
        scratch_shapes=list(scratch),
        input_output_aliases=aliases or {},
        cost_estimate=pl.CostEstimate(flops=flops, bytes_accessed=moved, transcendentals=0),
        compiler_params=pltpu.CompilerParams(vmem_limit_bytes=VMEM_LIMIT),
        name=name,
    )
    return lambda *args: inner(*args, *after)


def cuts(size, chunks):
    ends = [size * (c + 1) // (TILE * chunks) * TILE for c in range(chunks)]
    return [end - start for start, end in zip([0] + ends, ends)]


def slots_of(owners, experts, capacity):
    tokens = owners.shape[1]
    lanes = 128
    blocks = tokens // lanes
    named = owners == lax.broadcasted_iota(I32, (experts, tokens), 0)
    ones = named.astype(F32)
    stacked = jnp.concatenate([ones[:, b * lanes:(b + 1) * lanes] for b in range(blocks)], axis=0)
    upto = lax.broadcasted_iota(I32, (lanes, lanes), 0) <= lax.broadcasted_iota(I32, (lanes, lanes), 1)
    within = jnp.dot(stacked.astype(BF16), upto.astype(F32).astype(BF16), preferred_element_type=F32)
    carry = jnp.zeros((experts, 1), F32)
    parts = []
    for b in range(blocks):
        part = within[b * experts:(b + 1) * experts]
        parts.append(part + carry)
        carry = carry + part[:, lanes - 1:lanes]
    counted = jnp.concatenate(parts, axis=1)
    rank = jnp.sum(jnp.where(named, counted - 1.0, 0.0), axis=0, keepdims=True)
    return owners * capacity + rank.astype(I32)


def place(key, rows_ref, experts, capacity, out_refs, ready=lambda c: None):
    tokens, hidden = rows_ref.shape
    places = lax.broadcasted_iota(I32, (capacity, tokens), 0)
    chosen = jnp.concatenate(
        [(places == key - e * capacity).astype(F32).astype(BF16) for e in experts], axis=0
    )
    for c in range(0, hidden, WIDTH):
        ready(c // WIDTH)
        got = jnp.dot(chosen, rows_ref[:, c:c + WIDTH], preferred_element_type=F32).astype(BF16)
        for k, out_ref in enumerate(out_refs):
            out_ref[:, c:c + WIDTH] = got[k * capacity:(k + 1) * capacity]


def first_kernel(peers, slots, all_experts, capacity, me_ref, owner_any, rows_any, key_ref, *refs):
    out_refs, (owner_ref, rows_ref, owner_done, rows_done) = refs[:-4], refs[-4:]
    owner_copy = pltpu.make_async_copy(owner_any, owner_ref, owner_done)
    owner_copy.start()
    copies = []
    for c in range(rows_ref.shape[1] // WIDTH):
        columns = pl.ds(c * WIDTH, WIDTH)
        copies.append(pltpu.make_async_copy(rows_any.at[:, columns], rows_ref.at[:, columns], rows_done.at[c]))
        copies[-1].start()
    me = me_ref[0]
    owner_copy.wait()
    key = slots_of(owner_ref[...], all_experts, capacity)
    key_ref[...] = key
    experts = [lax.bitwise_xor(me, k) * slots for k in range(1, peers)]
    place(key, rows_ref, experts, capacity, out_refs, lambda c: copies[c].wait())


def second_kernel(peers, slots, capacity, me_ref, key_ref, rows_ref, *out_refs):
    me = me_ref[0]
    where = [(0, a) for a in range(slots)] + [(k, a) for a in range(1, slots) for k in range(1, peers)]
    place(key_ref[...], rows_ref, [lax.bitwise_xor(me, k) * slots + a for k, a in where], capacity, out_refs)


def layout(hidden, halvings):
    blocks = hidden // BLOCK
    off = [(i, j) for i in range(blocks) for j in range(i + 1, blocks)]
    pairs = [(i, i + 1 if i + 1 < blocks else None) for i in range(0, blocks, 2)]
    tail = (len(off) + len(pairs)) * BLOCK
    unit = TILE << halvings
    return off, pairs, tail, -(-tail // unit) * unit


def eye_of(compare):
    return compare(lax.broadcasted_iota(I32, (BLOCK, BLOCK), 0), lax.broadcasted_iota(I32, (BLOCK, BLOCK), 1))


def bit_of(where, bit):
    return lax.bitwise_and(lax.shift_right_logical(where, bit), 1)


def diagonal_rows(hidden):
    return -(-(hidden // BLOCK) // 8) * 8


def exponent_of(diagonal):
    return jnp.ceil(0.5 * jnp.log2(jnp.maximum(diagonal, tiny)))


def spread(hidden, halvings, factor, out_ref):
    off, pairs, tail, length = layout(hidden, halvings)
    if length > tail:
        out_ref[tail:length] = jnp.zeros((length - tail, BLOCK), F32)
    across = [jnp.broadcast_to(factor[b:b + 1], (BLOCK, BLOCK)) for b in range(hidden // BLOCK)]
    down = [a.T for a in across]
    for n, (i, j) in enumerate(off):
        out_ref[n * BLOCK:(n + 1) * BLOCK] = down[i] * across[j]
    for n, (first, second) in enumerate(pairs):
        block = down[first] * across[first]
        if second is not None:
            block = jnp.where(eye_of(lax.lt), block, down[second] * across[second])
        row = (len(off) + n) * BLOCK
        out_ref[row:row + BLOCK] = block


def add_gram(halvings, chunk_refs, before, packed):
    hidden = chunk_refs[0].shape[1]
    off, pairs, tail, length = layout(hidden, halvings)
    at = {pair: n for n, pair in enumerate(off)}
    x = jnp.concatenate([r[...] for r in chunk_refs], axis=0) if len(chunk_refs) > 1 else chunk_refs[0][...]
    strip = 2 * BLOCK

    def put(n, value):
        rows = slice(n * BLOCK, (n + 1) * BLOCK)
        packed[rows] = value if before is None else before[rows] + value

    def put_diagonal(i, block):
        value = jnp.sum(jnp.where(eye_of(lax.eq), block, 0.0), axis=0, keepdims=True)
        row = slice(length + i, length + i + 1)
        packed[row] = value if before is None else before[row] + value

    packed[tail:] = jnp.zeros((packed.shape[0] - tail, BLOCK), F32)
    for n, (first, second) in enumerate(pairs):
        low, high = first * BLOCK, min(first * BLOCK + strip, hidden)
        product = lax.dot_general(
            x[:, low:high], x[:, low:], (((0,), (0,)), ((), ())), preferred_element_type=F32
        )
        for i in range((high - low) // BLOCK):
            for j in range((hidden - low) // BLOCK):
                pair = (first + i, first + j)
                if pair in at:
                    put(at[pair], product[i * BLOCK:(i + 1) * BLOCK, j * BLOCK:(j + 1) * BLOCK])
        mixed = product[:BLOCK, :BLOCK]
        put_diagonal(first, mixed)
        if second is not None:
            other = product[BLOCK:, BLOCK:2 * BLOCK]
            put_diagonal(second, other)
            mixed = jnp.where(eye_of(lax.lt), mixed, other)
        put(len(off) + n, jnp.where(eye_of(lax.eq), 0.0, mixed))


def early_gram_kernel(halvings, *refs):
    add_gram(halvings, refs[:-1], None, refs[-1])


def late_gram_kernel(halvings, pieces, where_ref, before_ref, *refs):
    chunk_refs, (keep_ref, diagonal_ref, *send_refs, packed) = refs[:pieces], refs[pieces:]
    add_gram(halvings, chunk_refs, before_ref, packed)
    half, rows = keep_ref.shape[0], diagonal_ref.shape[0]
    mine = bit_of(where_ref[0], 0)
    keep_ref[...] = packed[pl.ds(pl.multiple_of(mine * half, TILE), half)]
    diagonal = packed[2 * half:]
    diagonal_ref[...] = diagonal
    start = 0
    for n, send_ref in enumerate(send_refs):
        size = send_ref.shape[0] - (rows if n == 0 else 0)
        send_ref[:size] = packed[pl.ds(pl.multiple_of((1 - mine) * half + start, TILE), size)]
        if n == 0:
            send_ref[size:] = diagonal
        start += size


def encode(values, ref, exponent=None, digits=()):
    rows = values.shape[0]
    largest = jnp.max(jnp.abs(values), axis=0, keepdims=True)
    steps = jnp.ceil(OCTAVE * jnp.log2(jnp.maximum(largest, tiny)))
    factor = jnp.exp2(steps * (-1.0 / OCTAVE)) * LEVELS
    ref[:rows] = jnp.floor(values * factor + 0.5).astype(I32).astype(I16)
    notes = [jnp.broadcast_to(steps, (8, BLOCK))]
    if exponent is None:
        notes += notes
    else:
        notes += [exponent, *digits]
    notes = jnp.concatenate(notes, axis=0)
    if notes.shape[0] < ref.shape[0] - rows:
        notes = jnp.concatenate([notes, jnp.zeros((ref.shape[0] - rows - notes.shape[0], BLOCK), F32)], axis=0)
    ref[rows:] = notes.astype(I32).astype(I16)


def decode(ref, rows):
    notes = ref[rows:].astype(I32).astype(F32)
    return ref[:rows].astype(I32).astype(F32) * (jnp.exp2(notes[:1] * (1.0 / OCTAVE)) * (1.0 / LEVELS)), notes[8:]


def digits_of(diagonal, exponent):
    value = diagonal * jnp.exp2(-2.0 * exponent) * LEVELS
    first = jnp.floor(value + 0.5)
    return first, jnp.floor((value - first) * LEVELS + 0.5)


def from_digits(first, second, exponent):
    return (first + second * (1.0 / LEVELS)) * (1.0 / LEVELS) * jnp.exp2(2.0 * exponent)


def stage_kernel(hidden, halvings, bit, first, cut, parts, where_ref, keep_ref, diagonal_ref, *refs):
    got_refs, refs = refs[:parts], refs[parts:]
    sent_ref, diagonal_out, *kept, factors, total = refs
    rows, many = keep_ref.shape[0], diagonal_ref.shape[0]
    length = layout(hidden, halvings)[3]
    where = where_ref[0]
    place = sum(bit_of(where, b) * (length >> (b + 1)) for b in range(bit))
    here = pl.ds(pl.multiple_of(place, TILE), rows)
    diagonal = diagonal_ref[...]
    if first:
        start = 0
        for n, ref in enumerate(got_refs):
            size = ref.shape[0] - (many if n == 0 else 0)
            total[start:start + size] = keep_ref[start:start + size] + ref[:size]
            if n == 0:
                diagonal = diagonal + ref[size:]
            start += size
    else:
        value, notes = decode(got_refs[0], rows)
        theirs = notes[:many]
        spread(hidden, halvings, jnp.exp2(theirs), factors)
        total[...] = keep_ref[...] + value * factors[here]
        exponent = exponent_of(diagonal)
        ours = from_digits(*digits_of(diagonal, exponent), exponent)
        diagonal = ours + from_digits(notes[many:2 * many], notes[2 * many:3 * many], theirs)
    diagonal_out[...] = diagonal
    exponent = exponent_of(diagonal)
    spread(hidden, halvings, jnp.exp2(-exponent), factors)
    if cut:
        half = rows // 2
        mine = bit_of(where, bit)
        kept[0][...] = total[pl.ds(pl.multiple_of(mine * half, TILE), half)]
        away = (1 - mine) * half
        value = total[pl.ds(pl.multiple_of(away, TILE), half)] * factors[pl.ds(pl.multiple_of(place + away, TILE), half)]
        encode(value, sent_ref, exponent, digits_of(diagonal, exponent))
    elif kept:
        kept[0][...] = total[...]
        encode(total[...] * factors[here], sent_ref, exponent, digits_of(diagonal, exponent))
    else:
        encode(total[...] * factors[here], sent_ref)


def unpack_kernel(hidden, halvings, flips, where_ref, diagonal_ref, *refs):
    piece_refs, (high_ref, low_ref, packed) = refs[:len(flips)], refs[len(flips):]
    off, pairs, tail, length = layout(hidden, halvings)
    where = where_ref[0]
    rows = length >> halvings
    for flip, piece_ref in zip(flips, piece_refs):
        owner = lax.bitwise_xor(where, flip)
        start = sum(bit_of(owner, b) * (length >> (b + 1)) for b in range(halvings))
        packed[pl.ds(pl.multiple_of(start, TILE), rows)] = decode(piece_ref, rows)[0]

    def put(i, j, block):
        rows, cols = slice(i * BLOCK, (i + 1) * BLOCK), slice(j * BLOCK, (j + 1) * BLOCK)
        hi = block.astype(BF16)
        high_ref[rows, cols] = hi
        low_ref[rows, cols] = (block - hi.astype(F32)).astype(BF16)

    for n, (i, j) in enumerate(off):
        block = packed[n * BLOCK:(n + 1) * BLOCK]
        put(i, j, block)
        put(j, i, block.T)
    diagonal = diagonal_ref[...]
    ones = diagonal * jnp.exp2(-2.0 * exponent_of(diagonal))
    for n, (first, second) in enumerate(pairs):
        row = (len(off) + n) * BLOCK
        block = packed[row:row + BLOCK]
        turned = block.T
        for i, above in ((first, lax.lt), (second, lax.gt)):
            if i is not None:
                whole = jnp.where(eye_of(above), block, turned)
                put(i, i, jnp.where(eye_of(lax.eq), ones[i:i + 1], whole))


def sweeps_kernel(slot, diagonal_ref, weight_ref, mask_ref, high_ref, low_ref, *refs):
    out_ref, token_ref, result, done = refs[-4:]
    diagonal = jnp.concatenate([diagonal_ref[b:b + 1] for b in range(weight_ref.shape[-1] // BLOCK)], axis=1)
    back = jnp.exp2(exponent_of(diagonal))
    factor = relax_factor * (1.0 / (diagonal + diagonal_eps)) * back
    weight = weight_ref[slot].astype(F32)
    keep = mask_ref[slot].astype(F32)
    pruned = keep * weight
    for sweep in range(STEPS):
        change = (pruned - weight) * back
        top = change.astype(BF16)
        if sweep == 0:
            gradient = jnp.dot(top, high_ref[...], preferred_element_type=F32)
        else:
            rest = (change - top.astype(F32)).astype(BF16)
            both = jnp.dot(jnp.concatenate([top, rest], axis=0), high_ref[...], preferred_element_type=F32)
            gradient = both[:top.shape[0]] + both[top.shape[0]:]
        gradient = gradient + jnp.dot(top, low_ref[...], preferred_element_type=F32)
        pruned = keep * (pruned - gradient * factor)
    result[...] = pruned
    token_ref[...] = pruned[:8, :BLOCK]
    copy = pltpu.make_async_copy(result, out_ref.at[slot], done)
    copy.start()
    copy.wait()


def on_device(expert_inputs, row_expert, down_weight, keep_mask):
    tokens, hidden = expert_inputs.shape
    slots, features, _ = down_weight.shape
    peers = lax.axis_size("expert")
    copies = lax.axis_size("rows")
    all_experts = slots * peers
    capacity = tokens // 8
    halvings = copies.bit_length() - 2
    length = layout(hidden, halvings)[3]
    me = jnp.reshape(lax.axis_index("expert").astype(I32), (1,))
    where = jnp.reshape(lax.axis_index("rows").astype(I32), (1,))
    owners = row_expert.reshape(1, tokens)

    def shape(rows, columns=BLOCK, dtype=F32):
        return jax.ShapeDtypeStruct((rows, columns), dtype)

    def over_experts(array, flip):
        return lax.ppermute(array, "expert", [(i, i ^ flip) for i in range(peers)])

    def over_rows(array, bit):
        return lax.ppermute(array, "rows", [(i, i ^ (1 << bit)) for i in range(copies)])

    chunk = shape(capacity, hidden, BF16)
    place_flops = 2 * capacity * tokens * hidden
    key, *outgoing = call(
        functools.partial(first_kernel, peers, slots, all_experts, capacity),
        [shape(1, tokens, I32)] + [chunk] * (peers - 1), [SMEM, ANY, ANY],
        scratch=[
            pltpu.VMEM((1, tokens), I32), pltpu.VMEM((tokens, hidden), BF16),
            pltpu.SemaphoreType.DMA, pltpu.SemaphoreType.DMA((hidden // WIDTH,)),
        ],
        flops=place_flops * (peers - 1), moved=expert_inputs.size * 4, name="place_first",
    )(me, owners, expert_inputs)
    arrived = [[over_experts(outgoing[k - 1], k) for k in range(1, peers)]]
    count = slots + (slots - 1) * (peers - 1)
    rest = call(
        functools.partial(second_kernel, peers, slots, capacity), [chunk] * count, [SMEM, VMEM, VMEM],
        flops=place_flops * count, moved=expert_inputs.size * 4, name="place_rest",
    )(me, key, expert_inputs)
    own = rest[:slots]
    for a in range(1, slots):
        outgoing = rest[slots + (a - 1) * (peers - 1):slots + a * (peers - 1)]
        arrived.append([over_experts(outgoing[k - 1], k) for k in range(1, peers)])

    many = diagonal_rows(hidden)
    notes = -(-(8 + 3 * many) // TILE) * TILE

    def begin(a, after):
        chunks = [own[a]] + arrived[a][:1]
        return call(
            functools.partial(early_gram_kernel, halvings), shape(length + many), [VMEM] * len(chunks),
            flops=2 * capacity * len(chunks) * hidden * hidden, moved=length * BLOCK * 4, name=f"begin_{a}", after=after,
        )(*chunks)

    def stage(name, bit, keep, diagonal, got, cut, kept, after=()):
        rows = keep.shape[0]
        left = rows // 2 if cut else rows
        return call(
            functools.partial(stage_kernel, hidden, halvings, bit, got[0].dtype == F32, cut, len(got)),
            [shape(left + (notes if kept else TILE), dtype=I16), shape(many)] + ([shape(left)] if kept else []),
            [SMEM] + [VMEM] * (2 + len(got)),
            scratch=[pltpu.VMEM((length, BLOCK), F32), pltpu.VMEM((rows, BLOCK), F32)],
            moved=rows * BLOCK * 12, name=name, after=after,
        )(where, keep, diagonal, *got)

    def reduce(a, before, after, behind):
        size = length // 2
        sizes = cuts(size, PARTS if a == slots - 1 else 2)
        keep, diagonal, *sent = call(
            functools.partial(late_gram_kernel, halvings, peers - 2),
            [shape(size), shape(many)] + [shape(n + (many if i == 0 else 0)) for i, n in enumerate(sizes)],
            [SMEM] + [VMEM] * (peers - 1), scratch=[pltpu.VMEM((length + many, BLOCK), F32)],
            name=f"gram_{a}", after=after,
        )(where, before, *arrived[a][1:])
        for bit in range(1, halvings + 1):
            cut = bit < halvings
            got = [over_rows(part, bit - 1) for part in sent]
            coded, diagonal, keep = stage(f"stage_{a}_{bit}", bit, keep, diagonal, got, cut, True, behind if bit == 1 else ())
            sent = [coded]
            if bit == 1:
                halved = coded
        return halved, (coded, diagonal, keep)

    def end(a, sums, after):
        coded, diagonal, keep = sums
        return stage(f"total_{a}", halvings, keep, diagonal, [over_rows(coded, halvings)], False, False, after)

    def pieces_of(coded):
        held = [(0, coded)]
        for bit in range(halvings - 1, -1, -1):
            held += [(flip ^ (1 << bit), over_rows(piece, bit)) for flip, piece in held]
        return held

    def gather(a, held, diagonal, after):
        high, low = call(
            functools.partial(unpack_kernel, hidden, halvings, [flip for flip, _ in held]),
            [shape(hidden, hidden, BF16)] * 2, [SMEM] + [VMEM] * (1 + len(held)),
            scratch=[pltpu.VMEM((length, BLOCK), F32)], moved=length * BLOCK * 4, name=f"unpack_{a}", after=after,
        )(where, diagonal, *[piece for _, piece in held])
        return diagonal, high, low

    def sweeps(a, diagonal, high, low, result):
        args = [diagonal, down_weight, keep_mask, high, low] + ([] if result is None else [result])
        return call(
            functools.partial(sweeps_kernel, a),
            [jax.ShapeDtypeStruct((slots, features, hidden), F32), shape(8)],
            [VMEM] * 5 + [ANY] * (len(args) - 5),
            out_specs=[ANY, VMEM],
            scratch=[pltpu.VMEM((features, hidden), F32), pltpu.SemaphoreType.DMA],
            aliases={} if result is None else {5: 0},
            flops=2 * 3 * STEPS * features * hidden * hidden, moved=hidden * hidden * 4, name=f"sweeps_{a}",
        )(*args)

    result, held, halved = None, [], ()
    for a in range(slots):
        before = begin(a, halved)
        halved, sums = reduce(a, before, [piece for _, piece in held[:1]], [piece for _, piece in held[1:2]])
        halved, token = [halved], ()
        if a > 0:
            result, *token = sweeps(a - 1, *gather(a - 1, held, diagonal, [sums[0]]), result)
        coded, diagonal = end(a, sums, token)
        held = pieces_of(coded)
    return sweeps(slots - 1, *gather(slots - 1, held, diagonal, ()), result)[0]


def solution(mesh):
    return jax.shard_map(
        on_device,
        mesh=mesh,
        in_specs=(
            P(("expert", "rows"), None),
            P(("expert", "rows"), None),
            P("expert", "rows", None),
            P("expert", "rows", None),
        ),
        out_specs=P("expert", "rows", None),
        check_vma=False,
    )
```

```python
import functools

import jax
import jax.numpy as jnp
from jax import lax
from jax.experimental import pallas as pl
from jax.experimental.pallas import tpu as pltpu
from jax.sharding import PartitionSpec as P

STEPS = 4
BLOCK = 128
TILE = 16
PARTS = 4
WIDTH = 2 * BLOCK
LEVELS = 32760.0
OCTAVE = 8.0
relax_factor = 0.5
diagonal_eps = 1e-06
tiny = 1e-30
VMEM_LIMIT = 50 * 2**20

VMEM = pl.BlockSpec(memory_space=pltpu.VMEM)
ANY = pl.BlockSpec(memory_space=pl.ANY)
HBM = pl.BlockSpec(memory_space=pltpu.HBM)
SMEM = pl.BlockSpec(memory_space=pltpu.SMEM)
F32, BF16, I32, I16 = jnp.float32, jnp.bfloat16, jnp.int32, jnp.int16


def call(kernel, out_shape, in_specs, scratch=(), flops=0, moved=0, out_specs=None, aliases=None, name=None, after=()):
    many = isinstance(out_shape, (list, tuple))
    used, idle = len(in_specs), len(after)

    def body(*refs):
        kernel(*refs[:used], *refs[used + idle:])

    inner = pl.pallas_call(
        body,
        out_shape=out_shape,
        in_specs=list(in_specs) + [ANY] * idle,
        out_specs=out_specs if out_specs is not None else ([VMEM] * len(out_shape) if many else VMEM),
        scratch_shapes=list(scratch),
        input_output_aliases=aliases or {},
        cost_estimate=pl.CostEstimate(flops=flops, bytes_accessed=moved, transcendentals=0),
        compiler_params=pltpu.CompilerParams(vmem_limit_bytes=VMEM_LIMIT),
        name=name,
    )
    return lambda *args: inner(*args, *after)


def cuts(size, chunks):
    ends = [size * (c + 1) // (TILE * chunks) * TILE for c in range(chunks)]
    return [end - start for start, end in zip([0] + ends, ends)]


def slots_of(owners, experts, capacity):
    tokens = owners.shape[1]
    lanes = 128
    blocks = tokens // lanes
    named = owners == lax.broadcasted_iota(I32, (experts, tokens), 0)
    ones = named.astype(F32)
    stacked = jnp.concatenate([ones[:, b * lanes:(b + 1) * lanes] for b in range(blocks)], axis=0)
    upto = lax.broadcasted_iota(I32, (lanes, lanes), 0) <= lax.broadcasted_iota(I32, (lanes, lanes), 1)
    within = jnp.dot(stacked.astype(BF16), upto.astype(F32).astype(BF16), preferred_element_type=F32)
    carry = jnp.zeros((experts, 1), F32)
    parts = []
    for b in range(blocks):
        part = within[b * experts:(b + 1) * experts]
        parts.append(part + carry)
        carry = carry + part[:, lanes - 1:lanes]
    counted = jnp.concatenate(parts, axis=1)
    rank = jnp.sum(jnp.where(named, counted - 1.0, 0.0), axis=0, keepdims=True)
    return owners * capacity + rank.astype(I32)


def place(key, rows_ref, experts, capacity, out_refs):
    tokens, hidden = rows_ref.shape
    places = lax.broadcasted_iota(I32, (capacity, tokens), 0)
    chosen = jnp.concatenate(
        [(places == key - e * capacity).astype(F32).astype(BF16) for e in experts], axis=0
    )
    for c in range(0, hidden, WIDTH):
        got = jnp.dot(chosen, rows_ref[:, c:c + WIDTH], preferred_element_type=F32).astype(BF16)
        for k, out_ref in enumerate(out_refs):
            out_ref[:, c:c + WIDTH] = got[k * capacity:(k + 1) * capacity]


def others(peers):
    return range(peers - 1, 0, -1)


def first_kernel(peers, slots, all_experts, capacity, me_ref, owner_any, rows_any, key_ref, *refs):
    out_refs, (owner_ref, rows_ref, owner_done, rows_done) = refs[:-4], refs[-4:]
    owner_copy = pltpu.make_async_copy(owner_any, owner_ref, owner_done)
    owner_copy.start()
    rows_copy = pltpu.make_async_copy(rows_any, rows_ref, rows_done)
    rows_copy.start()
    me = me_ref[0]
    owner_copy.wait()
    key = slots_of(owner_ref[...], all_experts, capacity)
    key_ref[...] = key
    rows_copy.wait()
    place(key, rows_ref, [lax.bitwise_xor(me, k) * slots for k in others(peers)], capacity, out_refs)


def second_kernel(peers, slots, capacity, me_ref, key_ref, rows_ref, *out_refs):
    me = me_ref[0]
    where = [(0, a) for a in range(slots)] + [(k, a) for a in range(1, slots) for k in others(peers)]
    place(key_ref[...], rows_ref, [lax.bitwise_xor(me, k) * slots + a for k, a in where], capacity, out_refs)


def layout(hidden, halvings):
    blocks = hidden // BLOCK
    off = [(i, j) for i in range(blocks) for j in range(i + 1, blocks)]
    pairs = [(i, i + 1 if i + 1 < blocks else None) for i in range(0, blocks, 2)]
    tail = (len(off) + len(pairs)) * BLOCK
    unit = TILE << halvings
    return off, pairs, tail, -(-tail // unit) * unit


def eye_of(compare):
    return compare(lax.broadcasted_iota(I32, (BLOCK, BLOCK), 0), lax.broadcasted_iota(I32, (BLOCK, BLOCK), 1))


def bit_of(where, bit):
    return lax.bitwise_and(lax.shift_right_logical(where, bit), 1)


def diagonal_rows(hidden):
    return -(-(hidden // BLOCK) // 8) * 8


def exponent_of(diagonal):
    return jnp.ceil(0.5 * jnp.log2(jnp.maximum(diagonal, tiny)))


def spread(hidden, halvings, factor, out_ref):
    off, pairs, tail, length = layout(hidden, halvings)
    if length > tail:
        out_ref[tail:length] = jnp.zeros((length - tail, BLOCK), F32)
    across = [jnp.broadcast_to(factor[b:b + 1], (BLOCK, BLOCK)) for b in range(hidden // BLOCK)]
    down = [a.T for a in across]
    for n, (i, j) in enumerate(off):
        out_ref[n * BLOCK:(n + 1) * BLOCK] = down[i] * across[j]
    for n, (first, second) in enumerate(pairs):
        block = down[first] * across[first]
        if second is not None:
            block = jnp.where(eye_of(lax.lt), block, down[second] * across[second])
        row = (len(off) + n) * BLOCK
        out_ref[row:row + BLOCK] = block


def add_gram(halvings, chunk_refs, before, packed):
    hidden = chunk_refs[0].shape[1]
    off, pairs, tail, length = layout(hidden, halvings)
    at = {pair: n for n, pair in enumerate(off)}
    x = jnp.concatenate([r[...] for r in chunk_refs], axis=0) if len(chunk_refs) > 1 else chunk_refs[0][...]
    strip = 2 * BLOCK

    def put(n, value):
        rows = slice(n * BLOCK, (n + 1) * BLOCK)
        packed[rows] = value if before is None else before[rows] + value

    def put_diagonal(i, block):
        value = jnp.sum(jnp.where(eye_of(lax.eq), block, 0.0), axis=0, keepdims=True)
        row = slice(length + i, length + i + 1)
        packed[row] = value if before is None else before[row] + value

    packed[tail:] = jnp.zeros((packed.shape[0] - tail, BLOCK), F32)
    for n, (first, second) in enumerate(pairs):
        low, high = first * BLOCK, min(first * BLOCK + strip, hidden)
        product = lax.dot_general(
            x[:, low:high], x[:, low:], (((0,), (0,)), ((), ())), preferred_element_type=F32
        )
        for i in range((high - low) // BLOCK):
            for j in range((hidden - low) // BLOCK):
                pair = (first + i, first + j)
                if pair in at:
                    put(at[pair], product[i * BLOCK:(i + 1) * BLOCK, j * BLOCK:(j + 1) * BLOCK])
        mixed = product[:BLOCK, :BLOCK]
        put_diagonal(first, mixed)
        if second is not None:
            other = product[BLOCK:, BLOCK:2 * BLOCK]
            put_diagonal(second, other)
            mixed = jnp.where(eye_of(lax.lt), mixed, other)
        put(len(off) + n, jnp.where(eye_of(lax.eq), 0.0, mixed))


def early_gram_kernel(halvings, *refs):
    add_gram(halvings, refs[:-1], None, refs[-1])


def late_gram_kernel(halvings, pieces, where_ref, before_ref, *refs):
    chunk_refs, (keep_ref, diagonal_ref, *send_refs, packed) = refs[:pieces], refs[pieces:]
    add_gram(halvings, chunk_refs, before_ref, packed)
    half, rows = keep_ref.shape[0], diagonal_ref.shape[0]
    mine = bit_of(where_ref[0], 0)
    keep_ref[...] = packed[pl.ds(pl.multiple_of(mine * half, TILE), half)]
    diagonal = packed[2 * half:]
    diagonal_ref[...] = diagonal
    start = 0
    for n, send_ref in enumerate(send_refs):
        size = send_ref.shape[0] - (rows if n == 0 else 0)
        send_ref[:size] = packed[pl.ds(pl.multiple_of((1 - mine) * half + start, TILE), size)]
        if n == 0:
            send_ref[size:] = diagonal
        start += size


def encode(values, ref, exponent=None, digits=()):
    rows = values.shape[0]
    largest = jnp.max(jnp.abs(values), axis=0, keepdims=True)
    steps = jnp.ceil(OCTAVE * jnp.log2(jnp.maximum(largest, tiny)))
    factor = jnp.exp2(steps * (-1.0 / OCTAVE)) * LEVELS
    ref[:rows] = jnp.floor(values * factor + 0.5).astype(I32).astype(I16)
    notes = [jnp.broadcast_to(steps, (8, BLOCK))]
    if exponent is None:
        notes += notes
    else:
        notes += [exponent, *digits]
    notes = jnp.concatenate(notes, axis=0)
    if notes.shape[0] < ref.shape[0] - rows:
        notes = jnp.concatenate([notes, jnp.zeros((ref.shape[0] - rows - notes.shape[0], BLOCK), F32)], axis=0)
    ref[rows:] = notes.astype(I32).astype(I16)


def decode(ref, rows):
    notes = ref[rows:].astype(I32).astype(F32)
    return ref[:rows].astype(I32).astype(F32) * (jnp.exp2(notes[:1] * (1.0 / OCTAVE)) * (1.0 / LEVELS)), notes[8:]


def digits_of(diagonal, exponent):
    value = diagonal * jnp.exp2(-2.0 * exponent) * LEVELS
    first = jnp.floor(value + 0.5)
    return first, jnp.floor((value - first) * LEVELS + 0.5)


def from_digits(first, second, exponent):
    return (first + second * (1.0 / LEVELS)) * (1.0 / LEVELS) * jnp.exp2(2.0 * exponent)


def stage_kernel(hidden, halvings, bit, first, cut, parts, where_ref, keep_ref, diagonal_ref, *refs):
    got_refs, refs = refs[:parts], refs[parts:]
    sent_ref, diagonal_out, *kept, factors, total = refs
    rows, many = keep_ref.shape[0], diagonal_ref.shape[0]
    length = layout(hidden, halvings)[3]
    where = where_ref[0]
    place = sum(bit_of(where, b) * (length >> (b + 1)) for b in range(bit))
    here = pl.ds(pl.multiple_of(place, TILE), rows)
    diagonal = diagonal_ref[...]
    if first:
        start = 0
        for n, ref in enumerate(got_refs):
            size = ref.shape[0] - (many if n == 0 else 0)
            total[start:start + size] = keep_ref[start:start + size] + ref[:size]
            if n == 0:
                diagonal = diagonal + ref[size:]
            start += size
    else:
        value, notes = decode(got_refs[0], rows)
        theirs = notes[:many]
        spread(hidden, halvings, jnp.exp2(theirs), factors)
        total[...] = keep_ref[...] + value * factors[here]
        exponent = exponent_of(diagonal)
        ours = from_digits(*digits_of(diagonal, exponent), exponent)
        diagonal = ours + from_digits(notes[many:2 * many], notes[2 * many:3 * many], theirs)
    diagonal_out[...] = diagonal
    exponent = exponent_of(diagonal)
    spread(hidden, halvings, jnp.exp2(-exponent), factors)
    if cut:
        half = rows // 2
        mine = bit_of(where, bit)
        kept[0][...] = total[pl.ds(pl.multiple_of(mine * half, TILE), half)]
        away = (1 - mine) * half
        value = total[pl.ds(pl.multiple_of(away, TILE), half)] * factors[pl.ds(pl.multiple_of(place + away, TILE), half)]
        encode(value, sent_ref, exponent, digits_of(diagonal, exponent))
    elif kept:
        kept[0][...] = total[...]
        encode(total[...] * factors[here], sent_ref, exponent, digits_of(diagonal, exponent))
    else:
        encode(total[...] * factors[here], sent_ref)


def unpack_kernel(hidden, halvings, flips, where_ref, diagonal_ref, *refs):
    piece_refs, (high_ref, low_ref, packed) = refs[:len(flips)], refs[len(flips):]
    off, pairs, tail, length = layout(hidden, halvings)
    where = where_ref[0]
    rows = length >> halvings
    for flip, piece_ref in zip(flips, piece_refs):
        owner = lax.bitwise_xor(where, flip)
        start = sum(bit_of(owner, b) * (length >> (b + 1)) for b in range(halvings))
        packed[pl.ds(pl.multiple_of(start, TILE), rows)] = decode(piece_ref, rows)[0]

    def put(i, j, block):
        rows, cols = slice(i * BLOCK, (i + 1) * BLOCK), slice(j * BLOCK, (j + 1) * BLOCK)
        hi = block.astype(BF16)
        high_ref[rows, cols] = hi
        low_ref[rows, cols] = (block - hi.astype(F32)).astype(BF16)

    for n, (i, j) in enumerate(off):
        block = packed[n * BLOCK:(n + 1) * BLOCK]
        put(i, j, block)
        put(j, i, block.T)
    diagonal = diagonal_ref[...]
    ones = diagonal * jnp.exp2(-2.0 * exponent_of(diagonal))
    for n, (first, second) in enumerate(pairs):
        row = (len(off) + n) * BLOCK
        block = packed[row:row + BLOCK]
        turned = block.T
        for i, above in ((first, lax.lt), (second, lax.gt)):
            if i is not None:
                whole = jnp.where(eye_of(above), block, turned)
                put(i, i, jnp.where(eye_of(lax.eq), ones[i:i + 1], whole))


def sweeps_kernel(slot, diagonal_ref, weight_ref, mask_ref, high_ref, low_ref, *refs):
    out_ref, token_ref, result, changes, done = refs[-5:]
    features, hidden = result.shape
    columns = [slice(c, c + WIDTH) for c in range(0, hidden, WIDTH)]
    diagonal = jnp.concatenate([diagonal_ref[b:b + 1] for b in range(hidden // BLOCK)], axis=1)
    back = jnp.exp2(exponent_of(diagonal))
    factor = relax_factor * (1.0 / (diagonal + diagonal_eps)) * back
    copies = []

    def note(sweep, part, change):
        change = change * back[:, part]
        top = change.astype(BF16)
        changes[sweep % 2, :features, part] = top
        if sweep > 0:
            changes[sweep % 2, features:, part] = (change - top.astype(F32)).astype(BF16)

    for part in columns:
        weight = weight_ref[slot, :, part].astype(F32)
        pruned = mask_ref[slot, :, part].astype(F32) * weight
        result[:, part] = pruned
        note(0, part, pruned - weight)
    for sweep in range(STEPS):
        now = changes.at[sweep % 2]
        for n, part in enumerate(columns):
            if sweep == 0:
                gradient = jnp.dot(now[:features], high_ref[:, part], preferred_element_type=F32)
            else:
                both = jnp.dot(now[...], high_ref[:, part], preferred_element_type=F32)
                gradient = both[:features] + both[features:]
            gradient = gradient + jnp.dot(now[:features], low_ref[:, part], preferred_element_type=F32)
            pruned = mask_ref[slot, :, part].astype(F32) * (result[:, part] - gradient * factor[:, part])
            result[:, part] = pruned
            if sweep < STEPS - 1:
                note(sweep + 1, part, pruned - weight_ref[slot, :, part].astype(F32))
            else:
                copies.append(pltpu.make_async_copy(result.at[:, part], out_ref.at[slot, :, part], done.at[n]))
                copies[-1].start()
    token_ref[...] = result[:8, :BLOCK]
    for copy in copies:
        copy.wait()


def on_device(expert_inputs, row_expert, down_weight, keep_mask):
    tokens, hidden = expert_inputs.shape
    slots, features, _ = down_weight.shape
    peers = lax.axis_size("expert")
    copies = lax.axis_size("rows")
    all_experts = slots * peers
    capacity = tokens // 8
    halvings = copies.bit_length() - 2
    length = layout(hidden, halvings)[3]
    me = jnp.reshape(lax.axis_index("expert").astype(I32), (1,))
    where = jnp.reshape(lax.axis_index("rows").astype(I32), (1,))
    owners = row_expert.reshape(1, tokens)

    def shape(rows, columns=BLOCK, dtype=F32):
        return jax.ShapeDtypeStruct((rows, columns), dtype)

    def over_experts(array, flip):
        return lax.ppermute(array, "expert", [(i, i ^ flip) for i in range(peers)])

    def over_rows(array, bit):
        return lax.ppermute(array, "rows", [(i, i ^ (1 << bit)) for i in range(copies)])

    chunk = shape(capacity, hidden, BF16)
    place_flops = 2 * capacity * tokens * hidden
    key, *outgoing = call(
        functools.partial(first_kernel, peers, slots, all_experts, capacity),
        [shape(1, tokens, I32)] + [chunk] * (peers - 1), [SMEM, HBM, HBM],
        scratch=[
            pltpu.VMEM((1, tokens), I32), pltpu.VMEM((tokens, hidden), BF16),
            pltpu.SemaphoreType.DMA, pltpu.SemaphoreType.DMA,
        ],
        flops=place_flops * (peers - 1), moved=expert_inputs.size * 4, name="place_first",
    )(me, owners, expert_inputs)
    arrived = [[over_experts(rows, k) for rows, k in zip(outgoing, others(peers))]]
    count = slots + (slots - 1) * (peers - 1)
    rest = call(
        functools.partial(second_kernel, peers, slots, capacity), [chunk] * count, [SMEM, VMEM, VMEM],
        flops=place_flops * count, moved=expert_inputs.size * 4, name="place_rest",
    )(me, key, expert_inputs)
    own = rest[:slots]
    for a in range(1, slots):
        outgoing = rest[slots + (a - 1) * (peers - 1):slots + a * (peers - 1)]
        arrived.append([over_experts(rows, k) for rows, k in zip(outgoing, others(peers))])

    many = diagonal_rows(hidden)
    notes = -(-(8 + 3 * many) // TILE) * TILE

    def begin(a, after):
        chunks = [own[a]] + arrived[a][:1]
        return call(
            functools.partial(early_gram_kernel, halvings), shape(length + many), [VMEM] * len(chunks),
            flops=2 * capacity * len(chunks) * hidden * hidden, moved=length * BLOCK * 4, name=f"begin_{a}", after=after,
        )(*chunks)

    def stage(name, bit, keep, diagonal, got, cut, kept, after=()):
        rows = keep.shape[0]
        left = rows // 2 if cut else rows
        return call(
            functools.partial(stage_kernel, hidden, halvings, bit, got[0].dtype == F32, cut, len(got)),
            [shape(left + (notes if kept else TILE), dtype=I16), shape(many)] + ([shape(left)] if kept else []),
            [SMEM] + [VMEM] * (2 + len(got)),
            scratch=[pltpu.VMEM((length, BLOCK), F32), pltpu.VMEM((rows, BLOCK), F32)],
            moved=rows * BLOCK * 12, name=name, after=after,
        )(where, keep, diagonal, *got)

    def reduce(a, before, after, behind):
        size = length // 2
        sizes = cuts(size, PARTS if a == slots - 1 else 2)
        keep, diagonal, *sent = call(
            functools.partial(late_gram_kernel, halvings, peers - 2),
            [shape(size), shape(many)] + [shape(n + (many if i == 0 else 0)) for i, n in enumerate(sizes)],
            [SMEM] + [VMEM] * (peers - 1), scratch=[pltpu.VMEM((length + many, BLOCK), F32)],
            name=f"gram_{a}", after=after,
        )(where, before, *arrived[a][1:])
        for bit in range(1, halvings + 1):
            cut = bit < halvings
            got = [over_rows(part, bit - 1) for part in sent]
            coded, diagonal, keep = stage(f"stage_{a}_{bit}", bit, keep, diagonal, got, cut, True, behind if bit == 1 else ())
            sent = [coded]
            if bit == 1:
                halved = coded
        return halved, (coded, diagonal, keep)

    def end(a, sums, after):
        coded, diagonal, keep = sums
        return stage(f"total_{a}", halvings, keep, diagonal, [over_rows(coded, halvings)], False, False, after)

    def pieces_of(coded):
        held = [(0, coded)]
        for bit in range(halvings - 1, -1, -1):
            held += [(flip ^ (1 << bit), over_rows(piece, bit)) for flip, piece in held]
        return held

    def gather(a, held, diagonal, after):
        high, low = call(
            functools.partial(unpack_kernel, hidden, halvings, [flip for flip, _ in held]),
            [shape(hidden, hidden, BF16)] * 2, [SMEM] + [VMEM] * (1 + len(held)),
            scratch=[pltpu.VMEM((length, BLOCK), F32)], moved=length * BLOCK * 4, name=f"unpack_{a}", after=after,
        )(where, diagonal, *[piece for _, piece in held])
        return diagonal, high, low

    def sweeps(a, diagonal, high, low, result):
        args = [diagonal, down_weight, keep_mask, high, low] + ([] if result is None else [result])
        return call(
            functools.partial(sweeps_kernel, a),
            [jax.ShapeDtypeStruct((slots, features, hidden), F32), shape(8)],
            [VMEM] * 5 + [ANY] * (len(args) - 5),
            out_specs=[ANY, VMEM],
            scratch=[
                pltpu.VMEM((features, hidden), F32), pltpu.VMEM((2, 2 * features, hidden), BF16),
                pltpu.SemaphoreType.DMA((hidden // WIDTH,)),
            ],
            aliases={} if result is None else {5: 0},
            flops=2 * 3 * STEPS * features * hidden * hidden, moved=hidden * hidden * 4, name=f"sweeps_{a}",
        )(*args)

    result, held, halved = None, [], ()
    for a in range(slots):
        before = begin(a, halved)
        halved, sums = reduce(a, before, [piece for _, piece in held[:1]], [piece for _, piece in held[1:2]])
        halved, token = [halved], ()
        if a > 0:
            result, *token = sweeps(a - 1, *gather(a - 1, held, diagonal, [sums[0]]), result)
        coded, diagonal = end(a, sums, token)
        held = pieces_of(coded)
    return sweeps(slots - 1, *gather(slots - 1, held, diagonal, ()), result)[0]


def solution(mesh):
    return jax.shard_map(
        on_device,
        mesh=mesh,
        in_specs=(
            P(("expert", "rows"), None),
            P(("expert", "rows"), None),
            P("expert", "rows", None),
            P("expert", "rows", None),
        ),
        out_specs=P("expert", "rows", None),
        check_vma=False,
    )
```

```python
import functools

import jax
import jax.numpy as jnp
from jax import lax
from jax.experimental import pallas as pl
from jax.experimental.pallas import tpu as pltpu
from jax.sharding import PartitionSpec as P

STEPS = 4
BLOCK = 128
TILE = 16
PARTS = 4
WIDTH = 2 * BLOCK
LEVELS = 32760.0
OCTAVE = 8.0
relax_factor = 0.5
diagonal_eps = 1e-06
tiny = 1e-30
VMEM_LIMIT = 32 * 2**20

VMEM = pl.BlockSpec(memory_space=pltpu.VMEM)
ANY = pl.BlockSpec(memory_space=pl.ANY)
HBM = pl.BlockSpec(memory_space=pltpu.HBM)
SMEM = pl.BlockSpec(memory_space=pltpu.SMEM)
F32, BF16, I32, I16 = jnp.float32, jnp.bfloat16, jnp.int32, jnp.int16


def call(kernel, out_shape, in_specs, scratch=(), flops=0, moved=0, out_specs=None, aliases=None, name=None, after=()):
    many = isinstance(out_shape, (list, tuple))
    used, idle = len(in_specs), len(after)

    def body(*refs):
        kernel(*refs[:used], *refs[used + idle:])

    inner = pl.pallas_call(
        body,
        out_shape=out_shape,
        in_specs=list(in_specs) + [ANY] * idle,
        out_specs=out_specs if out_specs is not None else ([VMEM] * len(out_shape) if many else VMEM),
        scratch_shapes=list(scratch),
        input_output_aliases=aliases or {},
        cost_estimate=pl.CostEstimate(flops=flops, bytes_accessed=moved, transcendentals=0),
        compiler_params=pltpu.CompilerParams(vmem_limit_bytes=VMEM_LIMIT),
        name=name,
    )
    return lambda *args: inner(*args, *after)


def cuts(size, chunks):
    ends = [size * (c + 1) // (TILE * chunks) * TILE for c in range(chunks)]
    return [end - start for start, end in zip([0] + ends, ends)]


def slots_of(owners, experts, capacity):
    tokens = owners.shape[1]
    lanes = 128
    blocks = tokens // lanes
    named = owners == lax.broadcasted_iota(I32, (experts, tokens), 0)
    ones = named.astype(F32)
    stacked = jnp.concatenate([ones[:, b * lanes:(b + 1) * lanes] for b in range(blocks)], axis=0)
    upto = lax.broadcasted_iota(I32, (lanes, lanes), 0) <= lax.broadcasted_iota(I32, (lanes, lanes), 1)
    within = jnp.dot(stacked.astype(BF16), upto.astype(F32).astype(BF16), preferred_element_type=F32)
    carry = jnp.zeros((experts, 1), F32)
    parts = []
    for b in range(blocks):
        part = within[b * experts:(b + 1) * experts]
        parts.append(part + carry)
        carry = carry + part[:, lanes - 1:lanes]
    counted = jnp.concatenate(parts, axis=1)
    rank = jnp.sum(jnp.where(named, counted - 1.0, 0.0), axis=0, keepdims=True)
    return owners * capacity + rank.astype(I32)


def place(key, rows_ref, experts, capacity, out_refs):
    tokens, hidden = rows_ref.shape
    places = lax.broadcasted_iota(I32, (capacity, tokens), 0)
    chosen = jnp.concatenate(
        [(places == key - e * capacity).astype(F32).astype(BF16) for e in experts], axis=0
    )
    for c in range(0, hidden, WIDTH):
        got = jnp.dot(chosen, rows_ref[:, c:c + WIDTH], preferred_element_type=F32).astype(BF16)
        for k, out_ref in enumerate(out_refs):
            out_ref[:, c:c + WIDTH] = got[k * capacity:(k + 1) * capacity]


def others(peers):
    return range(peers - 1, 0, -1)


def first_kernel(peers, slots, all_experts, capacity, me_ref, owner_any, rows_any, key_ref, *refs):
    out_refs, (owner_ref, rows_ref, owner_done, rows_done) = refs[:-4], refs[-4:]
    owner_copy = pltpu.make_async_copy(owner_any, owner_ref, owner_done)
    owner_copy.start()
    rows_copy = pltpu.make_async_copy(rows_any, rows_ref, rows_done)
    rows_copy.start()
    me = me_ref[0]
    owner_copy.wait()
    key = slots_of(owner_ref[...], all_experts, capacity)
    key_ref[...] = key
    rows_copy.wait()
    place(key, rows_ref, [lax.bitwise_xor(me, k) * slots for k in others(peers)], capacity, out_refs)


def second_kernel(peers, slots, capacity, me_ref, key_ref, rows_ref, *out_refs):
    me = me_ref[0]
    where = [(0, a) for a in range(slots)] + [(k, a) for a in range(1, slots) for k in others(peers)]
    place(key_ref[...], rows_ref, [lax.bitwise_xor(me, k) * slots + a for k, a in where], capacity, out_refs)


def layout(hidden, halvings):
    blocks = hidden // BLOCK
    off = [(i, j) for i in range(blocks) for j in range(i + 1, blocks)]
    pairs = [(i, i + 1 if i + 1 < blocks else None) for i in range(0, blocks, 2)]
    tail = (len(off) + len(pairs)) * BLOCK
    unit = TILE << halvings
    return off, pairs, tail, -(-tail // unit) * unit


def eye_of(compare):
    return compare(lax.broadcasted_iota(I32, (BLOCK, BLOCK), 0), lax.broadcasted_iota(I32, (BLOCK, BLOCK), 1))


def bit_of(where, bit):
    return lax.bitwise_and(lax.shift_right_logical(where, bit), 1)


def diagonal_rows(hidden):
    return -(-(hidden // BLOCK) // 8) * 8


def exponent_of(diagonal):
    return jnp.ceil(0.5 * jnp.log2(jnp.maximum(diagonal, tiny)))


def spread(hidden, halvings, factor, out_ref):
    off, pairs, tail, length = layout(hidden, halvings)
    if length > tail:
        out_ref[tail:length] = jnp.zeros((length - tail, BLOCK), F32)
    across = [jnp.broadcast_to(factor[b:b + 1], (BLOCK, BLOCK)) for b in range(hidden // BLOCK)]
    down = [a.T for a in across]
    for n, (i, j) in enumerate(off):
        out_ref[n * BLOCK:(n + 1) * BLOCK] = down[i] * across[j]
    for n, (first, second) in enumerate(pairs):
        block = down[first] * across[first]
        if second is not None:
            block = jnp.where(eye_of(lax.lt), block, down[second] * across[second])
        row = (len(off) + n) * BLOCK
        out_ref[row:row + BLOCK] = block


def add_gram(halvings, chunk_refs, before, packed):
    hidden = chunk_refs[0].shape[1]
    off, pairs, tail, length = layout(hidden, halvings)
    at = {pair: n for n, pair in enumerate(off)}
    x = jnp.concatenate([r[...] for r in chunk_refs], axis=0) if len(chunk_refs) > 1 else chunk_refs[0][...]
    strip = 2 * BLOCK

    def put(n, value):
        rows = slice(n * BLOCK, (n + 1) * BLOCK)
        packed[rows] = value if before is None else before[rows] + value

    def put_diagonal(i, block):
        value = jnp.sum(jnp.where(eye_of(lax.eq), block, 0.0), axis=0, keepdims=True)
        row = slice(length + i, length + i + 1)
        packed[row] = value if before is None else before[row] + value

    packed[tail:] = jnp.zeros((packed.shape[0] - tail, BLOCK), F32)
    for n, (first, second) in enumerate(pairs):
        low, high = first * BLOCK, min(first * BLOCK + strip, hidden)
        product = lax.dot_general(
            x[:, low:high], x[:, low:], (((0,), (0,)), ((), ())), preferred_element_type=F32
        )
        for i in range((high - low) // BLOCK):
            for j in range((hidden - low) // BLOCK):
                pair = (first + i, first + j)
                if pair in at:
                    put(at[pair], product[i * BLOCK:(i + 1) * BLOCK, j * BLOCK:(j + 1) * BLOCK])
        mixed = product[:BLOCK, :BLOCK]
        put_diagonal(first, mixed)
        if second is not None:
            other = product[BLOCK:, BLOCK:2 * BLOCK]
            put_diagonal(second, other)
            mixed = jnp.where(eye_of(lax.lt), mixed, other)
        put(len(off) + n, jnp.where(eye_of(lax.eq), 0.0, mixed))


def early_gram_kernel(halvings, *refs):
    add_gram(halvings, refs[:-1], None, refs[-1])


def late_gram_kernel(halvings, pieces, where_ref, before_ref, *refs):
    chunk_refs, (keep_ref, diagonal_ref, *send_refs, packed) = refs[:pieces], refs[pieces:]
    add_gram(halvings, chunk_refs, before_ref, packed)
    half, rows = keep_ref.shape[0], diagonal_ref.shape[0]
    mine = bit_of(where_ref[0], 0)
    keep_ref[...] = packed[pl.ds(pl.multiple_of(mine * half, TILE), half)]
    diagonal = packed[2 * half:]
    diagonal_ref[...] = diagonal
    start = 0
    for n, send_ref in enumerate(send_refs):
        size = send_ref.shape[0] - (rows if n == 0 else 0)
        send_ref[:size] = packed[pl.ds(pl.multiple_of((1 - mine) * half + start, TILE), size)]
        if n == 0:
            send_ref[size:] = diagonal
        start += size


def encode(values, ref, exponent=None, digits=()):
    rows = values.shape[0]
    largest = jnp.max(jnp.abs(values), axis=0, keepdims=True)
    steps = jnp.ceil(OCTAVE * jnp.log2(jnp.maximum(largest, tiny)))
    factor = jnp.exp2(steps * (-1.0 / OCTAVE)) * LEVELS
    ref[:rows] = jnp.floor(values * factor + 0.5).astype(I32).astype(I16)
    notes = [jnp.broadcast_to(steps, (8, BLOCK))]
    if exponent is None:
        notes += notes
    else:
        notes += [exponent, *digits]
    notes = jnp.concatenate(notes, axis=0)
    if notes.shape[0] < ref.shape[0] - rows:
        notes = jnp.concatenate([notes, jnp.zeros((ref.shape[0] - rows - notes.shape[0], BLOCK), F32)], axis=0)
    ref[rows:] = notes.astype(I32).astype(I16)


def decode(ref, rows):
    notes = ref[rows:].astype(I32).astype(F32)
    return ref[:rows].astype(I32).astype(F32) * (jnp.exp2(notes[:1] * (1.0 / OCTAVE)) * (1.0 / LEVELS)), notes[8:]


def digits_of(diagonal, exponent):
    value = diagonal * jnp.exp2(-2.0 * exponent) * LEVELS
    first = jnp.floor(value + 0.5)
    return first, jnp.floor((value - first) * LEVELS + 0.5)


def from_digits(first, second, exponent):
    return (first + second * (1.0 / LEVELS)) * (1.0 / LEVELS) * jnp.exp2(2.0 * exponent)


def stage_kernel(hidden, halvings, bit, first, cut, parts, where_ref, keep_ref, diagonal_ref, *refs):
    got_refs, refs = refs[:parts], refs[parts:]
    sent_ref, diagonal_out, *kept, factors, total = refs
    rows, many = keep_ref.shape[0], diagonal_ref.shape[0]
    length = layout(hidden, halvings)[3]
    where = where_ref[0]
    place = sum(bit_of(where, b) * (length >> (b + 1)) for b in range(bit))
    here = pl.ds(pl.multiple_of(place, TILE), rows)
    diagonal = diagonal_ref[...]
    if first:
        start = 0
        for n, ref in enumerate(got_refs):
            size = ref.shape[0] - (many if n == 0 else 0)
            total[start:start + size] = keep_ref[start:start + size] + ref[:size]
            if n == 0:
                diagonal = diagonal + ref[size:]
            start += size
    else:
        value, notes = decode(got_refs[0], rows)
        theirs = notes[:many]
        spread(hidden, halvings, jnp.exp2(theirs), factors)
        total[...] = keep_ref[...] + value * factors[here]
        exponent = exponent_of(diagonal)
        ours = from_digits(*digits_of(diagonal, exponent), exponent)
        diagonal = ours + from_digits(notes[many:2 * many], notes[2 * many:3 * many], theirs)
    diagonal_out[...] = diagonal
    exponent = exponent_of(diagonal)
    spread(hidden, halvings, jnp.exp2(-exponent), factors)
    if cut:
        half = rows // 2
        mine = bit_of(where, bit)
        kept[0][...] = total[pl.ds(pl.multiple_of(mine * half, TILE), half)]
        away = (1 - mine) * half
        value = total[pl.ds(pl.multiple_of(away, TILE), half)] * factors[pl.ds(pl.multiple_of(place + away, TILE), half)]
        encode(value, sent_ref, exponent, digits_of(diagonal, exponent))
    elif kept:
        kept[0][...] = total[...]
        encode(total[...] * factors[here], sent_ref, exponent, digits_of(diagonal, exponent))
    else:
        encode(total[...] * factors[here], sent_ref)


def unpack_kernel(hidden, halvings, flips, where_ref, diagonal_ref, *refs):
    piece_refs, (high_ref, low_ref, packed) = refs[:len(flips)], refs[len(flips):]
    off, pairs, tail, length = layout(hidden, halvings)
    where = where_ref[0]
    rows = length >> halvings
    for flip, piece_ref in zip(flips, piece_refs):
        owner = lax.bitwise_xor(where, flip)
        start = sum(bit_of(owner, b) * (length >> (b + 1)) for b in range(halvings))
        packed[pl.ds(pl.multiple_of(start, TILE), rows)] = decode(piece_ref, rows)[0]

    def put(i, j, block):
        rows, cols = slice(i * BLOCK, (i + 1) * BLOCK), slice(j * BLOCK, (j + 1) * BLOCK)
        hi = block.astype(BF16)
        high_ref[rows, cols] = hi
        low_ref[rows, cols] = (block - hi.astype(F32)).astype(BF16)

    for n, (i, j) in enumerate(off):
        block = packed[n * BLOCK:(n + 1) * BLOCK]
        put(i, j, block)
        put(j, i, block.T)
    diagonal = diagonal_ref[...]
    ones = diagonal * jnp.exp2(-2.0 * exponent_of(diagonal))
    for n, (first, second) in enumerate(pairs):
        row = (len(off) + n) * BLOCK
        block = packed[row:row + BLOCK]
        turned = block.T
        for i, above in ((first, lax.lt), (second, lax.gt)):
            if i is not None:
                whole = jnp.where(eye_of(above), block, turned)
                put(i, i, jnp.where(eye_of(lax.eq), ones[i:i + 1], whole))


def relay_kernel(in_ref, out_ref):
    out_ref[...] = in_ref[...]


def sweeps_kernel(slot, diagonal_ref, weight_ref, mask_ref, high_ref, low_ref, *refs):
    out_ref, token_ref, result, changes, done = refs[-5:]
    features, hidden = result.shape
    columns = [slice(c, c + WIDTH) for c in range(0, hidden, WIDTH)]
    diagonal = jnp.concatenate([diagonal_ref[b:b + 1] for b in range(hidden // BLOCK)], axis=1)
    back = jnp.exp2(exponent_of(diagonal))
    factor = relax_factor * (1.0 / (diagonal + diagonal_eps)) * back
    copies = []

    def note(sweep, part, change):
        change = change * back[:, part]
        top = change.astype(BF16)
        changes[sweep % 2, :features, part] = top
        if sweep > 0:
            changes[sweep % 2, features:, part] = (change - top.astype(F32)).astype(BF16)

    for part in columns:
        weight = weight_ref[slot, :, part].astype(F32)
        pruned = mask_ref[slot, :, part].astype(F32) * weight
        result[:, part] = pruned
        note(0, part, pruned - weight)
    for sweep in range(STEPS):
        now = changes.at[sweep % 2]
        for n, part in enumerate(columns):
            if sweep == 0:
                gradient = jnp.dot(now[:features], high_ref[:, part], preferred_element_type=F32)
            else:
                both = jnp.dot(now[...], high_ref[:, part], preferred_element_type=F32)
                gradient = both[:features] + both[features:]
            gradient = gradient + jnp.dot(now[:features], low_ref[:, part], preferred_element_type=F32)
            pruned = mask_ref[slot, :, part].astype(F32) * (result[:, part] - gradient * factor[:, part])
            result[:, part] = pruned
            if sweep < STEPS - 1:
                note(sweep + 1, part, pruned - weight_ref[slot, :, part].astype(F32))
            else:
                copies.append(pltpu.make_async_copy(result.at[:, part], out_ref.at[slot, :, part], done.at[n]))
                copies[-1].start()
    token_ref[...] = result[:8, :BLOCK]
    for copy in copies:
        copy.wait()


def on_device(expert_inputs, row_expert, down_weight, keep_mask):
    tokens, hidden = expert_inputs.shape
    slots, features, _ = down_weight.shape
    peers = lax.axis_size("expert")
    copies = lax.axis_size("rows")
    all_experts = slots * peers
    capacity = tokens // 8
    halvings = copies.bit_length() - 2
    length = layout(hidden, halvings)[3]
    me = jnp.reshape(lax.axis_index("expert").astype(I32), (1,))
    where = jnp.reshape(lax.axis_index("rows").astype(I32), (1,))
    owners = row_expert.reshape(1, tokens)

    def shape(rows, columns=BLOCK, dtype=F32):
        return jax.ShapeDtypeStruct((rows, columns), dtype)

    def over_experts(array, flip):
        return lax.ppermute(array, "expert", [(i, i ^ flip) for i in range(peers)])

    def over_rows(array, bit):
        return lax.ppermute(array, "rows", [(i, i ^ (1 << bit)) for i in range(copies)])

    chunk = shape(capacity, hidden, BF16)
    place_flops = 2 * capacity * tokens * hidden
    key, *outgoing = call(
        functools.partial(first_kernel, peers, slots, all_experts, capacity),
        [shape(1, tokens, I32)] + [chunk] * (peers - 1), [SMEM, HBM, HBM],
        scratch=[
            pltpu.VMEM((1, tokens), I32), pltpu.VMEM((tokens, hidden), BF16),
            pltpu.SemaphoreType.DMA, pltpu.SemaphoreType.DMA,
        ],
        flops=place_flops * (peers - 1), moved=expert_inputs.size * 4, name="place_first",
    )(me, owners, expert_inputs)
    arrived = [[over_experts(rows, k) for rows, k in zip(outgoing, others(peers))]]
    count = slots + (slots - 1) * (peers - 1)
    rest = call(
        functools.partial(second_kernel, peers, slots, capacity), [chunk] * count, [SMEM, VMEM, VMEM],
        flops=place_flops * count, moved=expert_inputs.size * 4, name="place_rest",
    )(me, key, expert_inputs)
    own = rest[:slots]
    for a in range(1, slots):
        outgoing = rest[slots + (a - 1) * (peers - 1):slots + a * (peers - 1)]
        arrived.append([over_experts(rows, k) for rows, k in zip(outgoing, others(peers))])

    many = diagonal_rows(hidden)
    notes = -(-(8 + 3 * many) // TILE) * TILE

    def begin(a, after):
        chunks = [own[a]] + arrived[a][:1]
        return call(
            functools.partial(early_gram_kernel, halvings), shape(length + many), [VMEM] * len(chunks),
            flops=2 * capacity * len(chunks) * hidden * hidden, moved=length * BLOCK * 4, name=f"begin_{a}", after=after,
        )(*chunks)

    def stage(name, bit, keep, diagonal, got, cut, kept, after=()):
        rows = keep.shape[0]
        left = rows // 2 if cut else rows
        return call(
            functools.partial(stage_kernel, hidden, halvings, bit, got[0].dtype == F32, cut, len(got)),
            [shape(left + (notes if kept else TILE), dtype=I16), shape(many)] + ([shape(left)] if kept else []),
            [SMEM] + [VMEM] * (2 + len(got)),
            scratch=[pltpu.VMEM((length, BLOCK), F32), pltpu.VMEM((rows, BLOCK), F32)],
            name=name, after=after,
        )(where, keep, diagonal, *got)

    def reduce(a, before, after, behind):
        size = length // 2
        sizes = cuts(size, PARTS if a == slots - 1 else 2)
        keep, diagonal, *sent = call(
            functools.partial(late_gram_kernel, halvings, peers - 2),
            [shape(size), shape(many)] + [shape(n + (many if i == 0 else 0)) for i, n in enumerate(sizes)],
            [SMEM] + [VMEM] * (peers - 1), scratch=[pltpu.VMEM((length + many, BLOCK), F32)],
            name=f"gram_{a}", after=after,
        )(where, before, *arrived[a][1:])
        for bit in range(1, halvings + 1):
            cut = bit < halvings
            got = [over_rows(part, bit - 1) for part in sent]
            coded, diagonal, keep = stage(f"stage_{a}_{bit}", bit, keep, diagonal, got, cut, True, behind if bit == 1 else ())
            sent = [coded]
        return coded, diagonal, keep

    def end(a, sums, after):
        coded, diagonal, keep = sums
        return stage(f"total_{a}", halvings, keep, diagonal, [over_rows(coded, halvings)], False, False, after)

    def pieces_of(coded, after):
        held = [(0, coded)]
        for bit in range(halvings - 1, -1, -1):
            came = [(flip ^ (1 << bit), over_rows(piece, bit)) for flip, piece in held]
            if after and bit == halvings - 1 and bit > 0:
                came = [
                    (flip, call(relay_kernel, shape(piece.shape[0], dtype=I16), [VMEM], name="relay", after=after)(piece))
                    for flip, piece in came
                ]
            held += came
        return held

    def gather(a, held, diagonal, after):
        high, low = call(
            functools.partial(unpack_kernel, hidden, halvings, [flip for flip, _ in held]),
            [shape(hidden, hidden, BF16)] * 2, [SMEM] + [VMEM] * (1 + len(held)),
            scratch=[pltpu.VMEM((length, BLOCK), F32)], moved=length * BLOCK * 4, name=f"unpack_{a}", after=after,
        )(where, diagonal, *[piece for _, piece in held])
        return diagonal, high, low

    def sweeps(a, diagonal, high, low, result, after):
        args = [diagonal, down_weight, keep_mask, high, low] + ([] if result is None else [result])
        return call(
            functools.partial(sweeps_kernel, a),
            [jax.ShapeDtypeStruct((slots, features, hidden), F32), shape(8)],
            [VMEM] * 5 + [ANY] * (len(args) - 5),
            out_specs=[ANY, VMEM],
            scratch=[
                pltpu.VMEM((features, hidden), F32), pltpu.VMEM((2, 2 * features, hidden), BF16),
                pltpu.SemaphoreType.DMA((hidden // WIDTH,)),
            ],
            aliases={} if result is None else {5: 0},
            flops=2 * 3 * STEPS * features * hidden * hidden, moved=hidden * hidden * 4, name=f"sweeps_{a}",
            after=after,
        )(*args)

    early = [begin(a, ()) for a in range(slots)]
    result, whole, total, sums, token = None, None, (), (), []
    for a in range(slots):
        sums = reduce(a, early[a], sums[:1], [*early[a + 1:a + 2], *total[:1]])
        if a > 0:
            whole = gather(a - 1, pieces_of(total[0], token), total[1], ())
        total = end(a, sums, whole[1:2] if whole else ())
        if a > 0:
            result, *token = sweeps(a - 1, *whole, result, total[:1])
    return sweeps(slots - 1, *gather(slots - 1, pieces_of(total[0], token), total[1], ()), result, ())[0]


def solution(mesh):
    return jax.shard_map(
        on_device,
        mesh=mesh,
        in_specs=(
            P(("expert", "rows"), None),
            P(("expert", "rows"), None),
            P("expert", "rows", None),
            P("expert", "rows", None),
        ),
        out_specs=P("expert", "rows", None),
        check_vma=False,
    )
```

```python
import functools

import jax
import jax.numpy as jnp
from jax import lax
from jax.experimental import pallas as pl
from jax.experimental.pallas import tpu as pltpu
from jax.sharding import PartitionSpec as P

STEPS = 4
BLOCK = 128
TILE = 16
PARTS = 4
COPIES = 8
WIDTH = 2 * BLOCK
LEVELS = 32760.0
OCTAVE = 8.0
relax_factor = 0.5
diagonal_eps = 1e-06
tiny = 1e-30
VMEM_LIMIT = 24
PLACE_LIMITS = (50, 50)

VMEM = pl.BlockSpec(memory_space=pltpu.VMEM)
ANY = pl.BlockSpec(memory_space=pl.ANY)
HBM = pl.BlockSpec(memory_space=pltpu.HBM)
SMEM = pl.BlockSpec(memory_space=pltpu.SMEM)
F32, BF16, I32, I16 = jnp.float32, jnp.bfloat16, jnp.int32, jnp.int16


def call(kernel, out_shape, in_specs, scratch=(), flops=0, moved=0, out_specs=None, aliases=None, name=None, after=(), limit=VMEM_LIMIT):
    many = isinstance(out_shape, (list, tuple))
    used, idle = len(in_specs), len(after)

    def body(*refs):
        kernel(*refs[:used], *refs[used + idle:])

    inner = pl.pallas_call(
        body,
        out_shape=out_shape,
        in_specs=list(in_specs) + [ANY] * idle,
        out_specs=out_specs if out_specs is not None else ([VMEM] * len(out_shape) if many else VMEM),
        scratch_shapes=list(scratch),
        input_output_aliases=aliases or {},
        cost_estimate=pl.CostEstimate(flops=flops, bytes_accessed=moved, transcendentals=0),
        compiler_params=pltpu.CompilerParams(vmem_limit_bytes=limit * 2**20),
        name=name,
    )
    return lambda *args: inner(*args, *after)


def cuts(size, chunks):
    ends = [size * (c + 1) // (TILE * chunks) * TILE for c in range(chunks)]
    return [end - start for start, end in zip([0] + ends, ends)]


def slots_of(owners, experts, capacity):
    tokens = owners.shape[1]
    lanes = 128
    blocks = tokens // lanes
    named = owners == lax.broadcasted_iota(I32, (experts, tokens), 0)
    ones = named.astype(F32)
    stacked = jnp.concatenate([ones[:, b * lanes:(b + 1) * lanes] for b in range(blocks)], axis=0)
    upto = lax.broadcasted_iota(I32, (lanes, lanes), 0) <= lax.broadcasted_iota(I32, (lanes, lanes), 1)
    within = jnp.dot(stacked.astype(BF16), upto.astype(F32).astype(BF16), preferred_element_type=F32)
    carry = jnp.zeros((experts, 1), F32)
    parts = []
    for b in range(blocks):
        part = within[b * experts:(b + 1) * experts]
        parts.append(part + carry)
        carry = carry + part[:, lanes - 1:lanes]
    counted = jnp.concatenate(parts, axis=1)
    rank = jnp.sum(jnp.where(named, counted - 1.0, 0.0), axis=0, keepdims=True)
    return owners * capacity + rank.astype(I32)


def place(key, rows_ref, experts, capacity, out_refs):
    tokens, hidden = rows_ref.shape
    places = lax.broadcasted_iota(I32, (capacity, tokens), 0)
    chosen = jnp.concatenate(
        [(places == key - e * capacity).astype(F32).astype(BF16) for e in experts], axis=0
    )
    for c in range(0, hidden, WIDTH):
        got = jnp.dot(chosen, rows_ref[:, c:c + WIDTH], preferred_element_type=F32).astype(BF16)
        start = 0
        for out_ref in out_refs:
            out_ref[:, c:c + WIDTH] = got[start:start + out_ref.shape[0]]
            start += out_ref.shape[0]


def others(peers):
    return range(peers - 1, 0, -1)


def bring(rows_any, rows_ref, done):
    count = done.shape[0]
    part = rows_ref.shape[0] // count
    copies = []
    for n in range(count):
        rows = pl.ds(n * part, part)
        copies.append(pltpu.make_async_copy(rows_any.at[rows], rows_ref.at[rows], done.at[n]))
        copies[-1].start()
    return copies


def first_kernel(peers, slots, all_experts, capacity, me_ref, owner_any, rows_any, key_ref, *refs):
    out_refs, (owner_ref, rows_ref, owner_done, rows_done) = refs[:-4], refs[-4:]
    owner_copy = pltpu.make_async_copy(owner_any, owner_ref, owner_done)
    owner_copy.start()
    rows_copies = bring(rows_any, rows_ref, rows_done)
    me = me_ref[0]
    owner_copy.wait()
    key = slots_of(owner_ref[...], all_experts, capacity)
    key_ref[...] = key
    for copy in rows_copies:
        copy.wait()
    place(key, rows_ref, [lax.bitwise_xor(me, k) * slots for k in others(peers)], capacity, out_refs)


def second_kernel(peers, slots, capacity, me_ref, key_ref, rows_any, *refs):
    out_refs, (rows_ref, rows_done) = refs[:-2], refs[-2:]
    rows_copies = bring(rows_any, rows_ref, rows_done)
    me = me_ref[0]
    for copy in rows_copies:
        copy.wait()
    where = [(0, a) for a in range(slots)] + [(k, a) for a in range(1, slots) for k in others(peers)]
    place(key_ref[...], rows_ref, [lax.bitwise_xor(me, k) * slots + a for k, a in where], capacity, out_refs)


def layout(hidden, halvings):
    blocks = hidden // BLOCK
    off = [(i, j) for i in range(blocks) for j in range(i + 1, blocks)]
    pairs = [(i, i + 1 if i + 1 < blocks else None) for i in range(0, blocks, 2)]
    tail = (len(off) + len(pairs)) * BLOCK
    unit = TILE << halvings
    return off, pairs, tail, -(-tail // unit) * unit


def eye_of(compare):
    return compare(lax.broadcasted_iota(I32, (BLOCK, BLOCK), 0), lax.broadcasted_iota(I32, (BLOCK, BLOCK), 1))


def bit_of(where, bit):
    return lax.bitwise_and(lax.shift_right_logical(where, bit), 1)


def diagonal_rows(hidden):
    return -(-(hidden // BLOCK) // 8) * 8


def exponent_of(diagonal):
    return jnp.ceil(0.5 * jnp.log2(jnp.maximum(diagonal, tiny)))


def spread(hidden, halvings, factor, out_ref):
    off, pairs, tail, length = layout(hidden, halvings)
    if length > tail:
        out_ref[tail:length] = jnp.zeros((length - tail, BLOCK), F32)
    across = [jnp.broadcast_to(factor[b:b + 1], (BLOCK, BLOCK)) for b in range(hidden // BLOCK)]
    down = [a.T for a in across]
    for n, (i, j) in enumerate(off):
        out_ref[n * BLOCK:(n + 1) * BLOCK] = down[i] * across[j]
    for n, (first, second) in enumerate(pairs):
        block = down[first] * across[first]
        if second is not None:
            block = jnp.where(eye_of(lax.lt), block, down[second] * across[second])
        row = (len(off) + n) * BLOCK
        out_ref[row:row + BLOCK] = block


def add_gram(halvings, chunk_refs, before, packed):
    hidden = chunk_refs[0].shape[1]
    off, pairs, tail, length = layout(hidden, halvings)
    at = {pair: n for n, pair in enumerate(off)}
    x = jnp.concatenate([r[...] for r in chunk_refs], axis=0) if len(chunk_refs) > 1 else chunk_refs[0][...]
    strip = 2 * BLOCK

    def put(n, value):
        rows = slice(n * BLOCK, (n + 1) * BLOCK)
        packed[rows] = value if before is None else before[rows] + value

    def put_diagonal(i, block):
        value = jnp.sum(jnp.where(eye_of(lax.eq), block, 0.0), axis=0, keepdims=True)
        row = slice(length + i, length + i + 1)
        packed[row] = value if before is None else before[row] + value

    packed[tail:] = jnp.zeros((packed.shape[0] - tail, BLOCK), F32)
    for n, (first, second) in enumerate(pairs):
        low, high = first * BLOCK, min(first * BLOCK + strip, hidden)
        product = lax.dot_general(
            x[:, low:high], x[:, low:], (((0,), (0,)), ((), ())), preferred_element_type=F32
        )
        for i in range((high - low) // BLOCK):
            for j in range((hidden - low) // BLOCK):
                pair = (first + i, first + j)
                if pair in at:
                    put(at[pair], product[i * BLOCK:(i + 1) * BLOCK, j * BLOCK:(j + 1) * BLOCK])
        mixed = product[:BLOCK, :BLOCK]
        put_diagonal(first, mixed)
        if second is not None:
            other = product[BLOCK:, BLOCK:2 * BLOCK]
            put_diagonal(second, other)
            mixed = jnp.where(eye_of(lax.lt), mixed, other)
        put(len(off) + n, jnp.where(eye_of(lax.eq), 0.0, mixed))


def early_gram_kernel(halvings, *refs):
    add_gram(halvings, refs[:-1], None, refs[-1])


def late_gram_kernel(halvings, pieces, where_ref, before_ref, *refs):
    chunk_refs, (keep_ref, diagonal_ref, *send_refs, packed) = refs[:pieces], refs[pieces:]
    add_gram(halvings, chunk_refs, before_ref, packed)
    half, rows = keep_ref.shape[0], diagonal_ref.shape[0]
    mine = bit_of(where_ref[0], 0)
    keep_ref[...] = packed[pl.ds(pl.multiple_of(mine * half, TILE), half)]
    diagonal = packed[2 * half:]
    diagonal_ref[...] = diagonal
    start = 0
    for n, send_ref in enumerate(send_refs):
        size = send_ref.shape[0] - (rows if n == 0 else 0)
        send_ref[:size] = packed[pl.ds(pl.multiple_of((1 - mine) * half + start, TILE), size)]
        if n == 0:
            send_ref[size:] = diagonal
        start += size


def encode(values, ref, exponent=None, digits=()):
    rows = values.shape[0]
    largest = jnp.max(jnp.abs(values), axis=0, keepdims=True)
    steps = jnp.ceil(OCTAVE * jnp.log2(jnp.maximum(largest, tiny)))
    factor = jnp.exp2(steps * (-1.0 / OCTAVE)) * LEVELS
    ref[:rows] = jnp.floor(values * factor + 0.5).astype(I32).astype(I16)
    notes = [jnp.broadcast_to(steps, (8, BLOCK))]
    if exponent is None:
        notes += notes
    else:
        notes += [exponent, *digits]
    notes = jnp.concatenate(notes, axis=0)
    if notes.shape[0] < ref.shape[0] - rows:
        notes = jnp.concatenate([notes, jnp.zeros((ref.shape[0] - rows - notes.shape[0], BLOCK), F32)], axis=0)
    ref[rows:] = notes.astype(I32).astype(I16)


def decode(ref, rows):
    notes = ref[rows:].astype(I32).astype(F32)
    return ref[:rows].astype(I32).astype(F32) * (jnp.exp2(notes[:1] * (1.0 / OCTAVE)) * (1.0 / LEVELS)), notes[8:]


def digits_of(diagonal, exponent):
    value = diagonal * jnp.exp2(-2.0 * exponent) * LEVELS
    first = jnp.floor(value + 0.5)
    return first, jnp.floor((value - first) * LEVELS + 0.5)


def from_digits(first, second, exponent):
    return (first + second * (1.0 / LEVELS)) * (1.0 / LEVELS) * jnp.exp2(2.0 * exponent)


def stage_kernel(hidden, halvings, bit, first, cut, parts, where_ref, keep_ref, diagonal_ref, *refs):
    got_refs, refs = refs[:parts], refs[parts:]
    sent_ref, diagonal_out, *kept, factors, total = refs
    rows, many = keep_ref.shape[0], diagonal_ref.shape[0]
    length = layout(hidden, halvings)[3]
    where = where_ref[0]
    place = sum(bit_of(where, b) * (length >> (b + 1)) for b in range(bit))
    here = pl.ds(pl.multiple_of(place, TILE), rows)
    diagonal = diagonal_ref[...]
    if first:
        start = 0
        for n, ref in enumerate(got_refs):
            size = ref.shape[0] - (many if n == 0 else 0)
            total[start:start + size] = keep_ref[start:start + size] + ref[:size]
            if n == 0:
                diagonal = diagonal + ref[size:]
            start += size
    else:
        value, notes = decode(got_refs[0], rows)
        theirs = notes[:many]
        spread(hidden, halvings, jnp.exp2(theirs), factors)
        total[...] = keep_ref[...] + value * factors[here]
        exponent = exponent_of(diagonal)
        ours = from_digits(*digits_of(diagonal, exponent), exponent)
        diagonal = ours + from_digits(notes[many:2 * many], notes[2 * many:3 * many], theirs)
    diagonal_out[...] = diagonal
    exponent = exponent_of(diagonal)
    spread(hidden, halvings, jnp.exp2(-exponent), factors)
    if cut:
        half = rows // 2
        mine = bit_of(where, bit)
        kept[0][...] = total[pl.ds(pl.multiple_of(mine * half, TILE), half)]
        away = (1 - mine) * half
        value = total[pl.ds(pl.multiple_of(away, TILE), half)] * factors[pl.ds(pl.multiple_of(place + away, TILE), half)]
        encode(value, sent_ref, exponent, digits_of(diagonal, exponent))
    elif kept:
        kept[0][...] = total[...]
        encode(total[...] * factors[here], sent_ref, exponent, digits_of(diagonal, exponent))
    else:
        encode(total[...] * factors[here], sent_ref)


def unpack_kernel(hidden, halvings, flips, where_ref, diagonal_ref, *refs):
    piece_refs, (high_ref, low_ref, packed) = refs[:len(flips)], refs[len(flips):]
    off, pairs, tail, length = layout(hidden, halvings)
    where = where_ref[0]
    rows = length >> halvings
    for flip, piece_ref in zip(flips, piece_refs):
        owner = lax.bitwise_xor(where, flip)
        start = sum(bit_of(owner, b) * (length >> (b + 1)) for b in range(halvings))
        packed[pl.ds(pl.multiple_of(start, TILE), rows)] = decode(piece_ref, rows)[0]

    def put(i, j, block):
        rows, cols = slice(i * BLOCK, (i + 1) * BLOCK), slice(j * BLOCK, (j + 1) * BLOCK)
        hi = block.astype(BF16)
        high_ref[rows, cols] = hi
        low_ref[rows, cols] = (block - hi.astype(F32)).astype(BF16)

    for n, (i, j) in enumerate(off):
        block = packed[n * BLOCK:(n + 1) * BLOCK]
        put(i, j, block)
        put(j, i, block.T)
    diagonal = diagonal_ref[...]
    ones = diagonal * jnp.exp2(-2.0 * exponent_of(diagonal))
    for n, (first, second) in enumerate(pairs):
        row = (len(off) + n) * BLOCK
        block = packed[row:row + BLOCK]
        turned = block.T
        for i, above in ((first, lax.lt), (second, lax.gt)):
            if i is not None:
                whole = jnp.where(eye_of(above), block, turned)
                put(i, i, jnp.where(eye_of(lax.eq), ones[i:i + 1], whole))


def relay_kernel(in_ref, out_ref):
    out_ref[...] = in_ref[...]


def sweeps_kernel(slot, diagonal_ref, weight_ref, mask_ref, high_ref, low_ref, *refs):
    out_ref, token_ref, result, changes, done = refs[-5:]
    features, hidden = result.shape
    columns = [slice(c, c + WIDTH) for c in range(0, hidden, WIDTH)]
    diagonal = jnp.concatenate([diagonal_ref[b:b + 1] for b in range(hidden // BLOCK)], axis=1)
    back = jnp.exp2(exponent_of(diagonal))
    factor = relax_factor * (1.0 / (diagonal + diagonal_eps)) * back
    copies = []

    def note(sweep, part, change):
        change = change * back[:, part]
        top = change.astype(BF16)
        changes[sweep % 2, :features, part] = top
        if sweep > 0:
            changes[sweep % 2, features:, part] = (change - top.astype(F32)).astype(BF16)

    for part in columns:
        weight = weight_ref[slot, :, part].astype(F32)
        pruned = mask_ref[slot, :, part].astype(F32) * weight
        result[:, part] = pruned
        note(0, part, pruned - weight)
    for sweep in range(STEPS):
        now = changes.at[sweep % 2]
        for n, part in enumerate(columns):
            if sweep == 0:
                gradient = jnp.dot(now[:features], high_ref[:, part], preferred_element_type=F32)
            else:
                both = jnp.dot(now[...], high_ref[:, part], preferred_element_type=F32)
                gradient = both[:features] + both[features:]
            gradient = gradient + jnp.dot(now[:features], low_ref[:, part], preferred_element_type=F32)
            pruned = mask_ref[slot, :, part].astype(F32) * (result[:, part] - gradient * factor[:, part])
            result[:, part] = pruned
            if sweep < STEPS - 1:
                note(sweep + 1, part, pruned - weight_ref[slot, :, part].astype(F32))
            else:
                copies.append(pltpu.make_async_copy(result.at[:, part], out_ref.at[slot, :, part], done.at[n]))
                copies[-1].start()
    token_ref[...] = result[:8, :BLOCK]
    for copy in copies:
        copy.wait()


def on_device(expert_inputs, row_expert, down_weight, keep_mask):
    tokens, hidden = expert_inputs.shape
    slots, features, _ = down_weight.shape
    peers = lax.axis_size("expert")
    copies = lax.axis_size("rows")
    all_experts = slots * peers
    capacity = tokens // 8
    halvings = copies.bit_length() - 2
    length = layout(hidden, halvings)[3]
    me = jnp.reshape(lax.axis_index("expert").astype(I32), (1,))
    where = jnp.reshape(lax.axis_index("rows").astype(I32), (1,))
    owners = row_expert.reshape(1, tokens)

    def shape(rows, columns=BLOCK, dtype=F32):
        return jax.ShapeDtypeStruct((rows, columns), dtype)

    def over_experts(array, flip):
        return lax.ppermute(array, "expert", [(i, i ^ flip) for i in range(peers)])

    def over_rows(array, bit):
        return lax.ppermute(array, "rows", [(i, i ^ (1 << bit)) for i in range(copies)])

    chunk = shape(capacity, hidden, BF16)
    place_flops = 2 * capacity * tokens * hidden
    key, *outgoing = call(
        functools.partial(first_kernel, peers, slots, all_experts, capacity),
        [shape(1, tokens, I32)] + [chunk] * (peers - 1), [SMEM, HBM, HBM],
        scratch=[
            pltpu.VMEM((1, tokens), I32), pltpu.VMEM((tokens, hidden), BF16),
            pltpu.SemaphoreType.DMA, pltpu.SemaphoreType.DMA((COPIES,)),
        ],
        flops=place_flops * (peers - 1), moved=expert_inputs.size * 4, name="place_first", limit=PLACE_LIMITS[0],
    )(me, owners, expert_inputs)
    arrived = [[over_experts(rows, k) for rows, k in zip(outgoing, others(peers))]]
    count = slots + (slots - 1) * (peers - 1)
    parts = [shape(n, hidden, BF16) for n in cuts(capacity, 2)]
    flips = [peers - 1, *others(peers)]
    rest = call(
        functools.partial(second_kernel, peers, slots, capacity),
        [chunk] * slots + (parts + [chunk] * (peers - 2)) * (slots - 1), [SMEM, VMEM, HBM],
        scratch=[pltpu.VMEM((tokens, hidden), BF16), pltpu.SemaphoreType.DMA((COPIES,))],
        flops=place_flops * count, moved=expert_inputs.size * 4, name="place_rest", limit=PLACE_LIMITS[1],
    )(me, key, expert_inputs)
    own = rest[:slots]
    for a in range(1, slots):
        outgoing = rest[slots + (a - 1) * peers:slots + a * peers]
        arrived.append([over_experts(rows, k) for rows, k in zip(outgoing, flips)])

    many = diagonal_rows(hidden)
    notes = -(-(8 + 3 * many) // TILE) * TILE

    def begin(a, after):
        chunks = [own[a]] + arrived[a][:1]
        return call(
            functools.partial(early_gram_kernel, halvings), shape(length + many), [VMEM] * len(chunks),
            flops=2 * capacity * len(chunks) * hidden * hidden, moved=length * BLOCK * 4, name=f"begin_{a}", after=after,
        )(*chunks)

    def stage(name, bit, keep, diagonal, got, cut, kept, after=()):
        rows = keep.shape[0]
        left = rows // 2 if cut else rows
        return call(
            functools.partial(stage_kernel, hidden, halvings, bit, got[0].dtype == F32, cut, len(got)),
            [shape(left + (notes if kept else TILE), dtype=I16), shape(many)] + ([shape(left)] if kept else []),
            [SMEM] + [VMEM] * (2 + len(got)),
            scratch=[pltpu.VMEM((length, BLOCK), F32), pltpu.VMEM((rows, BLOCK), F32)],
            name=name, after=after,
        )(where, keep, diagonal, *got)

    def reduce(a, before, after, behind):
        size = length // 2
        sizes = cuts(size, PARTS if a == slots - 1 else 3)
        keep, diagonal, *sent = call(
            functools.partial(late_gram_kernel, halvings, len(arrived[a]) - 1),
            [shape(size), shape(many)] + [shape(n + (many if i == 0 else 0)) for i, n in enumerate(sizes)],
            [SMEM] + [VMEM] * len(arrived[a]), scratch=[pltpu.VMEM((length + many, BLOCK), F32)],
            name=f"gram_{a}", after=after,
        )(where, before, *arrived[a][1:])
        for bit in range(1, halvings + 1):
            cut = bit < halvings
            got = [over_rows(part, bit - 1) for part in sent]
            coded, diagonal, keep = stage(f"stage_{a}_{bit}", bit, keep, diagonal, got, cut, True, behind if bit == 1 else ())
            sent = [coded]
        return coded, diagonal, keep

    def end(a, sums, after):
        coded, diagonal, keep = sums
        return stage(f"total_{a}", halvings, keep, diagonal, [over_rows(coded, halvings)], False, False, after)

    def pieces_of(coded, after):
        held = [(0, coded)]
        for bit in range(halvings - 1, -1, -1):
            came = [(flip ^ (1 << bit), over_rows(piece, bit)) for flip, piece in held]
            if after and bit == halvings - 1 and bit > 0:
                came = [
                    (flip, call(relay_kernel, shape(piece.shape[0], dtype=I16), [VMEM], name="relay", after=after)(piece))
                    for flip, piece in came
                ]
            held += came
        return held

    def gather(a, held, diagonal, after):
        high, low = call(
            functools.partial(unpack_kernel, hidden, halvings, [flip for flip, _ in held]),
            [shape(hidden, hidden, BF16)] * 2, [SMEM] + [VMEM] * (1 + len(held)),
            scratch=[pltpu.VMEM((length, BLOCK), F32)], moved=length * BLOCK * 4, name=f"unpack_{a}", after=after,
        )(where, diagonal, *[piece for _, piece in held])
        return diagonal, high, low

    def sweeps(a, diagonal, high, low, result, after):
        args = [diagonal, down_weight, keep_mask, high, low] + ([] if result is None else [result])
        return call(
            functools.partial(sweeps_kernel, a),
            [jax.ShapeDtypeStruct((slots, features, hidden), F32), shape(8)],
            [VMEM] * 5 + [ANY] * (len(args) - 5),
            out_specs=[ANY, VMEM],
            scratch=[
                pltpu.VMEM((features, hidden), F32), pltpu.VMEM((2, 2 * features, hidden), BF16),
                pltpu.SemaphoreType.DMA((hidden // WIDTH,)),
            ],
            aliases={} if result is None else {5: 0},
            flops=2 * 3 * STEPS * features * hidden * hidden, moved=hidden * hidden * 4, name=f"sweeps_{a}",
            after=after,
        )(*args)

    early = [begin(a, ()) for a in range(slots)]
    result, whole, total, sums, token = None, None, (), (), []
    for a in range(slots):
        sums = reduce(a, early[a], sums[:1], [*early[a + 1:a + 2], *total[:1]])
        if a > 0:
            whole = gather(a - 1, pieces_of(total[0], token), total[1], ())
        total = end(a, sums, whole[1:2] if whole else ())
        if a > 0:
            result, *token = sweeps(a - 1, *whole, result, total[:1])
    return sweeps(slots - 1, *gather(slots - 1, pieces_of(total[0], token), total[1], ()), result, ())[0]


def solution(mesh):
    return jax.shard_map(
        on_device,
        mesh=mesh,
        in_specs=(
            P(("expert", "rows"), None),
            P(("expert", "rows"), None),
            P("expert", "rows", None),
            P("expert", "rows", None),
        ),
        out_specs=P("expert", "rows", None),
        check_vma=False,
    )
```

```python
import functools

import jax
import jax.numpy as jnp
from jax import lax
from jax.experimental import pallas as pl
from jax.experimental.pallas import tpu as pltpu
from jax.sharding import PartitionSpec as P

STEPS = 4
BLOCK = 128
TILE = 16
PARTS = 4
COPIES = 8
WIDTH = 2 * BLOCK
LEVELS = 32760.0
OCTAVE = 8.0
relax_factor = 0.5
diagonal_eps = 1e-06
tiny = 1e-30
VMEM_LIMIT = 32

VMEM = pl.BlockSpec(memory_space=pltpu.VMEM)
ANY = pl.BlockSpec(memory_space=pl.ANY)
HBM = pl.BlockSpec(memory_space=pltpu.HBM)
SMEM = pl.BlockSpec(memory_space=pltpu.SMEM)
F32, BF16, I32, I16 = jnp.float32, jnp.bfloat16, jnp.int32, jnp.int16


def call(kernel, out_shape, in_specs, scratch=(), flops=0, moved=0, out_specs=None, aliases=None, name=None, after=(), limit=VMEM_LIMIT):
    many = isinstance(out_shape, (list, tuple))
    used, idle = len(in_specs), len(after)

    def body(*refs):
        kernel(*refs[:used], *refs[used + idle:])

    inner = pl.pallas_call(
        body,
        out_shape=out_shape,
        in_specs=list(in_specs) + [ANY] * idle,
        out_specs=out_specs if out_specs is not None else ([VMEM] * len(out_shape) if many else VMEM),
        scratch_shapes=list(scratch),
        input_output_aliases=aliases or {},
        cost_estimate=pl.CostEstimate(flops=flops, bytes_accessed=moved, transcendentals=0),
        compiler_params=pltpu.CompilerParams(vmem_limit_bytes=limit * 2**20),
        name=name,
    )
    return lambda *args: inner(*args, *after)


def cuts(size, chunks):
    ends = [size * (c + 1) // (TILE * chunks) * TILE for c in range(chunks)]
    return [end - start for start, end in zip([0] + ends, ends)]


def slots_of(owners, experts, capacity):
    tokens = owners.shape[1]
    lanes = 128
    blocks = tokens // lanes
    named = owners == lax.broadcasted_iota(I32, (experts, tokens), 0)
    ones = named.astype(F32)
    stacked = jnp.concatenate([ones[:, b * lanes:(b + 1) * lanes] for b in range(blocks)], axis=0)
    upto = lax.broadcasted_iota(I32, (lanes, lanes), 0) <= lax.broadcasted_iota(I32, (lanes, lanes), 1)
    within = jnp.dot(stacked.astype(BF16), upto.astype(F32).astype(BF16), preferred_element_type=F32)
    carry = jnp.zeros((experts, 1), F32)
    parts = []
    for b in range(blocks):
        part = within[b * experts:(b + 1) * experts]
        parts.append(part + carry)
        carry = carry + part[:, lanes - 1:lanes]
    counted = jnp.concatenate(parts, axis=1)
    rank = jnp.sum(jnp.where(named, counted - 1.0, 0.0), axis=0, keepdims=True)
    return owners * capacity + rank.astype(I32)


def place(key, rows_ref, experts, capacity, out_refs):
    tokens, hidden = rows_ref.shape
    places = lax.broadcasted_iota(I32, (capacity, tokens), 0)
    chosen = jnp.concatenate(
        [(places == key - e * capacity).astype(F32).astype(BF16) for e in experts], axis=0
    )
    for c in range(0, hidden, WIDTH):
        got = jnp.dot(chosen, rows_ref[:, c:c + WIDTH], preferred_element_type=F32).astype(BF16)
        start = 0
        for out_ref in out_refs:
            out_ref[:, c:c + WIDTH] = got[start:start + out_ref.shape[0]]
            start += out_ref.shape[0]


def others(peers):
    return range(peers - 1, 0, -1)


def bring(rows_any, rows_ref, done):
    count = done.shape[0]
    part = rows_ref.shape[0] // count
    copies = []
    for n in range(count):
        rows = pl.ds(n * part, part)
        copies.append(pltpu.make_async_copy(rows_any.at[rows], rows_ref.at[rows], done.at[n]))
        copies[-1].start()
    return copies


def first_kernel(peers, slots, all_experts, capacity, me_ref, owner_any, rows_any, key_ref, *refs):
    out_refs, (owner_ref, rows_ref, owner_done, rows_done) = refs[:-4], refs[-4:]
    owner_copy = pltpu.make_async_copy(owner_any, owner_ref, owner_done)
    owner_copy.start()
    rows_copies = bring(rows_any, rows_ref, rows_done)
    me = me_ref[0]
    owner_copy.wait()
    key = slots_of(owner_ref[...], all_experts, capacity)
    key_ref[...] = key
    for copy in rows_copies:
        copy.wait()
    place(key, rows_ref, [lax.bitwise_xor(me, k) * slots for k in others(peers)], capacity, out_refs)


def second_kernel(peers, slots, capacity, me_ref, key_ref, rows_ref, *out_refs):
    me = me_ref[0]
    where = [(0, a) for a in range(slots)] + [(k, a) for a in range(1, slots) for k in others(peers)]
    place(key_ref[...], rows_ref, [lax.bitwise_xor(me, k) * slots + a for k, a in where], capacity, out_refs)


def layout(hidden, halvings):
    blocks = hidden // BLOCK
    off = [(i, j) for i in range(blocks) for j in range(i + 1, blocks)]
    pairs = [(i, i + 1 if i + 1 < blocks else None) for i in range(0, blocks, 2)]
    tail = (len(off) + len(pairs)) * BLOCK
    unit = TILE << halvings
    return off, pairs, tail, -(-tail // unit) * unit


def eye_of(compare):
    return compare(lax.broadcasted_iota(I32, (BLOCK, BLOCK), 0), lax.broadcasted_iota(I32, (BLOCK, BLOCK), 1))


def bit_of(where, bit):
    return lax.bitwise_and(lax.shift_right_logical(where, bit), 1)


def diagonal_rows(hidden):
    return -(-(hidden // BLOCK) // 8) * 8


def exponent_of(diagonal):
    return jnp.ceil(0.5 * jnp.log2(jnp.maximum(diagonal, tiny)))


def spread(hidden, halvings, factor, out_ref):
    off, pairs, tail, length = layout(hidden, halvings)
    if length > tail:
        out_ref[tail:length] = jnp.zeros((length - tail, BLOCK), F32)
    across = [jnp.broadcast_to(factor[b:b + 1], (BLOCK, BLOCK)) for b in range(hidden // BLOCK)]
    down = [a.T for a in across]
    for n, (i, j) in enumerate(off):
        out_ref[n * BLOCK:(n + 1) * BLOCK] = down[i] * across[j]
    for n, (first, second) in enumerate(pairs):
        block = down[first] * across[first]
        if second is not None:
            block = jnp.where(eye_of(lax.lt), block, down[second] * across[second])
        row = (len(off) + n) * BLOCK
        out_ref[row:row + BLOCK] = block


def add_gram(halvings, chunk_refs, before, packed):
    hidden = chunk_refs[0].shape[1]
    off, pairs, tail, length = layout(hidden, halvings)
    at = {pair: n for n, pair in enumerate(off)}
    x = jnp.concatenate([r[...] for r in chunk_refs], axis=0) if len(chunk_refs) > 1 else chunk_refs[0][...]
    strip = 2 * BLOCK

    def put(n, value):
        rows = slice(n * BLOCK, (n + 1) * BLOCK)
        packed[rows] = value if before is None else before[rows] + value

    def put_diagonal(i, block):
        value = jnp.sum(jnp.where(eye_of(lax.eq), block, 0.0), axis=0, keepdims=True)
        row = slice(length + i, length + i + 1)
        packed[row] = value if before is None else before[row] + value

    packed[tail:] = jnp.zeros((packed.shape[0] - tail, BLOCK), F32)
    for n, (first, second) in enumerate(pairs):
        low, high = first * BLOCK, min(first * BLOCK + strip, hidden)
        product = lax.dot_general(
            x[:, low:high], x[:, low:], (((0,), (0,)), ((), ())), preferred_element_type=F32
        )
        for i in range((high - low) // BLOCK):
            for j in range((hidden - low) // BLOCK):
                pair = (first + i, first + j)
                if pair in at:
                    put(at[pair], product[i * BLOCK:(i + 1) * BLOCK, j * BLOCK:(j + 1) * BLOCK])
        mixed = product[:BLOCK, :BLOCK]
        put_diagonal(first, mixed)
        if second is not None:
            other = product[BLOCK:, BLOCK:2 * BLOCK]
            put_diagonal(second, other)
            mixed = jnp.where(eye_of(lax.lt), mixed, other)
        put(len(off) + n, jnp.where(eye_of(lax.eq), 0.0, mixed))


def early_gram_kernel(halvings, *refs):
    add_gram(halvings, refs[:-1], None, refs[-1])


def late_gram_kernel(halvings, pieces, where_ref, before_ref, *refs):
    chunk_refs, (keep_ref, diagonal_ref, *send_refs, packed) = refs[:pieces], refs[pieces:]
    add_gram(halvings, chunk_refs, before_ref, packed)
    half, rows = keep_ref.shape[0], diagonal_ref.shape[0]
    mine = bit_of(where_ref[0], 0)
    keep_ref[...] = packed[pl.ds(pl.multiple_of(mine * half, TILE), half)]
    diagonal = packed[2 * half:]
    diagonal_ref[...] = diagonal
    start = 0
    for n, send_ref in enumerate(send_refs):
        size = send_ref.shape[0] - (rows if n == 0 else 0)
        send_ref[:size] = packed[pl.ds(pl.multiple_of((1 - mine) * half + start, TILE), size)]
        if n == 0:
            send_ref[size:] = diagonal
        start += size


def encode(values, ref, exponent=None, digits=()):
    rows = values.shape[0]
    largest = jnp.max(jnp.abs(values), axis=0, keepdims=True)
    steps = jnp.ceil(OCTAVE * jnp.log2(jnp.maximum(largest, tiny)))
    factor = jnp.exp2(steps * (-1.0 / OCTAVE)) * LEVELS
    ref[:rows] = jnp.floor(values * factor + 0.5).astype(I32).astype(I16)
    notes = [jnp.broadcast_to(steps, (8, BLOCK))]
    if exponent is None:
        notes += notes
    else:
        notes += [exponent, *digits]
    notes = jnp.concatenate(notes, axis=0)
    if notes.shape[0] < ref.shape[0] - rows:
        notes = jnp.concatenate([notes, jnp.zeros((ref.shape[0] - rows - notes.shape[0], BLOCK), F32)], axis=0)
    ref[rows:] = notes.astype(I32).astype(I16)


def decode(ref, rows):
    notes = ref[rows:].astype(I32).astype(F32)
    return ref[:rows].astype(I32).astype(F32) * (jnp.exp2(notes[:1] * (1.0 / OCTAVE)) * (1.0 / LEVELS)), notes[8:]


def digits_of(diagonal, exponent):
    value = diagonal * jnp.exp2(-2.0 * exponent) * LEVELS
    first = jnp.floor(value + 0.5)
    return first, jnp.floor((value - first) * LEVELS + 0.5)


def from_digits(first, second, exponent):
    return (first + second * (1.0 / LEVELS)) * (1.0 / LEVELS) * jnp.exp2(2.0 * exponent)


def stage_kernel(hidden, halvings, bit, first, cut, parts, where_ref, keep_ref, diagonal_ref, *refs):
    got_refs, refs = refs[:parts], refs[parts:]
    sent_ref, diagonal_out, *kept, factors, total = refs
    rows, many = keep_ref.shape[0], diagonal_ref.shape[0]
    length = layout(hidden, halvings)[3]
    where = where_ref[0]
    place = sum(bit_of(where, b) * (length >> (b + 1)) for b in range(bit))
    here = pl.ds(pl.multiple_of(place, TILE), rows)
    diagonal = diagonal_ref[...]
    if first:
        start = 0
        for n, ref in enumerate(got_refs):
            size = ref.shape[0] - (many if n == 0 else 0)
            total[start:start + size] = keep_ref[start:start + size] + ref[:size]
            if n == 0:
                diagonal = diagonal + ref[size:]
            start += size
    else:
        value, notes = decode(got_refs[0], rows)
        theirs = notes[:many]
        spread(hidden, halvings, jnp.exp2(theirs), factors)
        total[...] = keep_ref[...] + value * factors[here]
        exponent = exponent_of(diagonal)
        ours = from_digits(*digits_of(diagonal, exponent), exponent)
        diagonal = ours + from_digits(notes[many:2 * many], notes[2 * many:3 * many], theirs)
    diagonal_out[...] = diagonal
    exponent = exponent_of(diagonal)
    spread(hidden, halvings, jnp.exp2(-exponent), factors)
    if cut:
        half = rows // 2
        mine = bit_of(where, bit)
        kept[0][...] = total[pl.ds(pl.multiple_of(mine * half, TILE), half)]
        away = (1 - mine) * half
        value = total[pl.ds(pl.multiple_of(away, TILE), half)] * factors[pl.ds(pl.multiple_of(place + away, TILE), half)]
        encode(value, sent_ref, exponent, digits_of(diagonal, exponent))
    elif kept:
        kept[0][...] = total[...]
        encode(total[...] * factors[here], sent_ref, exponent, digits_of(diagonal, exponent))
    else:
        encode(total[...] * factors[here], sent_ref)


def unpack_kernel(hidden, halvings, flips, where_ref, diagonal_ref, *refs):
    piece_refs, (high_ref, low_ref, packed) = refs[:len(flips)], refs[len(flips):]
    off, pairs, tail, length = layout(hidden, halvings)
    where = where_ref[0]
    rows = length >> halvings
    for flip, piece_ref in zip(flips, piece_refs):
        owner = lax.bitwise_xor(where, flip)
        start = sum(bit_of(owner, b) * (length >> (b + 1)) for b in range(halvings))
        packed[pl.ds(pl.multiple_of(start, TILE), rows)] = decode(piece_ref, rows)[0]

    def put(i, j, block):
        rows, cols = slice(i * BLOCK, (i + 1) * BLOCK), slice(j * BLOCK, (j + 1) * BLOCK)
        hi = block.astype(BF16)
        high_ref[rows, cols] = hi
        low_ref[rows, cols] = (block - hi.astype(F32)).astype(BF16)

    for n, (i, j) in enumerate(off):
        block = packed[n * BLOCK:(n + 1) * BLOCK]
        put(i, j, block)
        put(j, i, block.T)
    diagonal = diagonal_ref[...]
    ones = diagonal * jnp.exp2(-2.0 * exponent_of(diagonal))
    for n, (first, second) in enumerate(pairs):
        row = (len(off) + n) * BLOCK
        block = packed[row:row + BLOCK]
        turned = block.T
        for i, above in ((first, lax.lt), (second, lax.gt)):
            if i is not None:
                whole = jnp.where(eye_of(above), block, turned)
                put(i, i, jnp.where(eye_of(lax.eq), ones[i:i + 1], whole))


def relay_kernel(in_ref, out_ref):
    out_ref[...] = in_ref[...]


def sweeps_kernel(slot, diagonal_ref, weight_ref, mask_ref, high_ref, low_ref, *refs):
    out_ref, token_ref, result, changes, done = refs[-5:]
    features, hidden = result.shape
    columns = [slice(c, c + WIDTH) for c in range(0, hidden, WIDTH)]
    diagonal = jnp.concatenate([diagonal_ref[b:b + 1] for b in range(hidden // BLOCK)], axis=1)
    back = jnp.exp2(exponent_of(diagonal))
    factor = relax_factor * (1.0 / (diagonal + diagonal_eps)) * back
    copies = []

    def note(sweep, part, change):
        change = change * back[:, part]
        top = change.astype(BF16)
        changes[sweep % 2, :features, part] = top
        if sweep > 0:
            changes[sweep % 2, features:, part] = (change - top.astype(F32)).astype(BF16)

    for part in columns:
        weight = weight_ref[slot, :, part].astype(F32)
        pruned = mask_ref[slot, :, part].astype(F32) * weight
        result[:, part] = pruned
        note(0, part, pruned - weight)
    for sweep in range(STEPS):
        now = changes.at[sweep % 2]
        for n, part in enumerate(columns):
            if sweep == 0:
                gradient = jnp.dot(now[:features], high_ref[:, part], preferred_element_type=F32)
            else:
                both = jnp.dot(now[...], high_ref[:, part], preferred_element_type=F32)
                gradient = both[:features] + both[features:]
            gradient = gradient + jnp.dot(now[:features], low_ref[:, part], preferred_element_type=F32)
            pruned = mask_ref[slot, :, part].astype(F32) * (result[:, part] - gradient * factor[:, part])
            result[:, part] = pruned
            if sweep < STEPS - 1:
                note(sweep + 1, part, pruned - weight_ref[slot, :, part].astype(F32))
            else:
                copies.append(pltpu.make_async_copy(result.at[:, part], out_ref.at[slot, :, part], done.at[n]))
                copies[-1].start()
    token_ref[...] = result[:8, :BLOCK]
    for copy in copies:
        copy.wait()


def on_device(expert_inputs, row_expert, down_weight, keep_mask):
    tokens, hidden = expert_inputs.shape
    slots, features, _ = down_weight.shape
    peers = lax.axis_size("expert")
    copies = lax.axis_size("rows")
    all_experts = slots * peers
    capacity = tokens // 8
    halvings = copies.bit_length() - 2
    length = layout(hidden, halvings)[3]
    me = jnp.reshape(lax.axis_index("expert").astype(I32), (1,))
    where = jnp.reshape(lax.axis_index("rows").astype(I32), (1,))
    owners = row_expert.reshape(1, tokens)

    def shape(rows, columns=BLOCK, dtype=F32):
        return jax.ShapeDtypeStruct((rows, columns), dtype)

    def over_experts(array, flip):
        return lax.ppermute(array, "expert", [(i, i ^ flip) for i in range(peers)])

    def over_rows(array, bit):
        return lax.ppermute(array, "rows", [(i, i ^ (1 << bit)) for i in range(copies)])

    chunk = shape(capacity, hidden, BF16)
    place_flops = 2 * capacity * tokens * hidden
    key, *outgoing = call(
        functools.partial(first_kernel, peers, slots, all_experts, capacity),
        [shape(1, tokens, I32)] + [chunk] * (peers - 1), [SMEM, HBM, HBM],
        scratch=[
            pltpu.VMEM((1, tokens), I32), pltpu.VMEM((tokens, hidden), BF16),
            pltpu.SemaphoreType.DMA, pltpu.SemaphoreType.DMA((COPIES,)),
        ],
        flops=place_flops * (peers - 1), moved=expert_inputs.size * 4, name="place_first",
    )(me, owners, expert_inputs)
    arrived = [[over_experts(rows, k) for rows, k in zip(outgoing, others(peers))]]
    count = slots + (slots - 1) * (peers - 1)
    parts = [shape(n, hidden, BF16) for n in cuts(capacity, 2)]
    flips = [peers - 1, *others(peers)]
    rest = call(
        functools.partial(second_kernel, peers, slots, capacity),
        [chunk] * slots + (parts + [chunk] * (peers - 2)) * (slots - 1), [SMEM, VMEM, VMEM],
        flops=place_flops * count, moved=expert_inputs.size * 4, name="place_rest",
    )(me, key, expert_inputs)
    own = rest[:slots]
    for a in range(1, slots):
        outgoing = rest[slots + (a - 1) * peers:slots + a * peers]
        arrived.append([over_experts(rows, k) for rows, k in zip(outgoing, flips)])

    many = diagonal_rows(hidden)
    notes = -(-(8 + 3 * many) // TILE) * TILE

    def begin(a, after):
        chunks = [own[a]] + arrived[a][:1]
        return call(
            functools.partial(early_gram_kernel, halvings), shape(length + many), [VMEM] * len(chunks),
            flops=2 * capacity * len(chunks) * hidden * hidden, moved=length * BLOCK * 4, name=f"begin_{a}", after=after,
        )(*chunks)

    def stage(name, bit, keep, diagonal, got, cut, kept, after=()):
        rows = keep.shape[0]
        left = rows // 2 if cut else rows
        return call(
            functools.partial(stage_kernel, hidden, halvings, bit, got[0].dtype == F32, cut, len(got)),
            [shape(left + (notes if kept else TILE), dtype=I16), shape(many)] + ([shape(left)] if kept else []),
            [SMEM] + [VMEM] * (2 + len(got)),
            scratch=[pltpu.VMEM((length, BLOCK), F32), pltpu.VMEM((rows, BLOCK), F32)],
            name=name, after=after,
        )(where, keep, diagonal, *got)

    def reduce(a, before, after, behind):
        size = length // 2
        sizes = cuts(size, PARTS if a == slots - 1 else 3)
        keep, diagonal, *sent = call(
            functools.partial(late_gram_kernel, halvings, len(arrived[a]) - 1),
            [shape(size), shape(many)] + [shape(n + (many if i == 0 else 0)) for i, n in enumerate(sizes)],
            [SMEM] + [VMEM] * len(arrived[a]), scratch=[pltpu.VMEM((length + many, BLOCK), F32)],
            name=f"gram_{a}", after=after,
        )(where, before, *arrived[a][1:])
        for bit in range(1, halvings + 1):
            cut = bit < halvings
            got = [over_rows(part, bit - 1) for part in sent]
            coded, diagonal, keep = stage(f"stage_{a}_{bit}", bit, keep, diagonal, got, cut, True, behind if bit == 1 else ())
            sent = [coded]
        return coded, diagonal, keep

    def end(a, sums, after):
        coded, diagonal, keep = sums
        return stage(f"total_{a}", halvings, keep, diagonal, [over_rows(coded, halvings)], False, False, after)

    def pieces_of(coded, after):
        held = [(0, coded)]
        for bit in range(halvings - 1, -1, -1):
            came = [(flip ^ (1 << bit), over_rows(piece, bit)) for flip, piece in held]
            if after and bit == halvings - 1 and bit > 0:
                came = [
                    (flip, call(relay_kernel, shape(piece.shape[0], dtype=I16), [VMEM], name="relay", after=after)(piece))
                    for flip, piece in came
                ]
            held += came
        return held

    def gather(a, held, diagonal, after):
        high, low = call(
            functools.partial(unpack_kernel, hidden, halvings, [flip for flip, _ in held]),
            [shape(hidden, hidden, BF16)] * 2, [SMEM] + [VMEM] * (1 + len(held)),
            scratch=[pltpu.VMEM((length, BLOCK), F32)], moved=length * BLOCK * 4, name=f"unpack_{a}", after=after,
        )(where, diagonal, *[piece for _, piece in held])
        return diagonal, high, low

    def sweeps(a, diagonal, high, low, result, after):
        args = [diagonal, down_weight, keep_mask, high, low] + ([] if result is None else [result])
        return call(
            functools.partial(sweeps_kernel, a),
            [jax.ShapeDtypeStruct((slots, features, hidden), F32), shape(8)],
            [VMEM] * 5 + [ANY] * (len(args) - 5),
            out_specs=[ANY, VMEM],
            scratch=[
                pltpu.VMEM((features, hidden), F32), pltpu.VMEM((2, 2 * features, hidden), BF16),
                pltpu.SemaphoreType.DMA((hidden // WIDTH,)),
            ],
            aliases={} if result is None else {5: 0},
            flops=2 * 3 * STEPS * features * hidden * hidden, moved=hidden * hidden * 4, name=f"sweeps_{a}",
            after=after,
        )(*args)

    early = [begin(a, ()) for a in range(slots)]
    result, whole, total, sums, token = None, None, (), (), []
    for a in range(slots):
        sums = reduce(a, early[a], sums[:1], [*early[a + 1:a + 2], *total[:1]])
        if a > 0:
            whole = gather(a - 1, pieces_of(total[0], token), total[1], ())
        total = end(a, sums, whole[1:2] if whole else ())
        if a > 0:
            result, *token = sweeps(a - 1, *whole, result, total[:1])
    return sweeps(slots - 1, *gather(slots - 1, pieces_of(total[0], token), total[1], ()), result, ())[0]


def solution(mesh):
    return jax.shard_map(
        on_device,
        mesh=mesh,
        in_specs=(
            P(("expert", "rows"), None),
            P(("expert", "rows"), None),
            P("expert", "rows", None),
            P("expert", "rows", None),
        ),
        out_specs=P("expert", "rows", None),
        check_vma=False,
    )
```

```python
import functools

import jax
import jax.numpy as jnp
from jax import lax
from jax.experimental import pallas as pl
from jax.experimental.pallas import tpu as pltpu
from jax.sharding import PartitionSpec as P

STEPS = 4
BLOCK = 128
TILE = 16
PARTS = 4
WIDTH = 2 * BLOCK
LEVELS = 32760.0
OCTAVE = 8.0
relax_factor = 0.5
diagonal_eps = 1e-06
tiny = 1e-30
VMEM_LIMIT = 24 * 2**20
PLACE_LIMIT = 50 * 2**20

VMEM = pl.BlockSpec(memory_space=pltpu.VMEM)
ANY = pl.BlockSpec(memory_space=pl.ANY)
HBM = pl.BlockSpec(memory_space=pltpu.HBM)
SMEM = pl.BlockSpec(memory_space=pltpu.SMEM)
F32, BF16, I32, I16 = jnp.float32, jnp.bfloat16, jnp.int32, jnp.int16


def call(kernel, out_shape, in_specs, scratch=(), flops=0, moved=0, out_specs=None, aliases=None, name=None, after=(), limit=VMEM_LIMIT):
    many = isinstance(out_shape, (list, tuple))
    used, idle = len(in_specs), len(after)

    def body(*refs):
        kernel(*refs[:used], *refs[used + idle:])

    inner = pl.pallas_call(
        body,
        out_shape=out_shape,
        in_specs=list(in_specs) + [ANY] * idle,
        out_specs=out_specs if out_specs is not None else ([VMEM] * len(out_shape) if many else VMEM),
        scratch_shapes=list(scratch),
        input_output_aliases=aliases or {},
        cost_estimate=pl.CostEstimate(flops=flops, bytes_accessed=moved, transcendentals=0),
        compiler_params=pltpu.CompilerParams(vmem_limit_bytes=limit),
        name=name,
    )
    return lambda *args: inner(*args, *after)


def cuts(size, chunks):
    ends = [size * (c + 1) // (TILE * chunks) * TILE for c in range(chunks)]
    return [end - start for start, end in zip([0] + ends, ends)]


def slots_of(owners, experts, capacity):
    tokens = owners.shape[1]
    lanes = 128
    blocks = tokens // lanes
    named = owners == lax.broadcasted_iota(I32, (experts, tokens), 0)
    ones = named.astype(F32)
    stacked = jnp.concatenate([ones[:, b * lanes:(b + 1) * lanes] for b in range(blocks)], axis=0)
    upto = lax.broadcasted_iota(I32, (lanes, lanes), 0) <= lax.broadcasted_iota(I32, (lanes, lanes), 1)
    within = jnp.dot(stacked.astype(BF16), upto.astype(F32).astype(BF16), preferred_element_type=F32)
    carry = jnp.zeros((experts, 1), F32)
    parts = []
    for b in range(blocks):
        part = within[b * experts:(b + 1) * experts]
        parts.append(part + carry)
        carry = carry + part[:, lanes - 1:lanes]
    counted = jnp.concatenate(parts, axis=1)
    rank = jnp.sum(jnp.where(named, counted - 1.0, 0.0), axis=0, keepdims=True)
    return owners * capacity + rank.astype(I32)


def place(key, rows_ref, experts, capacity, out_refs, chosen_ref=None, ready=None):
    tokens, hidden = rows_ref.shape
    places = lax.broadcasted_iota(I32, (capacity, tokens), 0)
    chosen = jnp.concatenate(
        [(places == key - e * capacity).astype(F32).astype(BF16) for e in experts], axis=0
    )
    if ready is not None:
        chosen_ref[...] = chosen
        ready()
        chosen = chosen_ref[...]
    for c in range(0, hidden, WIDTH):
        got = jnp.dot(chosen, rows_ref[:, c:c + WIDTH], preferred_element_type=F32).astype(BF16)
        for k, out_ref in enumerate(out_refs):
            out_ref[:, c:c + WIDTH] = got[k * capacity:(k + 1) * capacity]


def others(peers):
    return range(peers - 1, 0, -1)


def first_kernel(peers, slots, all_experts, capacity, me_ref, owner_any, rows_any, key_ref, *refs):
    out_refs, (owner_ref, rows_ref, chosen_ref, owner_done, rows_done) = refs[:-5], refs[-5:]
    owner_copy = pltpu.make_async_copy(owner_any, owner_ref, owner_done)
    owner_copy.start()
    rows_copy = pltpu.make_async_copy(rows_any, rows_ref, rows_done)
    rows_copy.start()
    me = me_ref[0]
    owner_copy.wait()
    key = slots_of(owner_ref[...], all_experts, capacity)
    key_ref[...] = key
    experts = [lax.bitwise_xor(me, k) * slots for k in others(peers)]
    place(key, rows_ref, experts, capacity, out_refs, chosen_ref, rows_copy.wait)


def second_kernel(peers, slots, capacity, me_ref, key_ref, rows_ref, *out_refs):
    me = me_ref[0]
    where = [(0, a) for a in range(slots)] + [(k, a) for a in range(1, slots) for k in others(peers)]
    place(key_ref[...], rows_ref, [lax.bitwise_xor(me, k) * slots + a for k, a in where], capacity, out_refs)


def layout(hidden, halvings):
    blocks = hidden // BLOCK
    off = [(i, j) for i in range(blocks) for j in range(i + 1, blocks)]
    pairs = [(i, i + 1 if i + 1 < blocks else None) for i in range(0, blocks, 2)]
    tail = (len(off) + len(pairs)) * BLOCK
    unit = TILE << halvings
    return off, pairs, tail, -(-tail // unit) * unit


def eye_of(compare):
    return compare(lax.broadcasted_iota(I32, (BLOCK, BLOCK), 0), lax.broadcasted_iota(I32, (BLOCK, BLOCK), 1))


def bit_of(where, bit):
    return lax.bitwise_and(lax.shift_right_logical(where, bit), 1)


def diagonal_rows(hidden):
    return -(-(hidden // BLOCK) // 8) * 8


def exponent_of(diagonal):
    return jnp.ceil(0.5 * jnp.log2(jnp.maximum(diagonal, tiny)))


def spread(hidden, halvings, factor, out_ref):
    off, pairs, tail, length = layout(hidden, halvings)
    if length > tail:
        out_ref[tail:length] = jnp.zeros((length - tail, BLOCK), F32)
    across = [jnp.broadcast_to(factor[b:b + 1], (BLOCK, BLOCK)) for b in range(hidden // BLOCK)]
    down = [a.T for a in across]
    for n, (i, j) in enumerate(off):
        out_ref[n * BLOCK:(n + 1) * BLOCK] = down[i] * across[j]
    for n, (first, second) in enumerate(pairs):
        block = down[first] * across[first]
        if second is not None:
            block = jnp.where(eye_of(lax.lt), block, down[second] * across[second])
        row = (len(off) + n) * BLOCK
        out_ref[row:row + BLOCK] = block


def add_gram(halvings, chunk_refs, before, packed):
    hidden = chunk_refs[0].shape[1]
    off, pairs, tail, length = layout(hidden, halvings)
    at = {pair: n for n, pair in enumerate(off)}
    x = jnp.concatenate([r[...] for r in chunk_refs], axis=0) if len(chunk_refs) > 1 else chunk_refs[0][...]
    strip = 2 * BLOCK

    def put(n, value):
        rows = slice(n * BLOCK, (n + 1) * BLOCK)
        packed[rows] = value if before is None else before[rows] + value

    def put_diagonal(i, block):
        value = jnp.sum(jnp.where(eye_of(lax.eq), block, 0.0), axis=0, keepdims=True)
        row = slice(length + i, length + i + 1)
        packed[row] = value if before is None else before[row] + value

    packed[tail:] = jnp.zeros((packed.shape[0] - tail, BLOCK), F32)
    for n, (first, second) in enumerate(pairs):
        low, high = first * BLOCK, min(first * BLOCK + strip, hidden)
        product = lax.dot_general(
            x[:, low:high], x[:, low:], (((0,), (0,)), ((), ())), preferred_element_type=F32
        )
        for i in range((high - low) // BLOCK):
            for j in range((hidden - low) // BLOCK):
                pair = (first + i, first + j)
                if pair in at:
                    put(at[pair], product[i * BLOCK:(i + 1) * BLOCK, j * BLOCK:(j + 1) * BLOCK])
        mixed = product[:BLOCK, :BLOCK]
        put_diagonal(first, mixed)
        if second is not None:
            other = product[BLOCK:, BLOCK:2 * BLOCK]
            put_diagonal(second, other)
            mixed = jnp.where(eye_of(lax.lt), mixed, other)
        put(len(off) + n, jnp.where(eye_of(lax.eq), 0.0, mixed))


def early_gram_kernel(halvings, *refs):
    add_gram(halvings, refs[:-1], None, refs[-1])


def late_gram_kernel(halvings, pieces, where_ref, before_ref, *refs):
    chunk_refs, (keep_ref, diagonal_ref, *send_refs, packed) = refs[:pieces], refs[pieces:]
    add_gram(halvings, chunk_refs, before_ref, packed)
    half, rows = keep_ref.shape[0], diagonal_ref.shape[0]
    mine = bit_of(where_ref[0], 0)
    keep_ref[...] = packed[pl.ds(pl.multiple_of(mine * half, TILE), half)]
    diagonal = packed[2 * half:]
    diagonal_ref[...] = diagonal
    start = 0
    for n, send_ref in enumerate(send_refs):
        size = send_ref.shape[0] - (rows if n == 0 else 0)
        send_ref[:size] = packed[pl.ds(pl.multiple_of((1 - mine) * half + start, TILE), size)]
        if n == 0:
            send_ref[size:] = diagonal
        start += size


def encode(values, ref, exponent=None, digits=()):
    rows = values.shape[0]
    largest = jnp.max(jnp.abs(values), axis=0, keepdims=True)
    steps = jnp.ceil(OCTAVE * jnp.log2(jnp.maximum(largest, tiny)))
    factor = jnp.exp2(steps * (-1.0 / OCTAVE)) * LEVELS
    ref[:rows] = jnp.floor(values * factor + 0.5).astype(I32).astype(I16)
    notes = [jnp.broadcast_to(steps, (8, BLOCK))]
    if exponent is None:
        notes += notes
    else:
        notes += [exponent, *digits]
    notes = jnp.concatenate(notes, axis=0)
    if notes.shape[0] < ref.shape[0] - rows:
        notes = jnp.concatenate([notes, jnp.zeros((ref.shape[0] - rows - notes.shape[0], BLOCK), F32)], axis=0)
    ref[rows:] = notes.astype(I32).astype(I16)


def decode(ref, rows):
    notes = ref[rows:].astype(I32).astype(F32)
    return ref[:rows].astype(I32).astype(F32) * (jnp.exp2(notes[:1] * (1.0 / OCTAVE)) * (1.0 / LEVELS)), notes[8:]


def digits_of(diagonal, exponent):
    value = diagonal * jnp.exp2(-2.0 * exponent) * LEVELS
    first = jnp.floor(value + 0.5)
    return first, jnp.floor((value - first) * LEVELS + 0.5)


def from_digits(first, second, exponent):
    return (first + second * (1.0 / LEVELS)) * (1.0 / LEVELS) * jnp.exp2(2.0 * exponent)


def stage_kernel(hidden, halvings, bit, first, cut, parts, where_ref, keep_ref, diagonal_ref, *refs):
    got_refs, refs = refs[:parts], refs[parts:]
    sent_ref, diagonal_out, *kept, factors, total = refs
    rows, many = keep_ref.shape[0], diagonal_ref.shape[0]
    length = layout(hidden, halvings)[3]
    where = where_ref[0]
    place = sum(bit_of(where, b) * (length >> (b + 1)) for b in range(bit))
    here = pl.ds(pl.multiple_of(place, TILE), rows)
    diagonal = diagonal_ref[...]
    if first:
        start = 0
        for n, ref in enumerate(got_refs):
            size = ref.shape[0] - (many if n == 0 else 0)
            total[start:start + size] = keep_ref[start:start + size] + ref[:size]
            if n == 0:
                diagonal = diagonal + ref[size:]
            start += size
    else:
        value, notes = decode(got_refs[0], rows)
        theirs = notes[:many]
        spread(hidden, halvings, jnp.exp2(theirs), factors)
        total[...] = keep_ref[...] + value * factors[here]
        exponent = exponent_of(diagonal)
        ours = from_digits(*digits_of(diagonal, exponent), exponent)
        diagonal = ours + from_digits(notes[many:2 * many], notes[2 * many:3 * many], theirs)
    diagonal_out[...] = diagonal
    exponent = exponent_of(diagonal)
    spread(hidden, halvings, jnp.exp2(-exponent), factors)
    if cut:
        half = rows // 2
        mine = bit_of(where, bit)
        kept[0][...] = total[pl.ds(pl.multiple_of(mine * half, TILE), half)]
        away = (1 - mine) * half
        value = total[pl.ds(pl.multiple_of(away, TILE), half)] * factors[pl.ds(pl.multiple_of(place + away, TILE), half)]
        encode(value, sent_ref, exponent, digits_of(diagonal, exponent))
    elif kept:
        kept[0][...] = total[...]
        encode(total[...] * factors[here], sent_ref, exponent, digits_of(diagonal, exponent))
    else:
        encode(total[...] * factors[here], sent_ref)


def unpack_kernel(hidden, halvings, flips, where_ref, diagonal_ref, *refs):
    piece_refs, (high_ref, low_ref, packed) = refs[:len(flips)], refs[len(flips):]
    off, pairs, tail, length = layout(hidden, halvings)
    where = where_ref[0]
    rows = length >> halvings
    for flip, piece_ref in zip(flips, piece_refs):
        owner = lax.bitwise_xor(where, flip)
        start = sum(bit_of(owner, b) * (length >> (b + 1)) for b in range(halvings))
        packed[pl.ds(pl.multiple_of(start, TILE), rows)] = decode(piece_ref, rows)[0]

    def put(i, j, block):
        rows, cols = slice(i * BLOCK, (i + 1) * BLOCK), slice(j * BLOCK, (j + 1) * BLOCK)
        hi = block.astype(BF16)
        high_ref[rows, cols] = hi
        low_ref[rows, cols] = (block - hi.astype(F32)).astype(BF16)

    for n, (i, j) in enumerate(off):
        block = packed[n * BLOCK:(n + 1) * BLOCK]
        put(i, j, block)
        put(j, i, block.T)
    diagonal = diagonal_ref[...]
    ones = diagonal * jnp.exp2(-2.0 * exponent_of(diagonal))
    for n, (first, second) in enumerate(pairs):
        row = (len(off) + n) * BLOCK
        block = packed[row:row + BLOCK]
        turned = block.T
        for i, above in ((first, lax.lt), (second, lax.gt)):
            if i is not None:
                whole = jnp.where(eye_of(above), block, turned)
                put(i, i, jnp.where(eye_of(lax.eq), ones[i:i + 1], whole))


def relay_kernel(in_ref, out_ref):
    out_ref[...] = in_ref[...]


def sweeps_kernel(slot, diagonal_ref, weight_ref, mask_ref, high_ref, low_ref, *refs):
    out_ref, token_ref, result, changes, done = refs[-5:]
    features, hidden = result.shape
    columns = [slice(c, c + WIDTH) for c in range(0, hidden, WIDTH)]
    diagonal = jnp.concatenate([diagonal_ref[b:b + 1] for b in range(hidden // BLOCK)], axis=1)
    back = jnp.exp2(exponent_of(diagonal))
    factor = relax_factor * (1.0 / (diagonal + diagonal_eps)) * back
    copies = []

    def note(sweep, part, change):
        change = change * back[:, part]
        top = change.astype(BF16)
        changes[sweep % 2, :features, part] = top
        if sweep > 0:
            changes[sweep % 2, features:, part] = (change - top.astype(F32)).astype(BF16)

    for part in columns:
        weight = weight_ref[slot, :, part].astype(F32)
        pruned = mask_ref[slot, :, part].astype(F32) * weight
        result[:, part] = pruned
        note(0, part, pruned - weight)
    for sweep in range(STEPS):
        now = changes.at[sweep % 2]
        for n, part in enumerate(columns):
            if sweep == 0:
                gradient = jnp.dot(now[:features], high_ref[:, part], preferred_element_type=F32)
            else:
                both = jnp.dot(now[...], high_ref[:, part], preferred_element_type=F32)
                gradient = both[:features] + both[features:]
            gradient = gradient + jnp.dot(now[:features], low_ref[:, part], preferred_element_type=F32)
            pruned = mask_ref[slot, :, part].astype(F32) * (result[:, part] - gradient * factor[:, part])
            result[:, part] = pruned
            if sweep < STEPS - 1:
                note(sweep + 1, part, pruned - weight_ref[slot, :, part].astype(F32))
            else:
                copies.append(pltpu.make_async_copy(result.at[:, part], out_ref.at[slot, :, part], done.at[n]))
                copies[-1].start()
    token_ref[...] = result[:8, :BLOCK]
    for copy in copies:
        copy.wait()


def on_device(expert_inputs, row_expert, down_weight, keep_mask):
    tokens, hidden = expert_inputs.shape
    slots, features, _ = down_weight.shape
    peers = lax.axis_size("expert")
    copies = lax.axis_size("rows")
    all_experts = slots * peers
    capacity = tokens // 8
    halvings = copies.bit_length() - 2
    length = layout(hidden, halvings)[3]
    me = jnp.reshape(lax.axis_index("expert").astype(I32), (1,))
    where = jnp.reshape(lax.axis_index("rows").astype(I32), (1,))
    owners = row_expert.reshape(1, tokens)

    def shape(rows, columns=BLOCK, dtype=F32):
        return jax.ShapeDtypeStruct((rows, columns), dtype)

    def over_experts(array, flip):
        return lax.ppermute(array, "expert", [(i, i ^ flip) for i in range(peers)])

    def over_rows(array, bit):
        return lax.ppermute(array, "rows", [(i, i ^ (1 << bit)) for i in range(copies)])

    chunk = shape(capacity, hidden, BF16)
    place_flops = 2 * capacity * tokens * hidden
    key, *outgoing = call(
        functools.partial(first_kernel, peers, slots, all_experts, capacity),
        [shape(1, tokens, I32)] + [chunk] * (peers - 1), [SMEM, HBM, HBM],
        scratch=[
            pltpu.VMEM((1, tokens), I32), pltpu.VMEM((tokens, hidden), BF16),
            pltpu.VMEM(((peers - 1) * capacity, tokens), BF16),
            pltpu.SemaphoreType.DMA, pltpu.SemaphoreType.DMA,
        ],
        flops=place_flops * (peers - 1), moved=expert_inputs.size * 4, name="place_first", limit=PLACE_LIMIT,
    )(me, owners, expert_inputs)
    arrived = [[over_experts(rows, k) for rows, k in zip(outgoing, others(peers))]]
    count = slots + (slots - 1) * (peers - 1)
    rest = call(
        functools.partial(second_kernel, peers, slots, capacity), [chunk] * count, [SMEM, VMEM, VMEM],
        flops=place_flops * count, moved=expert_inputs.size * 4, name="place_rest", limit=PLACE_LIMIT,
    )(me, key, expert_inputs)
    own = rest[:slots]
    for a in range(1, slots):
        outgoing = rest[slots + (a - 1) * (peers - 1):slots + a * (peers - 1)]
        arrived.append([over_experts(rows, k) for rows, k in zip(outgoing, others(peers))])

    many = diagonal_rows(hidden)
    notes = -(-(8 + 3 * many) // TILE) * TILE

    def begin(a, after):
        chunks = [own[a]] + arrived[a][:1]
        return call(
            functools.partial(early_gram_kernel, halvings), shape(length + many), [VMEM] * len(chunks),
            flops=2 * capacity * len(chunks) * hidden * hidden, moved=length * BLOCK * 4, name=f"begin_{a}", after=after,
        )(*chunks)

    def stage(name, bit, keep, diagonal, got, cut, kept, after=()):
        rows = keep.shape[0]
        left = rows // 2 if cut else rows
        return call(
            functools.partial(stage_kernel, hidden, halvings, bit, got[0].dtype == F32, cut, len(got)),
            [shape(left + (notes if kept else TILE), dtype=I16), shape(many)] + ([shape(left)] if kept else []),
            [SMEM] + [VMEM] * (2 + len(got)),
            scratch=[pltpu.VMEM((length, BLOCK), F32), pltpu.VMEM((rows, BLOCK), F32)],
            name=name, after=after,
        )(where, keep, diagonal, *got)

    def reduce(a, before, after, behind):
        size = length // 2
        sizes = cuts(size, PARTS if a == slots - 1 else 2)
        keep, diagonal, *sent = call(
            functools.partial(late_gram_kernel, halvings, peers - 2),
            [shape(size), shape(many)] + [shape(n + (many if i == 0 else 0)) for i, n in enumerate(sizes)],
            [SMEM] + [VMEM] * (peers - 1), scratch=[pltpu.VMEM((length + many, BLOCK), F32)],
            name=f"gram_{a}", after=after,
        )(where, before, *arrived[a][1:])
        for bit in range(1, halvings + 1):
            cut = bit < halvings
            got = [over_rows(part, bit - 1) for part in sent]
            coded, diagonal, keep = stage(f"stage_{a}_{bit}", bit, keep, diagonal, got, cut, True, behind if bit == 1 else ())
            sent = [coded]
        return coded, diagonal, keep

    def end(a, sums, after):
        coded, diagonal, keep = sums
        return stage(f"total_{a}", halvings, keep, diagonal, [over_rows(coded, halvings)], False, False, after)

    def pieces_of(coded, after):
        held = [(0, coded)]
        for bit in range(halvings - 1, -1, -1):
            came = [(flip ^ (1 << bit), over_rows(piece, bit)) for flip, piece in held]
            if after and bit == halvings - 1 and bit > 0:
                came = [
                    (flip, call(relay_kernel, shape(piece.shape[0], dtype=I16), [VMEM], name="relay", after=after)(piece))
                    for flip, piece in came
                ]
            held += came
        return held

    def gather(a, held, diagonal, after):
        high, low = call(
            functools.partial(unpack_kernel, hidden, halvings, [flip for flip, _ in held]),
            [shape(hidden, hidden, BF16)] * 2, [SMEM] + [VMEM] * (1 + len(held)),
            scratch=[pltpu.VMEM((length, BLOCK), F32)], moved=length * BLOCK * 4, name=f"unpack_{a}", after=after,
        )(where, diagonal, *[piece for _, piece in held])
        return diagonal, high, low

    def sweeps(a, diagonal, high, low, result, after):
        args = [diagonal, down_weight, keep_mask, high, low] + ([] if result is None else [result])
        return call(
            functools.partial(sweeps_kernel, a),
            [jax.ShapeDtypeStruct((slots, features, hidden), F32), shape(8)],
            [VMEM] * 5 + [ANY] * (len(args) - 5),
            out_specs=[ANY, VMEM],
            scratch=[
                pltpu.VMEM((features, hidden), F32), pltpu.VMEM((2, 2 * features, hidden), BF16),
                pltpu.SemaphoreType.DMA((hidden // WIDTH,)),
            ],
            aliases={} if result is None else {5: 0},
            flops=2 * 3 * STEPS * features * hidden * hidden, moved=hidden * hidden * 4, name=f"sweeps_{a}",
            after=after,
        )(*args)

    early = [begin(a, ()) for a in range(slots)]
    result, whole, total, sums, token = None, None, (), (), []
    for a in range(slots):
        sums = reduce(a, early[a], sums[:1], [*early[a + 1:a + 2], *total[:1]])
        if a > 0:
            whole = gather(a - 1, pieces_of(total[0], token), total[1], ())
        total = end(a, sums, whole[1:2] if whole else ())
        if a > 0:
            result, *token = sweeps(a - 1, *whole, result, total[:1])
    return sweeps(slots - 1, *gather(slots - 1, pieces_of(total[0], token), total[1], ()), result, ())[0]


def solution(mesh):
    return jax.shard_map(
        on_device,
        mesh=mesh,
        in_specs=(
            P(("expert", "rows"), None),
            P(("expert", "rows"), None),
            P("expert", "rows", None),
            P("expert", "rows", None),
        ),
        out_specs=P("expert", "rows", None),
        check_vma=False,
    )
```

```python
import functools

import jax
import jax.numpy as jnp
from jax import lax
from jax.experimental import pallas as pl
from jax.experimental.pallas import tpu as pltpu
from jax.sharding import PartitionSpec as P

STEPS = 4
BLOCK = 128
TILE = 16
PARTS = 4
WIDTH = 2 * BLOCK
LEVELS = 32760.0
OCTAVE = 8.0
relax_factor = 0.5
diagonal_eps = 1e-06
tiny = 1e-30
VMEM_LIMIT = 24 * 2**20
PLACE_LIMIT = 50 * 2**20

VMEM = pl.BlockSpec(memory_space=pltpu.VMEM)
ANY = pl.BlockSpec(memory_space=pl.ANY)
HBM = pl.BlockSpec(memory_space=pltpu.HBM)
SMEM = pl.BlockSpec(memory_space=pltpu.SMEM)
F32, BF16, I32, I16 = jnp.float32, jnp.bfloat16, jnp.int32, jnp.int16


def call(kernel, out_shape, in_specs, scratch=(), flops=0, moved=0, out_specs=None, aliases=None, name=None, after=(), limit=VMEM_LIMIT):
    many = isinstance(out_shape, (list, tuple))
    used, idle = len(in_specs), len(after)

    def body(*refs):
        kernel(*refs[:used], *refs[used + idle:])

    inner = pl.pallas_call(
        body,
        out_shape=out_shape,
        in_specs=list(in_specs) + [ANY] * idle,
        out_specs=out_specs if out_specs is not None else ([VMEM] * len(out_shape) if many else VMEM),
        scratch_shapes=list(scratch),
        input_output_aliases=aliases or {},
        cost_estimate=pl.CostEstimate(flops=flops, bytes_accessed=moved, transcendentals=0),
        compiler_params=pltpu.CompilerParams(vmem_limit_bytes=limit),
        name=name,
    )
    return lambda *args: inner(*args, *after)


def cuts(size, chunks):
    ends = [size * (c + 1) // (TILE * chunks) * TILE for c in range(chunks)]
    return [end - start for start, end in zip([0] + ends, ends)]


def slots_of(owners, experts, capacity):
    tokens = owners.shape[1]
    lanes = 128
    blocks = tokens // lanes
    named = owners == lax.broadcasted_iota(I32, (experts, tokens), 0)
    ones = named.astype(F32)
    stacked = jnp.concatenate([ones[:, b * lanes:(b + 1) * lanes] for b in range(blocks)], axis=0)
    upto = lax.broadcasted_iota(I32, (lanes, lanes), 0) <= lax.broadcasted_iota(I32, (lanes, lanes), 1)
    within = jnp.dot(stacked.astype(BF16), upto.astype(F32).astype(BF16), preferred_element_type=F32)
    carry = jnp.zeros((experts, 1), F32)
    parts = []
    for b in range(blocks):
        part = within[b * experts:(b + 1) * experts]
        parts.append(part + carry)
        carry = carry + part[:, lanes - 1:lanes]
    counted = jnp.concatenate(parts, axis=1)
    rank = jnp.sum(jnp.where(named, counted - 1.0, 0.0), axis=0, keepdims=True)
    return owners * capacity + rank.astype(I32)


def place(key, rows_ref, experts, capacity, out_refs, chosen_ref=None, ready=None):
    tokens, hidden = rows_ref.shape
    places = lax.broadcasted_iota(I32, (capacity, tokens), 0)
    chosen = jnp.concatenate(
        [(places == key - e * capacity).astype(F32).astype(BF16) for e in experts], axis=0
    )
    if ready is not None:
        chosen_ref[...] = chosen
        ready()
        chosen = chosen_ref[...]
    for c in range(0, hidden, WIDTH):
        got = jnp.dot(chosen, rows_ref[:, c:c + WIDTH], preferred_element_type=F32).astype(BF16)
        for k, out_ref in enumerate(out_refs):
            out_ref[:, c:c + WIDTH] = got[k * capacity:(k + 1) * capacity]


def others(peers):
    return range(peers - 1, 0, -1)


def first_kernel(peers, slots, all_experts, capacity, me_ref, owner_any, rows_any, key_ref, *refs):
    out_refs, (owner_ref, rows_ref, chosen_ref, owner_done, rows_done) = refs[:-5], refs[-5:]
    owner_copy = pltpu.make_async_copy(owner_any, owner_ref, owner_done)
    owner_copy.start()
    rows_copy = pltpu.make_async_copy(rows_any, rows_ref, rows_done)
    rows_copy.start()
    me = me_ref[0]
    owner_copy.wait()
    key = slots_of(owner_ref[...], all_experts, capacity)
    key_ref[...] = key
    experts = [lax.bitwise_xor(me, k) * slots for k in others(peers)]
    place(key, rows_ref, experts, capacity, out_refs, chosen_ref, rows_copy.wait)


def second_kernel(peers, slots, capacity, me_ref, key_ref, rows_ref, *out_refs):
    me = me_ref[0]
    where = [(0, a) for a in range(slots)] + [(k, a) for a in range(1, slots) for k in others(peers)]
    place(key_ref[...], rows_ref, [lax.bitwise_xor(me, k) * slots + a for k, a in where], capacity, out_refs)


def layout(hidden, halvings):
    blocks = hidden // BLOCK
    off = [(i, j) for i in range(blocks) for j in range(i + 1, blocks)]
    pairs = [(i, i + 1 if i + 1 < blocks else None) for i in range(0, blocks, 2)]
    tail = (len(off) + len(pairs)) * BLOCK
    unit = TILE << halvings
    return off, pairs, tail, -(-tail // unit) * unit


def eye_of(compare):
    return compare(lax.broadcasted_iota(I32, (BLOCK, BLOCK), 0), lax.broadcasted_iota(I32, (BLOCK, BLOCK), 1))


def bit_of(where, bit):
    return lax.bitwise_and(lax.shift_right_logical(where, bit), 1)


def diagonal_rows(hidden):
    return -(-(hidden // BLOCK) // 8) * 8


def exponent_of(diagonal):
    return jnp.ceil(0.5 * jnp.log2(jnp.maximum(diagonal, tiny)))


def spread(hidden, halvings, factor, out_ref):
    off, pairs, tail, length = layout(hidden, halvings)
    if length > tail:
        out_ref[tail:length] = jnp.zeros((length - tail, BLOCK), F32)
    across = [jnp.broadcast_to(factor[b:b + 1], (BLOCK, BLOCK)) for b in range(hidden // BLOCK)]
    down = [a.T for a in across]
    for n, (i, j) in enumerate(off):
        out_ref[n * BLOCK:(n + 1) * BLOCK] = down[i] * across[j]
    for n, (first, second) in enumerate(pairs):
        block = down[first] * across[first]
        if second is not None:
            block = jnp.where(eye_of(lax.lt), block, down[second] * across[second])
        row = (len(off) + n) * BLOCK
        out_ref[row:row + BLOCK] = block


def add_gram(halvings, chunk_refs, before, packed):
    hidden = chunk_refs[0].shape[1]
    off, pairs, tail, length = layout(hidden, halvings)
    at = {pair: n for n, pair in enumerate(off)}
    x = jnp.concatenate([r[...] for r in chunk_refs], axis=0) if len(chunk_refs) > 1 else chunk_refs[0][...]
    strip = 2 * BLOCK

    def put(n, value):
        rows = slice(n * BLOCK, (n + 1) * BLOCK)
        packed[rows] = value if before is None else before[rows] + value

    def put_diagonal(i, block):
        value = jnp.sum(jnp.where(eye_of(lax.eq), block, 0.0), axis=0, keepdims=True)
        row = slice(length + i, length + i + 1)
        packed[row] = value if before is None else before[row] + value

    packed[tail:] = jnp.zeros((packed.shape[0] - tail, BLOCK), F32)
    for n, (first, second) in enumerate(pairs):
        low, high = first * BLOCK, min(first * BLOCK + strip, hidden)
        product = lax.dot_general(
            x[:, low:high], x[:, low:], (((0,), (0,)), ((), ())), preferred_element_type=F32
        )
        for i in range((high - low) // BLOCK):
            for j in range((hidden - low) // BLOCK):
                pair = (first + i, first + j)
                if pair in at:
                    put(at[pair], product[i * BLOCK:(i + 1) * BLOCK, j * BLOCK:(j + 1) * BLOCK])
        mixed = product[:BLOCK, :BLOCK]
        put_diagonal(first, mixed)
        if second is not None:
            other = product[BLOCK:, BLOCK:2 * BLOCK]
            put_diagonal(second, other)
            mixed = jnp.where(eye_of(lax.lt), mixed, other)
        put(len(off) + n, jnp.where(eye_of(lax.eq), 0.0, mixed))


def early_gram_kernel(halvings, *refs):
    add_gram(halvings, refs[:-1], None, refs[-1])


def late_gram_kernel(halvings, pieces, where_ref, before_ref, *refs):
    chunk_refs, (keep_ref, diagonal_ref, *send_refs, packed) = refs[:pieces], refs[pieces:]
    add_gram(halvings, chunk_refs, before_ref, packed)
    half, rows = keep_ref.shape[0], diagonal_ref.shape[0]
    mine = bit_of(where_ref[0], 0)
    keep_ref[...] = packed[pl.ds(pl.multiple_of(mine * half, TILE), half)]
    diagonal = packed[2 * half:]
    diagonal_ref[...] = diagonal
    start = 0
    for n, send_ref in enumerate(send_refs):
        size = send_ref.shape[0] - (rows if n == 0 else 0)
        send_ref[:size] = packed[pl.ds(pl.multiple_of((1 - mine) * half + start, TILE), size)]
        if n == 0:
            send_ref[size:] = diagonal
        start += size


def encode(values, ref, exponent=None, digits=()):
    rows = values.shape[0]
    largest = jnp.max(jnp.abs(values), axis=0, keepdims=True)
    steps = jnp.ceil(OCTAVE * jnp.log2(jnp.maximum(largest, tiny)))
    factor = jnp.exp2(steps * (-1.0 / OCTAVE)) * LEVELS
    ref[:rows] = jnp.floor(values * factor + 0.5).astype(I32).astype(I16)
    notes = [jnp.broadcast_to(steps, (8, BLOCK))]
    if exponent is None:
        notes += notes
    else:
        notes += [exponent, *digits]
    notes = jnp.concatenate(notes, axis=0)
    if notes.shape[0] < ref.shape[0] - rows:
        notes = jnp.concatenate([notes, jnp.zeros((ref.shape[0] - rows - notes.shape[0], BLOCK), F32)], axis=0)
    ref[rows:] = notes.astype(I32).astype(I16)


def decode(ref, rows):
    notes = ref[rows:].astype(I32).astype(F32)
    return ref[:rows].astype(I32).astype(F32) * (jnp.exp2(notes[:1] * (1.0 / OCTAVE)) * (1.0 / LEVELS)), notes[8:]


def digits_of(diagonal, exponent):
    value = diagonal * jnp.exp2(-2.0 * exponent) * LEVELS
    first = jnp.floor(value + 0.5)
    return first, jnp.floor((value - first) * LEVELS + 0.5)


def from_digits(first, second, exponent):
    return (first + second * (1.0 / LEVELS)) * (1.0 / LEVELS) * jnp.exp2(2.0 * exponent)


def stage_kernel(hidden, halvings, bit, first, cut, parts, where_ref, keep_ref, diagonal_ref, *refs):
    got_refs, refs = refs[:parts], refs[parts:]
    sent_ref, diagonal_out, *kept, factors, total = refs
    rows, many = keep_ref.shape[0], diagonal_ref.shape[0]
    length = layout(hidden, halvings)[3]
    where = where_ref[0]
    place = sum(bit_of(where, b) * (length >> (b + 1)) for b in range(bit))
    here = pl.ds(pl.multiple_of(place, TILE), rows)
    diagonal = diagonal_ref[...]
    if first:
        start = 0
        for n, ref in enumerate(got_refs):
            size = ref.shape[0] - (many if n == 0 else 0)
            total[start:start + size] = keep_ref[start:start + size] + ref[:size]
            if n == 0:
                diagonal = diagonal + ref[size:]
            start += size
    else:
        value, notes = decode(got_refs[0], rows)
        theirs = notes[:many]
        spread(hidden, halvings, jnp.exp2(theirs), factors)
        total[...] = keep_ref[...] + value * factors[here]
        exponent = exponent_of(diagonal)
        ours = from_digits(*digits_of(diagonal, exponent), exponent)
        diagonal = ours + from_digits(notes[many:2 * many], notes[2 * many:3 * many], theirs)
    diagonal_out[...] = diagonal
    exponent = exponent_of(diagonal)
    spread(hidden, halvings, jnp.exp2(-exponent), factors)
    if cut:
        half = rows // 2
        mine = bit_of(where, bit)
        kept[0][...] = total[pl.ds(pl.multiple_of(mine * half, TILE), half)]
        away = (1 - mine) * half
        value = total[pl.ds(pl.multiple_of(away, TILE), half)] * factors[pl.ds(pl.multiple_of(place + away, TILE), half)]
        encode(value, sent_ref, exponent, digits_of(diagonal, exponent))
    elif kept:
        kept[0][...] = total[...]
        encode(total[...] * factors[here], sent_ref, exponent, digits_of(diagonal, exponent))
    else:
        encode(total[...] * factors[here], sent_ref)


def unpack_kernel(hidden, halvings, flips, where_ref, diagonal_ref, *refs):
    piece_refs, (high_ref, low_ref, packed) = refs[:len(flips)], refs[len(flips):]
    off, pairs, tail, length = layout(hidden, halvings)
    where = where_ref[0]
    rows = length >> halvings
    for flip, piece_ref in zip(flips, piece_refs):
        owner = lax.bitwise_xor(where, flip)
        start = sum(bit_of(owner, b) * (length >> (b + 1)) for b in range(halvings))
        packed[pl.ds(pl.multiple_of(start, TILE), rows)] = decode(piece_ref, rows)[0]

    def put(i, j, block):
        rows, cols = slice(i * BLOCK, (i + 1) * BLOCK), slice(j * BLOCK, (j + 1) * BLOCK)
        hi = block.astype(BF16)
        high_ref[rows, cols] = hi
        low_ref[rows, cols] = (block - hi.astype(F32)).astype(BF16)

    for n, (i, j) in enumerate(off):
        block = packed[n * BLOCK:(n + 1) * BLOCK]
        put(i, j, block)
        put(j, i, block.T)
    diagonal = diagonal_ref[...]
    ones = diagonal * jnp.exp2(-2.0 * exponent_of(diagonal))
    for n, (first, second) in enumerate(pairs):
        row = (len(off) + n) * BLOCK
        block = packed[row:row + BLOCK]
        turned = block.T
        for i, above in ((first, lax.lt), (second, lax.gt)):
            if i is not None:
                whole = jnp.where(eye_of(above), block, turned)
                put(i, i, jnp.where(eye_of(lax.eq), ones[i:i + 1], whole))


def relay_kernel(in_ref, out_ref):
    out_ref[...] = in_ref[...]


def sweeps_kernel(slot, diagonal_ref, weight_ref, mask_ref, high_ref, low_ref, *refs):
    out_ref, token_ref, result, changes, done = refs[-5:]
    features, hidden = result.shape
    columns = [slice(c, c + WIDTH) for c in range(0, hidden, WIDTH)]
    diagonal = jnp.concatenate([diagonal_ref[b:b + 1] for b in range(hidden // BLOCK)], axis=1)
    back = jnp.exp2(exponent_of(diagonal))
    factor = relax_factor * (1.0 / (diagonal + diagonal_eps)) * back
    copies = []

    def note(sweep, part, change):
        change = change * back[:, part]
        top = change.astype(BF16)
        changes[sweep % 2, :features, part] = top
        if sweep > 0:
            changes[sweep % 2, features:, part] = (change - top.astype(F32)).astype(BF16)

    for part in columns:
        weight = weight_ref[slot, :, part].astype(F32)
        pruned = mask_ref[slot, :, part].astype(F32) * weight
        result[:, part] = pruned
        note(0, part, pruned - weight)
    for sweep in range(STEPS):
        now = changes.at[sweep % 2]
        for n, part in enumerate(columns):
            if sweep == 0:
                gradient = jnp.dot(now[:features], high_ref[:, part], preferred_element_type=F32)
            else:
                both = jnp.dot(now[...], high_ref[:, part], preferred_element_type=F32)
                gradient = both[:features] + both[features:]
            gradient = gradient + jnp.dot(now[:features], low_ref[:, part], preferred_element_type=F32)
            pruned = mask_ref[slot, :, part].astype(F32) * (result[:, part] - gradient * factor[:, part])
            result[:, part] = pruned
            if sweep < STEPS - 1:
                note(sweep + 1, part, pruned - weight_ref[slot, :, part].astype(F32))
            else:
                copies.append(pltpu.make_async_copy(result.at[:, part], out_ref.at[slot, :, part], done.at[n]))
                copies[-1].start()
    token_ref[...] = result[:8, :BLOCK]
    for copy in copies:
        copy.wait()


def on_device(expert_inputs, row_expert, down_weight, keep_mask):
    tokens, hidden = expert_inputs.shape
    slots, features, _ = down_weight.shape
    peers = lax.axis_size("expert")
    copies = lax.axis_size("rows")
    all_experts = slots * peers
    capacity = tokens // 8
    halvings = copies.bit_length() - 2
    length = layout(hidden, halvings)[3]
    me = jnp.reshape(lax.axis_index("expert").astype(I32), (1,))
    where = jnp.reshape(lax.axis_index("rows").astype(I32), (1,))
    owners = row_expert.reshape(1, tokens)

    def shape(rows, columns=BLOCK, dtype=F32):
        return jax.ShapeDtypeStruct((rows, columns), dtype)

    def over_experts(array, flip):
        return lax.ppermute(array, "expert", [(i, i ^ flip) for i in range(peers)])

    def over_rows(array, bit):
        return lax.ppermute(array, "rows", [(i, i ^ (1 << bit)) for i in range(copies)])

    chunk = shape(capacity, hidden, BF16)
    place_flops = 2 * capacity * tokens * hidden
    key, *outgoing = call(
        functools.partial(first_kernel, peers, slots, all_experts, capacity),
        [shape(1, tokens, I32)] + [chunk] * (peers - 1), [SMEM, HBM, HBM],
        scratch=[
            pltpu.VMEM((1, tokens), I32), pltpu.VMEM((tokens, hidden), BF16),
            pltpu.VMEM(((peers - 1) * capacity, tokens), BF16),
            pltpu.SemaphoreType.DMA, pltpu.SemaphoreType.DMA,
        ],
        flops=place_flops * (peers - 1), moved=expert_inputs.size * 4, name="place_first", limit=PLACE_LIMIT,
    )(me, owners, expert_inputs)
    arrived = [[over_experts(rows, k) for rows, k in zip(outgoing, others(peers))]]
    count = slots + (slots - 1) * (peers - 1)
    rest = call(
        functools.partial(second_kernel, peers, slots, capacity), [chunk] * count, [SMEM, VMEM, VMEM],
        flops=place_flops * count, moved=expert_inputs.size * 4, name="place_rest", limit=PLACE_LIMIT,
    )(me, key, expert_inputs)
    own = rest[:slots]
    for a in range(1, slots):
        outgoing = rest[slots + (a - 1) * (peers - 1):slots + a * (peers - 1)]
        arrived.append([over_experts(rows, k) for rows, k in zip(outgoing, others(peers))])

    many = diagonal_rows(hidden)
    notes = -(-(8 + 3 * many) // TILE) * TILE

    def begin(a, after):
        chunks = [own[a]] + arrived[a][:1]
        return call(
            functools.partial(early_gram_kernel, halvings), shape(length + many), [VMEM] * len(chunks),
            flops=2 * capacity * len(chunks) * hidden * hidden, moved=length * BLOCK * 4, name=f"begin_{a}", after=after,
        )(*chunks)

    def stage(name, bit, keep, diagonal, got, cut, kept, after=()):
        rows = keep.shape[0]
        left = rows // 2 if cut else rows
        return call(
            functools.partial(stage_kernel, hidden, halvings, bit, got[0].dtype == F32, cut, len(got)),
            [shape(left + (notes if kept else TILE), dtype=I16), shape(many)] + ([shape(left)] if kept else []),
            [SMEM] + [VMEM] * (2 + len(got)),
            scratch=[pltpu.VMEM((length, BLOCK), F32), pltpu.VMEM((rows, BLOCK), F32)],
            name=name, after=after,
        )(where, keep, diagonal, *got)

    def reduce(a, before, after, behind):
        size = length // 2
        sizes = cuts(size, PARTS if a == slots - 1 else 2)
        keep, diagonal, *sent = call(
            functools.partial(late_gram_kernel, halvings, peers - 2),
            [shape(size), shape(many)] + [shape(n + (many if i == 0 else 0)) for i, n in enumerate(sizes)],
            [SMEM] + [VMEM] * (peers - 1), scratch=[pltpu.VMEM((length + many, BLOCK), F32)],
            name=f"gram_{a}", after=after,
        )(where, before, *arrived[a][1:])
        for bit in range(1, halvings + 1):
            cut = bit < halvings
            got = [over_rows(part, bit - 1) for part in sent]
            coded, diagonal, keep = stage(f"stage_{a}_{bit}", bit, keep, diagonal, got, cut, True, behind if bit == 1 else ())
            sent = [coded]
        return coded, diagonal, keep

    def end(a, sums, after):
        coded, diagonal, keep = sums
        return stage(f"total_{a}", halvings, keep, diagonal, [over_rows(coded, halvings)], False, False, after)

    def pieces_of(coded, after):
        held = [(0, coded)]
        for bit in range(halvings - 1, -1, -1):
            came = [(flip ^ (1 << bit), over_rows(piece, bit)) for flip, piece in held]
            if after and bit == halvings - 1 and bit > 0:
                came = [
                    (flip, call(relay_kernel, shape(piece.shape[0], dtype=I16), [VMEM], name="relay", after=after)(piece))
                    for flip, piece in came
                ]
            held += came
        return held

    def gather(a, held, diagonal, after):
        high, low = call(
            functools.partial(unpack_kernel, hidden, halvings, [flip for flip, _ in held]),
            [shape(hidden, hidden, BF16)] * 2, [SMEM] + [VMEM] * (1 + len(held)),
            scratch=[pltpu.VMEM((length, BLOCK), F32)], moved=length * BLOCK * 4, name=f"unpack_{a}", after=after,
        )(where, diagonal, *[piece for _, piece in held])
        return diagonal, high, low

    def sweeps(a, diagonal, high, low, result, after):
        args = [diagonal, down_weight, keep_mask, high, low] + ([] if result is None else [result])
        return call(
            functools.partial(sweeps_kernel, a),
            [jax.ShapeDtypeStruct((slots, features, hidden), F32), shape(8)],
            [VMEM] * 5 + [ANY] * (len(args) - 5),
            out_specs=[ANY, VMEM],
            scratch=[
                pltpu.VMEM((features, hidden), F32), pltpu.VMEM((2, 2 * features, hidden), BF16),
                pltpu.SemaphoreType.DMA((hidden // WIDTH,)),
            ],
            aliases={} if result is None else {5: 0},
            flops=2 * 3 * STEPS * features * hidden * hidden, moved=hidden * hidden * 4, name=f"sweeps_{a}",
            after=after,
        )(*args)

    early = [begin(a, ()) for a in range(slots)]
    result, whole, total, sums, token = None, None, (), (), []
    for a in range(slots):
        sums = reduce(a, early[a], sums[:1], [*(rows[0] for rows in arrived[a + 1:a + 2]), *total[:1]])
        if a > 0:
            whole = gather(a - 1, pieces_of(total[0], token), total[1], ())
        total = end(a, sums, whole[1:2] if whole else ())
        if a > 0:
            result, *token = sweeps(a - 1, *whole, result, total[:1])
    return sweeps(slots - 1, *gather(slots - 1, pieces_of(total[0], token), total[1], ()), result, ())[0]


def solution(mesh):
    return jax.shard_map(
        on_device,
        mesh=mesh,
        in_specs=(
            P(("expert", "rows"), None),
            P(("expert", "rows"), None),
            P("expert", "rows", None),
            P("expert", "rows", None),
        ),
        out_specs=P("expert", "rows", None),
        check_vma=False,
    )
```
